32 devices in a mesh: tm: 8 (over y, x, core), rows: 4 (over z).
Axes of the slice: x: 2, y: 2, z: 4, core: 2. Of those that a mesh axis runs over, the one named last changes fastest.
Arguments:
- inputs: bfloat16 [8, 2048, 512], P('rows', 'tm'), may hold values from -6 to 6
- resets: int32 [8, 2048], P('rows', 'tm'), may hold values from 0 to 1, as said below
- norm_gains: float32 [2, 512], replicated, may hold values from 0.5 to 1.5
- lam_re: float32 [2, 384], replicated, may hold values from -0.5 to -0.0022097087
- lam_im: float32 [2, 384], replicated, may hold values from -3.140625 to 3.140625
- time_steps: float32 [2, 384], replicated, may hold values from 0.011048543 to 0.4
- b_re: bfloat16 [2, 512, 384], replicated, may hold values from -0.25 to 0.25
- b_im: bfloat16 [2, 512, 384], replicated, may hold values from -0.25 to 0.25
- c_re: bfloat16 [2, 384, 512], replicated, may hold values from -0.21875 to 0.21875
- c_im: bfloat16 [2, 384, 512], replicated, may hold values from -0.21875 to 0.21875
- skip_weight: float32 [2, 512], replicated, may hold values from -3 to 3
- glu_w: bfloat16 [2, 512, 512], replicated, may hold values from -0.25 to 0.25
- glu_bias: float32 [2, 512], replicated, may hold values from -3 to 3
- cotangent: bfloat16 [8, 2048, 512], P('rows', 'tm'), may hold values from -6 to 6
Outputs:
- output: bfloat16 [8, 2048, 512], P('rows', 'tm')
- input_grad: bfloat16 [8, 2048, 512], P('rows', 'tm')
- gain_grad: float32 [2, 512], replicated
- lam_re_grad: float32 [2, 384], replicated
- lam_im_grad: float32 [2, 384], replicated
- step_grad: float32 [2, 384], replicated
- b_re_grad: float32 [2, 512, 384], replicated
- b_im_grad: float32 [2, 512, 384], replicated
- c_re_grad: float32 [2, 384, 512], replicated
- c_im_grad: float32 [2, 384, 512], replicated
- skip_grad: float32 [2, 512], replicated
- glu_w_grad: float32 [2, 512, 512], replicated
- glu_bias_grad: float32 [2, 512], replicated
The draws below stay inside these ranges and needn't reach their ends.
Inputs may be any that keep to these rules, and one draw needn't show every extreme that they name: `resets`: every row starts a document at its first position; in each aligned block of 2 rows, one row chosen by the seed has no other start.
All inputs are finite; a program needn't handle non-finite values.
Results may differ from the reference program's by a relative error of at most 0.012.
Values sent between devices are 32-bit elements; how exact they have to be, the bound alone decides.
A program may use at most 128 MiB of HBM per device.

```python
from functools import partial
import jax
import jax.numpy as jnp
from jax import lax

H = 512
P_SIZE = 384
GROUP = 256
ROWS_DEV = 2
LENGTH = 2048
ROWS = 8


def rate_step(key, slow_share):
    key_class, key_rate, key_step = jax.random.split(key, 3)
    slow_mask = jax.random.uniform(key_class, (2, P_SIZE)) < slow_share
    rate_pick = jax.random.uniform(key_rate, (2, P_SIZE))
    step_pick = jax.random.uniform(key_step, (2, P_SIZE))
    length = jnp.float32(LENGTH)
    slow_rate = 0.2 / length * jnp.exp(rate_pick * jnp.log(10.0))
    fast_rate = 0.02 * jnp.exp(rate_pick * jnp.log(2.5))
    slow_step = 0.5 / jnp.sqrt(length) * jnp.exp(step_pick * jnp.log(4.0))
    fast_step = 0.1 * jnp.exp(step_pick * jnp.log(4.0))
    return (jnp.where(slow_mask, slow_rate, fast_rate), jnp.where(slow_mask, slow_step, fast_step))


def draw_lam_re(key, part):
    slow_share = 0.5
    rate_all, step_all = rate_step(key, slow_share)
    return (-rate_all / step_all).astype(jnp.float32)


def draw_time_steps(key, part):
    slow_share = 0.5
    rate_all, step_all = rate_step(key, slow_share)
    return step_all.astype(jnp.float32)


def draw_resets(key, part):
    key = jax.random.fold_in(key, 7)
    key_start, key_whole = jax.random.split(key)
    starts = (jax.random.randint(key_start, (ROWS, LENGTH), 0, GROUP) < 2).astype(jnp.int32)
    chosen = jax.random.randint(key_whole, (ROWS // ROWS_DEV, 1), 0, ROWS_DEV)
    row_index = lax.broadcasted_iota(jnp.int32, (ROWS, 1), 0)
    whole_row = row_index % ROWS_DEV == jnp.repeat(chosen, ROWS_DEV, axis=0)
    position = lax.broadcasted_iota(jnp.int32, (ROWS, LENGTH), 1)
    flag_rows = jnp.where(whole_row, 0, starts)
    flag_rows = jnp.where(position == 0, 1, flag_rows)
    return flag_rows.astype(jnp.int32)


def levels(own_key, dims, cuts, low, high):
    def one(axis_at, blocks):
        steps = jax.random.uniform(jax.random.fold_in(jax.random.fold_in(own_key, 6), axis_at), (blocks,), jnp.float32, low / len(cuts), high / len(cuts))
        return jnp.repeat(jnp.exp(steps), dims[axis_at] // blocks).reshape((-1,) + (1,) * (len(dims) - axis_at - 1))

    loudness = one(*cuts[0])
    for cut in cuts[1:]:
        loudness = loudness * one(*cut)
    return loudness


def scatter_about(own_key, dims, scale, reach, pieces=(), held_as=jnp.bfloat16):
    array = scale * jax.random.normal(own_key, dims, jnp.float32)
    if pieces:
        array = array * levels(own_key, dims, pieces, -0.22, 0.18)
    return jnp.clip(array, -reach, reach).astype(held_as)


def setup_inputs(seed: int = 0) -> dict:
    keys = jax.random.split(jax.random.key(seed), 15)
    return {
        "inputs": scatter_about(keys[0], (ROWS, LENGTH, H), 1.0, 6.0, ((0, 4), (1, 8))),
        "resets": draw_resets(jax.random.fold_in(keys[14], 71), 0),
        "norm_gains": jnp.clip(1.0 + 0.1 * jax.random.normal(keys[2], (2, H), jnp.float32), 0.5, 1.5),
        "lam_re": draw_lam_re(jax.random.fold_in(keys[14], 71), 0),
        "lam_im": jnp.clip(jax.random.uniform(keys[4], (2, P_SIZE), jnp.float32, -3.140625, 3.140625), -3.140625, 3.140625),
        "time_steps": draw_time_steps(jax.random.fold_in(keys[14], 71), 0),
        "b_re": scatter_about(keys[6], (2, H, P_SIZE), H ** -0.5, 0.25),
        "b_im": scatter_about(keys[7], (2, H, P_SIZE), H ** -0.5, 0.25),
        "c_re": scatter_about(keys[8], (2, P_SIZE, H), (2 * P_SIZE) ** -0.5, 0.21875),
        "c_im": scatter_about(keys[9], (2, P_SIZE, H), (2 * P_SIZE) ** -0.5, 0.21875),
        "skip_weight": scatter_about(keys[10], (2, H), 0.5, 3.0, (), jnp.float32),
        "glu_w": scatter_about(keys[11], (2, H, H), H ** -0.5, 0.25),
        "glu_bias": scatter_about(keys[12], (2, H), 0.5, 3.0, (), jnp.float32),
        "cotangent": scatter_about(keys[13], (ROWS, LENGTH, H), 1.0, 6.0, ((0, 4), (1, 8))),
    }


NORM_EPS = 1e-05

@jax.custom_vjp
def low(v):
    return lax.optimization_barrier(v.astype(jnp.bfloat16)).astype(jnp.float32)

@jax.custom_vjp
def low_back(v):
    return v

def low_keep(v):
    return (low(v), None)

def low_pass(kept, grad):
    return (grad,)

def back_keep(v):
    return (v, None)

def back_low(kept, grad):
    return (low(grad),)
low.defvjp(low_keep, low_pass)
low_back.defvjp(back_keep, back_low)

def matmul_high(left, right):
    return jnp.dot(left, right, precision=lax.Precision.HIGHEST, preferred_element_type=jnp.float32)

def discretize(lam_re, lam_im, time_steps):
    growth = lam_re * time_steps
    angles = lam_im * time_steps
    magnitude = jnp.exp(growth)
    a_re = magnitude * jnp.cos(angles)
    a_im = magnitude * jnp.sin(angles)
    e_re = jnp.expm1(growth) * jnp.cos(angles) - 2.0 * jnp.sin(0.5 * angles) ** 2
    modulus = lam_re * lam_re + lam_im * lam_im
    q_re = (e_re * lam_re + a_im * lam_im) / modulus
    q_im = (a_im * lam_re - e_re * lam_im) / modulus
    return (a_re, a_im, q_re, q_im)

def combine(earlier, latter):
    dec_re = latter[0] * earlier[0] - latter[1] * earlier[1]
    dec_im = latter[0] * earlier[1] + latter[1] * earlier[0]
    sta_re = latter[0] * earlier[2] - latter[1] * earlier[3] + latter[2]
    sta_im = latter[0] * earlier[3] + latter[1] * earlier[2] + latter[3]
    return (dec_re, dec_im, sta_re, sta_im)

def normalize(hidden, gain_row):
    average = lax.optimization_barrier(jnp.mean(hidden, axis=-1, keepdims=True))
    centred = hidden - average
    spread = lax.optimization_barrier(jnp.mean(centred * centred, axis=-1, keepdims=True))
    return centred * lax.rsqrt(spread + NORM_EPS) * gain_row

def block_pass(decay_pair, carry_pair, block_data):
    v_re, v_im, kept_mask = block_data
    scanned = lax.associative_scan(combine, (kept_mask[:, None] * decay_pair[0], kept_mask[:, None] * decay_pair[1], v_re, v_im), axis=0)
    x_re = scanned[2] + scanned[0] * carry_pair[0] - scanned[1] * carry_pair[1]
    x_im = scanned[3] + scanned[0] * carry_pair[1] + scanned[1] * carry_pair[0]
    return ((x_re[-1], x_im[-1]), (x_re, x_im))

def recurrence(v_re, v_im, a_re, a_im, kept_mask):
    blocks = LENGTH // GROUP
    shaped = (v_re.reshape(blocks, GROUP, P_SIZE), v_im.reshape(blocks, GROUP, P_SIZE), kept_mask.reshape(blocks, GROUP))
    start_pair = (jnp.zeros((P_SIZE,), jnp.float32), jnp.zeros((P_SIZE,), jnp.float32))
    stepper = jax.checkpoint(partial(block_pass, (a_re, a_im)))
    _, (x_re, x_im) = lax.scan(stepper, start_pair, shaped)
    return (x_re.reshape(LENGTH, P_SIZE), x_im.reshape(LENGTH, P_SIZE))

def sublayer(hidden, kept_f, kept_r, weights, forward):
    gain_row, lam_re, lam_im, time_steps, b_re, b_im, c_re, c_im, skip_row, glu_w, glu_bias = weights
    u_low = low(normalize(hidden, gain_row))
    a_re, a_im, q_re, q_im = discretize(lam_re, lam_im, time_steps)
    input_matrix = low(jnp.concatenate([q_re * b_re - q_im * b_im, q_re * b_im + q_im * b_re], axis=1))
    driven = low_back(matmul_high(u_low, input_matrix))
    v_re = driven[:, :P_SIZE]
    v_im = driven[:, P_SIZE:]
    if forward:
        x_re, x_im = recurrence(v_re, v_im, a_re, a_im, kept_f)
    else:
        x_re, x_im = recurrence(jnp.flip(v_re, 0), jnp.flip(v_im, 0), a_re, a_im, jnp.flip(kept_r, 0))
        x_re = jnp.flip(x_re, 0)
        x_im = jnp.flip(x_im, 0)
    state_low = low(jnp.concatenate([x_re, x_im], axis=-1))
    output_matrix = jnp.concatenate([c_re, -c_im], axis=0)
    pre_act = low_back(matmul_high(state_low, output_matrix) + skip_row * u_low)
    gelu_out = jax.nn.gelu(pre_act, approximate=False)
    pre_gate = low_back(matmul_high(low(gelu_out), glu_w) + glu_bias)
    return hidden + gelu_out * jax.nn.sigmoid(pre_gate)

def forward_pass(hidden, kept_f, kept_r, weights):
    layer_one = tuple((tensor[0] for tensor in weights))
    layer_two = tuple((tensor[1] for tensor in weights))
    middle = sublayer(hidden, kept_f, kept_r, layer_one, True)
    return sublayer(middle, kept_f, kept_r, layer_two, False)

def reference(inputs, resets, norm_gains, lam_re, lam_im, time_steps, b_re, b_im, c_re, c_im, skip_weight, glu_w, glu_bias, cotangent):
    weights = tuple((tensor.astype(jnp.float32) for tensor in (norm_gains, lam_re, lam_im, time_steps, b_re, b_im, c_re, c_im, skip_weight, glu_w, glu_bias)))

    def row_step(totals, row_data):
        row_input, row_resets, row_cotangent = row_data
        kept_f = 1.0 - row_resets.astype(jnp.float32)
        kept_r = jnp.concatenate([kept_f[1:], jnp.ones((1,), jnp.float32)])

        def row_forward(hidden, params):
            return forward_pass(hidden, kept_f, kept_r, params)
        result, pull = jax.vjp(row_forward, row_input.astype(jnp.float32), weights)
        d_input, d_weights = pull(row_cotangent.astype(jnp.float32))
        totals = tuple((total_item + grad_item for total_item, grad_item in zip(totals, d_weights)))
        return (totals, (result.astype(jnp.bfloat16), d_input.astype(jnp.bfloat16)))
    zero_sums = tuple((jnp.zeros_like(tensor) for tensor in weights))
    totals, (output, input_grad) = lax.scan(row_step, zero_sums, (inputs, resets, cotangent))
    return (output, input_grad, totals[0], totals[1], totals[2], totals[3], totals[4], totals[5], totals[6], totals[7], totals[8], totals[9], totals[10])
```

```python
import functools
import math

import jax
import jax.numpy as jnp
from jax import lax
from jax.experimental import pallas as pl
from jax.experimental.pallas import tpu as pltpu
from jax.sharding import PartitionSpec as P

NORM_EPS = 1e-05
MESH = pl.DeviceIdType.MESH
F32 = jnp.float32
BF16 = jnp.bfloat16
SUB = 8
UNROLL = 4
TILE = 128
CLEAR = 99.0
STEPS = [128, 128, 256, 256, 128, 128]
ORDERS = [
    "zx", "xy", "yx", "zx", "zx", "xy", "zy", "yx", "yx", "zx", "xy", "xy", "xy", "yx", "xy",
    "zy", "xy", "xy", "zy", "xy", "xy", "yx", "yz",
]


class Refs:
    pass


def horner(value, coeffs):
    total = coeffs[-1]
    for coeff in coeffs[-2::-1]:
        total = total * value + coeff
    return total


def discretize(lam_re, lam_im, time_steps):
    growth = lam_re * time_steps
    angles = lam_im * time_steps
    square = angles * angles
    fact = math.factorial
    grow = growth * horner(growth, [1.0 / fact(k + 1) for k in range(8)])
    sine = angles * horner(square, [(-1.0) ** k / fact(2 * k + 1) for k in range(7)])
    dip = square * horner(square, [(-1.0) ** k / fact(2 * k + 2) for k in range(7)])
    cosine = 1.0 - dip
    magnitude = 1.0 + grow
    a_re = magnitude * cosine
    a_im = magnitude * sine
    e_re = grow * cosine - dip
    modulus = lam_re * lam_re + lam_im * lam_im
    q_re = (e_re * lam_re + a_im * lam_im) / modulus
    q_im = (a_im * lam_re - e_re * lam_im) / modulus
    return (a_re, a_im, q_re, q_im)


def cmul(a, b):
    return (a[0] * b[0] - a[1] * b[1], a[0] * b[1] + a[1] * b[0])


def dot(a, b):
    return jnp.dot(a, b, preferred_element_type=F32)


def dot_nt(a, b):
    return lax.dot_general(a, b, (((1,), (1,)), ((), ())), preferred_element_type=F32)


def dot_tn(a, b):
    return lax.dot_general(a, b, (((0,), (0,)), ((), ())), preferred_element_type=F32)


def fold(value):
    rows, cols = value.shape
    return jnp.sum(value.reshape(rows // SUB, SUB, cols), axis=0)


def gauss(y):
    size = jnp.abs(y) * (0.5**0.5)
    bell = jnp.exp(-0.5 * (y * y))
    t = 1.0 / (1.0 + 0.3275911 * size)
    tail = (0.5 * t * bell) * horner(
        t, [0.254829592, -0.284496736, 1.421413741, -1.453152027, 1.061405429]
    )
    cdf = jnp.where(y >= 0.0, 1.0 - tail, tail)
    return cdf, y * bell * ((2.0 * math.pi) ** -0.5)


class Chunk:
    def __init__(self, index, grad, rows, cols, bits):
        self.index, self.grad, self.rows, self.cols, self.bits = index, grad, rows, cols, bits
        self.width = cols[1] - cols[0]
        self.stages = []
        size, land = rows, 0
        for bit in bits:
            halved = size % (2 * SUB) == 0
            size = size // 2 if halved else size
            self.stages.append((bit, size, halved, land))
            land += size
        self.land_rows = land
        self.steps = [("sum", i) for i in range(len(bits))]
        self.steps += [("get", i) for i in reversed(range(len(bits))) if self.stages[i][2]]


def plan_chunks(n_tm, n_rows, width, P2):
    tm_bits, row_bits = int(math.log2(n_tm)), int(math.log2(n_rows))
    core = [("tm", 0)]
    half = (tm_bits - 1) // 2
    xs = [("tm", 1 + k) for k in range(half)]
    ys = [("tm", 1 + half + k) for k in range(tm_bits - 1 - half)]
    zs = [("rows", k) for k in range(row_bits)]
    axes = {"x": xs, "y": ys, "z": zs[:1]}

    def order(first, second):
        third = ({"x", "y", "z"} - {first, second}).pop()
        return core + axes[first] + axes[second] + axes[third] + zs[1:]

    chunks = {}
    count = 0
    plan, steps = iter(ORDERS), iter(STEPS)
    for l in (1, 0):
        for name, rows, cols in (("w", width, width), ("c", P2, width), ("b", width, P2)):
            step = next(steps)
            for k in range(0, cols, step):
                chunks[name, l, k] = Chunk(
                    count, (name, l), rows, (k, k + step), order(*next(plan))
                )
                count += 1
    chunks["s"] = Chunk(count, ("s", None), 2 * SUB, (0, width), order("y", "x"))
    return chunks


class Mover:
    RATE = {"c": 650e3, "x": 44e3, "y": 44e3, "z": 44e3, "mid": 44e3}
    DELAY = {"c": 0.9, "x": 2.3, "y": 2.3, "z": 2.3}
    AHEAD = 2.5

    def __init__(self, chunks, refs, lands, at, half_bits):
        self.chunks, self.refs, self.at, self.half_bits = chunks, refs, at, half_bits
        self.lands = lands
        self.now = 0.0
        self.free = {k: 0.0 for k in self.RATE}
        self.queue = {k: [] for k in self.DELAY}
        self.pending = []
        self.copies = {}
        self.sent = []
        self.starts = {}
        self.clear = None

    def coord(self, bit):
        return lax.rem(self.at[bit[0]] // (1 << bit[1]), 2)

    def peer(self, bit):
        own = self.at[bit[0]]
        return {bit[0]: own + (1 - 2 * self.coord(bit)) * (1 << bit[1])}

    def begin(self, chunk, level):
        key = (chunk.rows, tuple(chunk.bits[:level]))
        if key not in self.starts:
            if level == 0:
                self.starts[key] = 0
            else:
                bit, size, halved, _ = chunk.stages[level - 1]
                before = self.begin(chunk, level - 1)
                self.starts[key] = before + self.coord(bit) * size if halved else before
        return self.starts[key]

    def view(self, chunk, start, size, done=False):
        ref = self.refs[1 if done else 0][chunk.grad[0]]
        rows = pl.ds(pl.multiple_of(start, SUB) if not isinstance(start, int) else start, size)
        cols = pl.ds(chunk.cols[0], chunk.width)
        l = chunk.grad[1]
        return ref.at[rows, cols] if l is None else ref.at[l, rows, cols]

    def link(self, bit):
        if bit[0] == "rows":
            return "z"
        return "c" if bit[1] == 0 else ("x" if bit[1] <= self.half_bits else "y")

    def cost(self, chunk, k):
        bit, size, _, _ = chunk.stages[chunk.steps[k][1]]
        return size * chunk.width * 4 / self.RATE[self.link(bit)]

    def left(self, chunk, k):
        total = 0.0
        for j in range(k, len(chunk.steps)):
            bit = chunk.stages[chunk.steps[j][1]][0]
            total += self.cost(chunk, j) + self.DELAY[self.link(bit)]
        return total

    def push(self, chunk, k):
        bit = chunk.stages[chunk.steps[k][1]][0]
        self.queue[self.link(bit)].append((-self.left(chunk, k), chunk.index, k, chunk))

    def pump(self):
        for link, queue in self.queue.items():
            while queue and self.free[link] < self.now + self.AHEAD:
                item = min(queue, key=lambda entry: entry[:3])
                if self.clear is not None and link in ("x", "y"):
                    end = max(self.now, self.free[link]) + self.cost(item[3], item[2])
                    if end > self.clear:
                        break
                queue.remove(item)
                self.launch(item[3], item[2])

    def keep_clear(self, after):
        self.clear = None if after is None else self.now + after
        if after is None:
            self.pump()

    def launch(self, chunk, k):
        kind, i = chunk.steps[k]
        bit, size, halved, land = chunk.stages[i]
        if self.refs is not None:
            if kind == "sum":
                before = self.begin(chunk, i)
                if halved:
                    before = before + (1 - self.coord(bit)) * size
                src = self.view(chunk, before, size)
                dst = self.lands[chunk.index].at[pl.ds(land, size)]
            else:
                src = dst = self.view(chunk, self.begin(chunk, i + 1), size, True)
            copy = pltpu.make_async_remote_copy(
                src,
                dst,
                self.refs[2].at[chunk.index, k],
                self.refs[3].at[chunk.index, k],
                device_id=self.peer(bit),
                device_id_type=MESH,
            )
            copy.start()
            self.copies[chunk.index, k] = copy
        link = self.link(bit)
        cost = self.cost(chunk, k)
        far = link == "z" and bit[1] > 0
        began = max(self.now, self.free[link], self.free["mid"] if far else 0.0)
        self.free[link] = done = began + cost
        if far:
            self.free["mid"] = done = began + 2 * cost
        self.pending.append((done + self.DELAY[link], chunk.index, k, chunk))
        self.now += 0.04

    def finish(self, item):
        _, _, k, chunk = item
        kind, i = chunk.steps[k]
        bit, size, halved, land = chunk.stages[i]
        real = self.refs is not None
        copy = self.copies.get((chunk.index, k))
        if real:
            copy.wait_recv()
            if halved:
                self.sent.append(copy)
            else:
                copy.wait_send()
        self.now += 0.08
        more = k + 1 < len(chunk.steps)
        if kind == "get":
            if more:
                self.push(chunk, k + 1)
            self.pump()
            return
        start = self.begin(chunk, i + 1) if real else 0

        def add(off, rows):
            self.now += rows * chunk.width * 4 / 3e6
            if not real:
                return
            ref = self.view(chunk, start + off, rows)
            at = land + off
            at = pl.multiple_of(at, SUB) if not isinstance(at, int) else at
            last = i + 1 == len(chunk.bits)
            into = self.view(chunk, start + off, rows, True) if last else ref
            into[...] = ref[...] + self.lands[chunk.index][pl.ds(at, rows), :]

        if i + 1 < len(chunk.bits) and chunk.stages[i + 1][2]:
            half = size // 2
            mine = self.coord(chunk.stages[i + 1][0]) if real else 0
            add((1 - mine) * half, half)
            self.push(chunk, k + 1)
            self.pump()
            add(mine * half, half)
        else:
            add(0, size)
            if more:
                self.push(chunk, k + 1)
            self.pump()

    def first(self):
        return min(self.pending, key=lambda item: item[:3])

    def start(self, chunk):
        self.push(chunk, 0)
        self.pump()

    def run(self, spent):
        self.now += spent
        while self.pending and self.first()[0] <= self.now:
            item = self.first()
            self.pending.remove(item)
            self.finish(item)

    def drain(self):
        while self.pending:
            item = self.first()
            self.pending.remove(item)
            self.now = max(self.now, item[0])
            self.finish(item)
        if self.refs is not None:
            for copy in self.sent:
                copy.wait_send()


def kernel(cfg, *refs):
    tokens, width, states, rows_dev, group, n_tm, n_rows, chunks = cfg
    R = Refs()
    (
        R.inputs, R.resets_in, R.gains_in, R.lam_re_in, R.lam_im_in, R.steps_in, R.b_re, R.b_im,
        R.c_re, R.c_im, R.skip_in, R.glu_w, R.glu_b_in, R.cot, R.out, R.in_grad, R.small_o, R.b_o,
        R.c_o, R.w_o, R.xin, R.cin, R.wb_re, R.wb_im, R.wc, R.wg, R.h1, R.h2, R.z1, R.z2, R.r1,
        R.r2, R.u1, R.u2, R.v, R.x1, R.x2, R.s1, R.s2, R.gl1, R.gl2, R.gd1, R.gate1, R.prod1,
        R.d_mid, R.dy1, R.dy2, R.ds1, R.ds2, R.dv1, R.dv2, R.m1, R.m2, R.keep, R.stage, R.result, R.small_g,
        R.b_g, R.c_g, R.w_g, R.msg, R.got, R.in_sem, R.send_sem,
        R.recv_sem, R.put_sem, R.get_sem, R.resets, R.gains, R.lam_re, R.lam_im, R.steps, R.skip,
        R.glu_b,
        *lands,
    ) = refs
    segs = SUB
    per_seg = group // segs
    at = lax.axis_index("tm")
    P2 = 2 * states

    barrier = pltpu.get_barrier_semaphore()
    others = [lax.rem(at + k, n_tm) for k in range(1, n_tm)]
    for other in others:
        pl.semaphore_signal(barrier, inc=1, device_id={"tm": other}, device_id_type=MESH)
    row_at = lax.axis_index("rows")
    grads = {"b": R.b_g, "c": R.c_g, "w": R.w_g, "s": R.small_g}
    sums = {"b": R.b_o, "c": R.c_o, "w": R.w_o, "s": R.small_o}
    mover_refs = (grads, sums, R.put_sem, R.get_sem)
    half_bits = (int(math.log2(n_tm)) - 1) // 2
    mover = Mover(chunks, mover_refs, lands, {"tm": at, "rows": row_at}, half_bits)
    row_bits = int(math.log2(n_rows))
    for k in range(row_bits):
        pl.semaphore_signal(
            barrier, inc=1, device_id=mover.peer(("rows", k)), device_id_type=MESH
        )

    def load(k, src, dst):
        copy = pltpu.make_async_copy(src, dst, R.in_sem.at[k])
        copy.start()
        return copy

    cp_x = [load(r, R.inputs.at[r], R.xin.at[pl.ds(r * group, group)]) for r in range(rows_dev)]
    k0 = 2 * rows_dev + 5
    pairs = [
        (R.resets_in, R.resets), (R.lam_re_in, R.lam_re), (R.lam_im_in, R.lam_im),
        (R.steps_in, R.steps), (R.gains_in, R.gains), (R.skip_in, R.skip), (R.glu_b_in, R.glu_b),
    ]
    cp_small = [load(k0 + k, src, dst) for k, (src, dst) in enumerate(pairs)]
    k0 = rows_dev
    cp_b = [load(k0, R.b_re, R.wb_re), load(k0 + 1, R.b_im, R.wb_im)]
    cp_c = [
        load(k0 + 2, R.c_re, R.wc.at[:, pl.ds(0, states)]),
        load(k0 + 3, R.c_im, R.wc.at[:, pl.ds(states, states)]),
    ]
    cp_w = [load(k0 + 4, R.glu_w, R.wg)]
    cp_t = [
        load(k0 + 5 + r, R.cot.at[r], R.cin.at[pl.ds(r * group, group)])
        for r in range(rows_dev)
    ]

    for cp in cp_small:
        cp.wait()

    place_bits = int(math.log2(per_seg))
    i0 = lax.broadcasted_iota(jnp.int32, (group, group), 0)
    i1 = lax.broadcasted_iota(jnp.int32, (group, group), 1)
    hit = i1 == (i0 & (SUB - 1)) * per_seg + (i0 >> 3)
    gather = jnp.where(hit, 1.0, 0.0).astype(BF16)
    kept = 1.0 - R.resets[...].astype(F32)
    for r in range(rows_dev):
        spread = jnp.where(hit, jnp.broadcast_to(kept[r : r + 1], (group, group)), 0.0)
        R.keep[r * group : (r + 1) * group, :] = dot(
            spread.astype(BF16), jnp.ones((group, 128), BF16)
        )

    seg_id = lax.broadcasted_iota(jnp.int32, (SUB, 128), 0)

    def shift(value, forward, by=1):
        return pltpu.roll(value, by if forward else SUB - by, 0)

    def wide(mask, cols):
        return jnp.concatenate([mask] * (cols // 128), axis=1)

    def inside(forward, by):
        return seg_id >= by if forward else seg_id < SUB - by

    window, excl, total_mask = {}, {}, {}
    for r in range(rows_dev):
        places = [R.keep[r * group + j * SUB : r * group + (j + 1) * SUB] for j in range(per_seg)]
        while len(places) > 1:
            places = [a * b for a, b in zip(places[::2], places[1::2])]
        for forward in (True, False):
            run, seen = places[0], places[0]
            for by in (1, 2, 4):
                ok = inside(forward, by)
                window[r, forward, by] = jnp.where(ok, run, 0.0)
                seen = jnp.where(ok, seen * shift(seen, forward, by), seen)
                run = run * shift(run, forward, by)
            excl[r, forward] = jnp.where(inside(forward, 1), shift(seen, forward), 1.0)
            if forward:
                total_mask[r] = seen[SUB - 1 : SUB]

    L = []
    for l in range(2):
        lam = [n[l : l + 1, :] for n in (R.lam_re, R.lam_im, R.steps)]
        a_re, a_im, q_re, q_im = discretize(*lam)
        power = (a_re, a_im)
        for _ in range(place_bits):
            power = cmul(power, power)
        powers = {1: power}
        for by in (1, 2, 4):
            powers[2 * by] = cmul(powers[by], powers[by])
        for forward in (True, False):
            index = wide(seg_id if forward else SUB - 1 - seg_id, states)
            at_seg = (jnp.ones((SUB, states), F32), jnp.zeros((SUB, states), F32))
            for by in (1, 2, 4):
                more = cmul(at_seg, powers[by])
                at_seg = tuple(
                    jnp.where((index & by) != 0, m, o) for m, o in zip(more, at_seg)
                )
            powers[forward, 0] = at_seg
        L.append(dict(lam=lam, a=(a_re, a_im), q=(q_re, q_im), powers=powers, l=l))

    def input_matrix(layer, m_ref):
        q_re, q_im = layer["q"]
        l = layer["l"]
        step = 128
        for i in range(width // step):
            sl = slice(i * step, (i + 1) * step)
            br = R.wb_re[l, sl, :].astype(F32)
            bi = R.wb_im[l, sl, :].astype(F32)
            m_ref[sl, 0:states] = (q_re * br - q_im * bi).astype(BF16)
            m_ref[sl, states:P2] = (q_re * bi + q_im * br).astype(BF16)

    def scan_pass(r, layer, forward, start, sink):
        a = [jnp.broadcast_to(p, (SUB, states)) for p in layer["a"]]
        v_ref, keep_ref = R.v, R.keep

        def one(j, carry):
            base = pl.multiple_of(r * group + j * SUB, SUB)
            keep = wide(keep_ref[pl.ds(base, SUB), :], states)
            v = (v_ref[pl.ds(base, SUB), 0:states], v_ref[pl.ds(base, SUB), states:P2])
            if forward:
                held = (keep * carry[0], keep * carry[1])
                prod = cmul(a, held)
                x = (prod[0] + v[0], prod[1] + v[1])
                return x, held, x
            prod = cmul(a, carry)
            x = (prod[0] + v[0], prod[1] + v[1])
            held = (keep * x[0], keep * x[1])
            return x, carry, held

        pair = 2

        def body(i, carry):
            state, extra = carry
            if forward:
                js = [i * pair + k for k in range(pair)]
            else:
                js = [per_seg - 1 - (i * pair + k) for k in range(pair)]
            xs = []
            for j in js:
                x, held, state = one(j, state)
                xs.append(x)
                if sink is not None:
                    extra = sink.each(r * group + j * SUB, x, held, extra)
            if sink is not None:
                low = js[0] if forward else js[-1]
                ordered = xs if forward else xs[::-1]
                sink.pair(r * group + low * SUB, ordered)
            return state, extra

        extra0 = sink.zero() if sink is not None else ()
        return lax.fori_loop(0, per_seg // pair, body, (start, extra0), unroll=UNROLL)

    class Forward:
        def __init__(self, x_ref, s_ref):
            self.x_ref, self.s_ref = x_ref, s_ref

        def zero(self):
            return ()

        def each(self, base, x, held, extra):
            base = pl.multiple_of(base, SUB)
            self.x_ref[pl.ds(base, SUB), 0:states] = x[0]
            self.x_ref[pl.ds(base, SUB), states:P2] = x[1]
            return extra

        def pair(self, base, xs):
            base = pl.multiple_of(base, 2 * SUB)
            re = jnp.concatenate([x[0] for x in xs], axis=0)
            im = jnp.concatenate([x[1] for x in xs], axis=0)
            self.s_ref[pl.ds(base, 2 * SUB), 0:states] = re.astype(BF16)
            self.s_ref[pl.ds(base, 2 * SUB), states:P2] = (-im).astype(BF16)

    class Adjoint:
        def __init__(self, x_ref, d_ref):
            self.x_ref, self.d_ref = x_ref, d_ref

        def zero(self):
            return (jnp.zeros((SUB, states), F32), jnp.zeros((SUB, states), F32))

        def each(self, base, x, held, extra):
            base = pl.multiple_of(base, SUB)
            xv = (self.x_ref[pl.ds(base, SUB), 0:states], self.x_ref[pl.ds(base, SUB), states:P2])
            prod = cmul(xv, held)
            return (extra[0] + prod[0], extra[1] + prod[1])

        def pair(self, base, xs):
            base = pl.multiple_of(base, 2 * SUB)
            re = jnp.concatenate([x[0] for x in xs], axis=0)
            im = jnp.concatenate([x[1] for x in xs], axis=0)
            self.d_ref[pl.ds(base, 2 * SUB), 0:states] = re.astype(BF16)
            self.d_ref[pl.ds(base, 2 * SUB), states:P2] = (-im).astype(BF16)

    first_wait = [True]

    def send_carry(e, r, layer, forward, ends):
        seen = ends
        for by in (1, 2, 4):
            mask = wide(window[r, forward, by], states)
            prod = cmul(layer["powers"][by], tuple(shift(p, forward, by) for p in seen))
            seen = (seen[0] + mask * prod[0], seen[1] + mask * prod[1])
        ok = wide(inside(forward, 1), states)
        run = tuple(jnp.where(ok, shift(p, forward), 0.0) for p in seen)
        last = slice(SUB - 1, SUB) if forward else slice(0, 1)
        R.msg[e, r, :, 0:states] = seen[0][last]
        R.msg[e, r, :, states:P2] = seen[1][last]
        R.msg[e, r, :, P2 : P2 + 128] = total_mask[r]
        if first_wait[0]:
            pl.semaphore_wait(barrier, n_tm - 1 + row_bits)
            first_wait[0] = False
        copies = []
        for k, other in enumerate(others):
            copy = pltpu.make_async_remote_copy(
                R.msg.at[e, r],
                R.got.at[e, r, at],
                R.send_sem.at[e, r, k],
                R.recv_sem.at[e, r, k],
                device_id={"tm": other},
                device_id_type=MESH,
            )
            copy.start()
            copies.append(copy)
        return copies, run

    def take_carry(e, r, layer, forward, sent):
        copies, run = sent
        for copy in copies:
            copy.wait()
        span = layer["powers"][SUB]
        carry = (jnp.zeros((1, states), F32), jnp.zeros((1, states), F32))
        order = range(n_tm) if forward else range(n_tm - 1, -1, -1)
        for k in list(order)[:-1]:
            before = (at > k) if forward else (at < k)
            mask = wide(R.got[e, r, k, :, P2 : P2 + 128], states)
            prod = cmul(span, carry)
            new = (
                R.got[e, r, k, :, 0:states] + mask * prod[0],
                R.got[e, r, k, :, states:P2] + mask * prod[1],
            )
            carry = tuple(jnp.where(before, n, c) for n, c in zip(new, carry))
        prod = cmul(layer["powers"][forward, 0], carry)
        mask = wide(excl[r, forward], states)
        return (run[0] + mask * prod[0], run[1] + mask * prod[1])

    zero_state = (jnp.zeros((SUB, states), F32), jnp.zeros((SUB, states), F32))

    tiles = {
        r: [(slice(r * group + i, r * group + i + TILE), slice(i, i + TILE)) for i in range(0, group, TILE)]
        for r in range(rows_dev)
    }
    line = [slice(r * group, (r + 1) * group) for r in range(rows_dev)]
    rows = range(rows_dev)

    def norm_front(h, layer, z_ref, r_ref, u_ref, m_ref, sl):
        mean = jnp.mean(h, axis=1, keepdims=True)
        centred = h - mean
        var = jnp.mean(centred * centred, axis=1, keepdims=True)
        r = lax.rsqrt(var + NORM_EPS)
        z = centred * r
        u = (z * R.gains[layer["l"] : layer["l"] + 1, :]).astype(BF16)
        z_ref[sl, :] = z
        r_ref[sl, :] = jnp.broadcast_to(r, (r.shape[0], 128))
        u_ref[sl, :] = u
        R.v[sl, :] = dot(u, m_ref[...])

    def mixer(layer, s_ref, u_ref, gl_ref, sl):
        l = layer["l"]
        s = s_ref[sl, :]
        y = dot(s, R.wc[l]) + R.skip[l : l + 1, :] * u_ref[sl, :].astype(F32)
        cdf, dens = gauss(y)
        gelu = y * cdf
        low = gelu.astype(BF16)
        gl_ref[sl, :] = low
        pre = dot(low, R.wg[l]) + R.glu_b[l : l + 1, :]
        gate = 1.0 / (1.0 + jnp.exp(-pre))
        gated = gelu * gate
        return gated, cdf + dens, gate, gated * (1.0 - gate)

    def back_front(layer, d_out, slope, gate, prod, u_ref, ds_ref, dy_ref, sums, sl):
        l = layer["l"]
        ds = (d_out * prod).astype(BF16)
        ds_ref[sl, :] = ds
        d_gelu = d_out * gate + dot_nt(ds, R.wg[l])
        dy = (d_gelu * slope).astype(BF16)
        dy_ref[sl, :] = dy
        R.v[sl, :] = dot_nt(dy, R.wc[l])
        sums["bias"] = sums["bias"] + fold(ds.astype(F32))
        sums["skip"] = sums["skip"] + fold(dy.astype(F32) * u_ref[sl, :].astype(F32))

    def back_norm(layer, d_out, dv_ref, m_ref, dy_ref, z_ref, r_ref, sums, sl):
        l = layer["l"]
        dn = dy_ref[sl, :].astype(F32) * R.skip[l : l + 1, :] + dot_nt(dv_ref[sl, :], m_ref[...])
        z = z_ref[sl, :]
        sums["gain"] = sums["gain"] + fold(dn * z)
        w = dn * R.gains[l : l + 1, :]
        mean_w = jnp.mean(w, axis=1, keepdims=True)
        mean_wz = jnp.mean(w * z, axis=1, keepdims=True)
        r = wide(r_ref[sl, :], width)
        return d_out + r * (w - mean_w - z * mean_wz)

    def fresh():
        return {k: jnp.zeros((SUB, width), F32) for k in ("gain", "skip", "bias")}

    def start(name, l, first, count):
        for k in range(first, first + count, SUB):
            if (name, l, k) in chunks:
                mover.start(chunks[name, l, k])

    def product_grads(layer, gl_ref, ds_ref, s_ref, dy_ref):
        l = layer["l"]
        for name, left, right in (("w", gl_ref, ds_ref), ("c", s_ref, dy_ref)):
            for k in range(0, width, 256):
                grads[name][l, :, k : k + 256] = dot_tn(left[...], right[:, k : k + 256])
                start(name, l, k, 256)
                mover.run(0.25)

    def matrix_grads(layer, u_ref, dv_ref, da):
        l = layer["l"]
        q_re, q_im = layer["q"]
        full = dot_tn(u_ref[...], dv_ref[...])
        g_re, g_im = full[:, 0:states], full[:, states:P2]
        R.b_g[l, :, 0:states] = q_re * g_re + q_im * g_im
        R.b_g[l, :, states:P2] = q_re * g_im - q_im * g_re
        start("b", l, 0, P2)
        br, bi = R.wb_re[l].astype(F32), R.wb_im[l].astype(F32)
        dq_re = jnp.sum(fold(br * g_re + bi * g_im), axis=0, keepdims=True)
        dq_im = jnp.sum(fold(br * g_im - bi * g_re), axis=0, keepdims=True)
        da_re = jnp.sum(da[0], axis=0, keepdims=True)
        da_im = -jnp.sum(da[1], axis=0, keepdims=True)
        _, pull = jax.vjp(discretize, *layer["lam"])
        lam_grads = pull((da_re, da_im, dq_re, dq_im))
        for k, grad in enumerate(lam_grads):
            row = 6 + 2 * k + l
            R.small_g[row : row + 1, 0:states] = grad

    one, two = L
    for cp in cp_b:
        cp.wait()
    input_matrix(one, R.m1)
    for cp in cp_x:
        cp.wait()
    sent = {}
    for r in rows:
        for sl, part in tiles[r]:
            h = dot(gather[part, :], R.xin[line[r], :])
            R.h1[sl, :] = h
            norm_front(h, one, R.z1, R.r1, R.u1, R.m1, sl)
        ends, _ = scan_pass(r, one, True, zero_state, None)
        sent[0, r] = send_carry(0, r, one, True, ends)
    input_matrix(two, R.m2)
    for cp in cp_c + cp_w + cp_t:
        cp.wait()

    for r in rows:
        carry = take_carry(0, r, one, True, sent[0, r])
        scan_pass(r, one, True, carry, Forward(R.x1, R.s1))
        for sl, _ in tiles[r]:
            gated, slope, gate, prod = mixer(one, R.s1, R.u1, R.gl1, sl)
            R.gd1[sl, :] = slope
            R.gate1[sl, :] = gate
            R.prod1[sl, :] = prod
            h = R.h1[sl, :] + gated
            R.h2[sl, :] = h
            norm_front(h, two, R.z2, R.r2, R.u2, R.m2, sl)
        ends, _ = scan_pass(r, two, False, zero_state, None)
        sent[1, r] = send_carry(1, r, two, False, ends)

    sums2 = fresh()
    for r in rows:
        carry = take_carry(1, r, two, False, sent[1, r])
        scan_pass(r, two, False, carry, Forward(R.x2, R.s2))
        for sl, part in tiles[r]:
            gated, slope, gate, prod = mixer(two, R.s2, R.u2, R.gl2, sl)
            R.result[sl, :] = (R.h2[sl, :] + gated).astype(BF16)
            d_out = dot(gather[part, :], R.cin[line[r], :])
            R.d_mid[sl, :] = d_out
            back_front(two, d_out, slope, gate, prod, R.u2, R.ds2, R.dy2, sums2, sl)
        ends, _ = scan_pass(r, two, True, zero_state, None)
        sent[2, r] = send_carry(2, r, two, True, ends)
    product_grads(two, R.gl2, R.ds2, R.s2, R.dy2)

    sums1 = fresh()
    da2, da1 = Adjoint(R.x2, R.dv2).zero(), Adjoint(R.x1, R.dv1).zero()
    for r in rows:
        mover.run(0.5)
        carry = take_carry(2, r, two, True, sent[2, r])
        mover.run(0.5)
        _, da = scan_pass(r, two, True, carry, Adjoint(R.x2, R.dv2))
        da2 = (da2[0] + da[0], da2[1] + da[1])
        mover.run(0.3)
        for sl, _ in tiles[r]:
            d_mid = back_norm(two, R.d_mid[sl, :], R.dv2, R.m2, R.dy2, R.z2, R.r2, sums2, sl)
            R.d_mid[sl, :] = d_mid
            back_front(
                one, d_mid, R.gd1[sl, :], R.gate1[sl, :], R.prod1[sl, :],
                R.u1, R.ds1, R.dy1, sums1, sl,
            )
            mover.run(0.8)
        ends, _ = scan_pass(r, one, False, zero_state, None)
        mover.run(0.3)
        sent[3, r] = send_carry(3, r, one, False, ends)
    R.small_g[...] = jnp.zeros((2 * SUB, width), F32)
    matrix_grads(two, R.u2, R.dv2, da2)
    mover.run(1.0)
    product_grads(one, R.gl1, R.ds1, R.s1, R.dy1)

    for r in rows:
        mover.run(0.5)
        carry = take_carry(3, r, one, False, sent[3, r])
        mover.run(0.5)
        _, da = scan_pass(r, one, False, carry, Adjoint(R.x1, R.dv1))
        da1 = (da1[0] + da[0], da1[1] + da[1])
        mover.run(0.3)
        for sl, _ in tiles[r]:
            d_in = back_norm(one, R.d_mid[sl, :], R.dv1, R.m1, R.dy1, R.z1, R.r1, sums1, sl)
            R.stage[sl, :] = d_in.astype(BF16)
        mover.run(0.6)
    matrix_grads(one, R.u1, R.dv1, da1)
    for k, name in enumerate(("gain", "skip", "bias")):
        for l, sums in enumerate((sums1, sums2)):
            row = 2 * k + l
            R.small_g[row : row + 1, :] = jnp.sum(sums[name], axis=0, keepdims=True)
    mover.start(chunks["s"])
    mover.run(1.0)
    ungather = jnp.where(i1 == (i0 & (per_seg - 1)) * SUB + (i0 >> place_bits), 1.0, 0.0).astype(BF16)
    for r in rows:
        R.in_grad[r] = dot(ungather, R.stage[line[r], :]).astype(BF16)
    mover.run(0.5)
    for r in rows:
        R.out[r] = dot(ungather, R.result[line[r], :]).astype(BF16)
    mover.run(0.5)
    mover.drain()


def finish_kernel(states, out_v, in_grad_v, small_v, b_v, c_v, w_v, *refs):
    out, in_grad, gain, lam_re, lam_im, steps, b_re, b_im, c_re, c_im, skip, w, bias, sem = refs
    pairs = [
        (b_v.at[:, :, pl.ds(0, states)], b_re),
        (b_v.at[:, :, pl.ds(states, states)], b_im),
        (c_v.at[:, pl.ds(0, states)], c_re),
        (c_v.at[:, pl.ds(states, states)], c_im),
        (w_v, w),
        (out_v, out),
        (in_grad_v, in_grad),
    ]
    copies = [pltpu.make_async_copy(a, b, sem.at[k]) for k, (a, b) in enumerate(pairs)]
    for copy in copies:
        copy.start()
    for k, ref in enumerate((gain, skip, bias)):
        ref[...] = small_v[2 * k : 2 * k + 2, :]
    for k, ref in enumerate((lam_re, lam_im, steps)):
        ref[...] = small_v[6 + 2 * k : 8 + 2 * k, 0:states]
    for copy in copies:
        copy.wait()


def on_device(n_tm, n_rows, *args):
    inputs, lam_re = args[0], args[3]
    rows_dev, group, width = inputs.shape
    states = lam_re.shape[1]
    tokens = rows_dev * group
    P2 = 2 * states
    chunks = plan_chunks(n_tm, n_rows, width, P2)
    cfg = (tokens, width, states, rows_dev, group, n_tm, n_rows, chunks)
    vm = pl.BlockSpec(memory_space=pltpu.VMEM)
    hbm = pl.BlockSpec(memory_space=pl.ANY)
    far = pl.BlockSpec(memory_space=pltpu.HBM)
    in_specs = [far] * 14
    out_specs = [vm] * 6
    out_shape = [
        jax.ShapeDtypeStruct(inputs.shape, BF16),
        jax.ShapeDtypeStruct(inputs.shape, BF16),
        jax.ShapeDtypeStruct((2 * SUB, width), F32),
        jax.ShapeDtypeStruct((2, width, P2), F32),
        jax.ShapeDtypeStruct((2, P2, width), F32),
        jax.ShapeDtypeStruct((2, width, width), F32),
    ]

    def big(cols, dtype=F32):
        return pltpu.VMEM((tokens, cols), dtype)

    steps = max(len(chunk.steps) for chunk in chunks.values())
    scratch = [
        big(width, BF16), big(width, BF16),
        pltpu.VMEM((2, width, states), BF16), pltpu.VMEM((2, width, states), BF16),
        pltpu.VMEM((2, P2, width), BF16), pltpu.VMEM((2, width, width), BF16),
        big(width), big(width), big(width), big(width), big(128), big(128),
        big(width, BF16), big(width, BF16), big(P2), big(P2), big(P2),
        big(P2, BF16), big(P2, BF16), big(width, BF16), big(width, BF16),
        big(width), big(width), big(width), big(width),
        big(width, BF16), big(width, BF16), big(width, BF16), big(width, BF16),
        big(P2, BF16), big(P2, BF16),
        pltpu.VMEM((width, P2), BF16), pltpu.VMEM((width, P2), BF16),
        big(128), big(width, BF16), big(width, BF16),
        pltpu.VMEM((2 * SUB, width), F32), pltpu.VMEM((2, width, P2), F32),
        pltpu.VMEM((2, P2, width), F32), pltpu.VMEM((2, width, width), F32),
        pltpu.VMEM((4, rows_dev, 1, P2 + 128), F32),
        pltpu.VMEM((4, rows_dev, n_tm, 1, P2 + 128), F32),
        pltpu.SemaphoreType.DMA((2 * rows_dev + 12,)),
        pltpu.SemaphoreType.DMA((4, rows_dev, n_tm - 1)),
        pltpu.SemaphoreType.DMA((4, rows_dev, n_tm - 1)),
        pltpu.SemaphoreType.DMA((len(chunks), steps)), pltpu.SemaphoreType.DMA((len(chunks), steps)),
    ]
    for k in (1, 2, 3, 4, 5, 10, 12):
        scratch.append(pltpu.VMEM(args[k].shape, args[k].dtype))
    for chunk in chunks.values():
        scratch.append(pltpu.VMEM((chunk.land_rows, chunk.width), F32))
    held = pl.pallas_call(
        functools.partial(kernel, cfg),
        out_shape=[pltpu.VMEM(o.shape, o.dtype) for o in out_shape],
        in_specs=in_specs,
        out_specs=out_specs,
        scratch_shapes=scratch,
        compiler_params=pltpu.CompilerParams(
            collective_id=0, has_side_effects=True, vmem_limit_bytes=53 * 2**20
        ),
    )(*args)
    grads = [args[k] for k in range(2, 13)]
    final_shape = [out_shape[0]] * 2 + [jax.ShapeDtypeStruct(g.shape, F32) for g in grads]
    final_specs = [hbm, hbm] + [vm] * 4 + [hbm] * 4 + [vm, hbm, vm]
    return tuple(
        pl.pallas_call(
            functools.partial(finish_kernel, states),
            out_shape=final_shape,
            in_specs=[hbm, hbm, vm, hbm, hbm, hbm],
            out_specs=final_specs,
            scratch_shapes=[pltpu.SemaphoreType.DMA((7,))],
            compiler_params=pltpu.CompilerParams(vmem_limit_bytes=2**20),
        )(*held)
    )


def solution(mesh):
    rows = P("rows", "tm", None)
    in_specs = (rows, P("rows", "tm")) + (P(),) * 11 + (rows,)
    out_specs = (rows, rows) + (P(),) * 11
    return jax.shard_map(
        functools.partial(on_device, mesh.shape["tm"], mesh.shape["rows"]),
        mesh=mesh,
        in_specs=in_specs,
        out_specs=out_specs,
        check_vma=False,
    )
```

```python
import functools
import math

import jax
import jax.numpy as jnp
from jax import lax
from jax.experimental import pallas as pl
from jax.experimental.pallas import tpu as pltpu
from jax.sharding import PartitionSpec as P

NORM_EPS = 1e-05
MESH = pl.DeviceIdType.MESH
F32 = jnp.float32
BF16 = jnp.bfloat16
SUB = 8
UNROLL = 16
PUTS, GETS = 28, 18
TILE = 256
STEPS = [128, 128, 128, 128, 128, 128]
ORDERS = [
    "zy", "xy", "xy", "yx", "zy", "zx", "yx", "xy", "zy", "yx", "xy", "yz", "xy", "xz", "yx",
    "xy", "xy", "xy", "zx", "zx", "yx", "xy", "yx", "xy", "yx", "xy", "yx", "xy",
]


class Refs:
    pass


def horner(value, coeffs):
    total = coeffs[-1]
    for coeff in coeffs[-2::-1]:
        total = total * value + coeff
    return total


def discretize(lam_re, lam_im, time_steps):
    growth = lam_re * time_steps
    angles = lam_im * time_steps
    square = angles * angles
    fact = math.factorial
    grow = growth * horner(growth, [1.0 / fact(k + 1) for k in range(8)])
    sine = angles * horner(square, [(-1.0) ** k / fact(2 * k + 1) for k in range(7)])
    dip = square * horner(square, [(-1.0) ** k / fact(2 * k + 2) for k in range(7)])
    cosine = 1.0 - dip
    magnitude = 1.0 + grow
    a_re = magnitude * cosine
    a_im = magnitude * sine
    e_re = grow * cosine - dip
    modulus = lam_re * lam_re + lam_im * lam_im
    q_re = (e_re * lam_re + a_im * lam_im) / modulus
    q_im = (a_im * lam_re - e_re * lam_im) / modulus
    return (a_re, a_im, q_re, q_im)


def cmul(a, b):
    return (a[0] * b[0] - a[1] * b[1], a[0] * b[1] + a[1] * b[0])


def dot(a, b):
    return jnp.dot(a, b, preferred_element_type=F32)


def dot_nt(a, b):
    return lax.dot_general(a, b, (((1,), (1,)), ((), ())), preferred_element_type=F32)


def dot_tn(a, b):
    return lax.dot_general(a, b, (((0,), (0,)), ((), ())), preferred_element_type=F32)


def fold(value):
    rows, cols = value.shape
    return jnp.sum(value.reshape(rows // SUB, SUB, cols), axis=0)


def gauss(y):
    size = jnp.abs(y) * (0.5**0.5)
    bell = jnp.exp(-0.5 * (y * y))
    t = pltpu.reciprocal(1.0 + 0.3275911 * size, approx=True)
    tail = (0.5 * t * bell) * horner(
        t, [0.254829592, -0.284496736, 1.421413741, -1.453152027, 1.061405429]
    )
    cdf = jnp.where(y >= 0.0, 1.0 - tail, tail)
    return cdf, y * bell * ((2.0 * math.pi) ** -0.5)


class Chunk:
    def __init__(self, index, grad, rows, cols, bits):
        self.index, self.grad, self.rows, self.cols, self.bits = index, grad, rows, cols, bits
        self.width = cols[1] - cols[0]
        self.stages = []
        size, land = rows, 0
        for bit in bits:
            halved = size % (2 * SUB) == 0
            size = size // 2 if halved else size
            self.stages.append((bit, size, halved, land))
            land += size
        self.land_rows = land
        self.steps = [("sum", i) for i in range(len(bits))]
        self.steps += [("get", i) for i in reversed(range(len(bits))) if self.stages[i][2]]


def plan_chunks(n_tm, n_rows, width, P2):
    tm_bits, row_bits = int(math.log2(n_tm)), int(math.log2(n_rows))
    core = [("tm", 0)]
    half = (tm_bits - 1) // 2
    xs = [("tm", 1 + k) for k in range(half)]
    ys = [("tm", 1 + half + k) for k in range(tm_bits - 1 - half)]
    zs = [("rows", k) for k in range(row_bits)]
    axes = {"x": xs, "y": ys, "z": zs[:1]}

    def order(first, second):
        third = ({"x", "y", "z"} - {first, second}).pop()
        return core + axes[first] + axes[second] + axes[third] + zs[1:]

    chunks = {}
    count = 0
    plan, steps = iter(ORDERS), iter(STEPS)
    for l in (1, 0):
        for name, rows, cols in (("w", width, width), ("c", P2, width), ("b", width, P2)):
            step = next(steps)
            for k in range(0, cols, step):
                chunks[name, l, k] = Chunk(
                    count, (name, l), rows, (k, k + step), order(*next(plan))
                )
                count += 1
    chunks["s"] = Chunk(count, ("s", None), 2 * SUB, (0, width), order("y", "x"))
    return chunks


class Mover:
    RATE = {"c": 650e3, "x": 46e3, "y": 46e3, "z": 46e3, "mid": 46e3}
    DELAY = {"c": 0.8, "x": 1.7, "y": 1.7, "z": 1.7}
    EXCHANGE = 3.2
    AHEAD = 2.5

    def __init__(self, chunks, refs, lands, at, half_bits):
        self.chunks, self.refs, self.at, self.half_bits = chunks, refs, at, half_bits
        self.lands = lands
        self.now = 0.0
        self.free = {k: 0.0 for k in self.RATE}
        self.queue = {k: [] for k in self.DELAY}
        self.pending = []
        self.copies = {}
        self.starts = {}
        self.clock = 0
        self.gets, self.acked, self.puts, self.used = {}, {}, [], {}

    def coord(self, bit):
        return lax.rem(self.at[bit[0]] // (1 << bit[1]), 2)

    def peer(self, bit):
        own = self.at[bit[0]]
        return {bit[0]: own + (1 - 2 * self.coord(bit)) * (1 << bit[1])}

    def begin(self, chunk, level):
        key = (chunk.rows, tuple(chunk.bits[:level]))
        if key not in self.starts:
            if level == 0:
                self.starts[key] = 0
            else:
                bit, size, halved, _ = chunk.stages[level - 1]
                before = self.begin(chunk, level - 1)
                self.starts[key] = before + self.coord(bit) * size if halved else before
        return self.starts[key]

    def view(self, chunk, start, size, done=False):
        ref = self.refs[1 if done else 0][chunk.grad[0]]
        rows = pl.ds(pl.multiple_of(start, SUB) if not isinstance(start, int) else start, size)
        cols = pl.ds(chunk.cols[0], chunk.width)
        l = chunk.grad[1]
        return ref.at[rows, cols] if l is None else ref.at[l, rows, cols]

    def link(self, bit):
        if bit[0] == "rows":
            return "z"
        return "c" if bit[1] == 0 else ("x" if bit[1] <= self.half_bits else "y")

    def cost(self, chunk, k):
        bit, size, _, _ = chunk.stages[chunk.steps[k][1]]
        return size * chunk.width * 4 / self.RATE[self.link(bit)]

    def left(self, chunk, k):
        total = 0.0
        for j in range(k, len(chunk.steps)):
            bit = chunk.stages[chunk.steps[j][1]][0]
            total += self.cost(chunk, j) + self.DELAY[self.link(bit)]
        return total

    def push(self, chunk, k):
        bit = chunk.stages[chunk.steps[k][1]][0]
        self.queue[self.link(bit)].append((-self.left(chunk, k), chunk.index, k, chunk))

    def take_get(self, bit):
        pool = self.gets.setdefault(bit, {})
        for k, released in pool.items():
            if released is not None and released < self.acked.get(bit, 0):
                pool[k] = None
                return k
        k = sum(len(other) for other in self.gets.values())
        pool[k] = None
        return k

    def take_put(self):
        if True in self.puts:
            k = self.puts.index(True)
            self.puts[k] = False
            return k
        self.puts.append(False)
        return len(self.puts) - 1

    def pump(self):
        for link, queue in self.queue.items():
            while queue and self.free[link] < self.now + self.AHEAD:
                item = min(queue, key=lambda entry: entry[:3])
                queue.remove(item)
                self.launch(item[3], item[2])

    def launch(self, chunk, k):
        kind, i = chunk.steps[k]
        bit, size, halved, land = chunk.stages[i]
        put, get = self.take_put(), self.take_get(bit)
        self.clock += 1
        self.used[chunk.index, k] = (put, get, self.clock)
        if self.refs is not None:
            if kind == "sum":
                before = self.begin(chunk, i)
                if halved:
                    before = before + (1 - self.coord(bit)) * size
                src = self.view(chunk, before, size)
                dst = self.lands[chunk.index].at[pl.ds(land, size)]
            else:
                src = dst = self.view(chunk, self.begin(chunk, i + 1), size, True)
            copy = pltpu.make_async_remote_copy(
                src,
                dst,
                self.refs[2].at[put],
                self.refs[3].at[get],
                device_id=self.peer(bit),
                device_id_type=MESH,
            )
            copy.start()
            self.copies[chunk.index, k] = copy
        link = self.link(bit)
        cost = self.cost(chunk, k)
        far = link == "z" and bit[1] > 0
        began = max(self.now, self.free[link], self.free["mid"] if far else 0.0)
        self.free[link] = done = began + cost
        if far:
            self.free["mid"] = done = began + 2 * cost
        self.pending.append((done + self.DELAY[link], chunk.index, k, chunk))
        self.now += 0.04

    def finish(self, item):
        _, _, k, chunk = item
        kind, i = chunk.steps[k]
        bit, size, _, land = chunk.stages[i]
        real = self.refs is not None
        copy = self.copies.get((chunk.index, k))
        if real:
            copy.wait()
        put, get, launched = self.used[chunk.index, k]
        self.clock += 1
        self.puts[put] = True
        self.gets[bit][get] = self.clock
        self.acked[bit] = max(self.acked.get(bit, 0), launched)
        self.now += 0.08
        more = k + 1 < len(chunk.steps)
        if kind == "get":
            if more:
                self.push(chunk, k + 1)
            self.pump()
            return
        start = self.begin(chunk, i + 1) if real else 0

        def add(off, rows):
            self.now += rows * chunk.width * 4 / 3e6
            if not real:
                return
            ref = self.view(chunk, start + off, rows)
            at = land + off
            at = pl.multiple_of(at, SUB) if not isinstance(at, int) else at
            last = i + 1 == len(chunk.bits)
            into = self.view(chunk, start + off, rows, True) if last else ref
            into[...] = ref[...] + self.lands[chunk.index][pl.ds(at, rows), :]

        if i + 1 < len(chunk.bits) and chunk.stages[i + 1][2]:
            half = size // 2
            mine = self.coord(chunk.stages[i + 1][0]) if real else 0
            add((1 - mine) * half, half)
            self.push(chunk, k + 1)
            self.pump()
            add(mine * half, half)
        else:
            add(0, size)
            if more:
                self.push(chunk, k + 1)
            self.pump()

    def first(self):
        return min(self.pending, key=lambda item: item[:3])

    def start(self, chunk):
        self.push(chunk, 0)
        self.pump()

    def run(self, spent):
        self.now += spent
        while self.pending and self.first()[0] <= self.now:
            item = self.first()
            self.pending.remove(item)
            self.finish(item)

    def message(self):
        return max(self.now, self.free["x"], self.free["y"]) + self.EXCHANGE

    def until(self, time):
        while self.pending and self.first()[0] <= time:
            item = self.first()
            self.pending.remove(item)
            self.now = max(self.now, item[0])
            self.finish(item)
        self.now = max(self.now, time)

    def drain(self):
        while self.pending:
            item = self.first()
            self.pending.remove(item)
            self.now = max(self.now, item[0])
            self.finish(item)


def kernel(cfg, *refs):
    tokens, width, states, rows_dev, group, n_tm, n_rows, chunks = cfg
    R = Refs()
    (
        R.inputs, R.resets_in, R.gains_in, R.lam_re_in, R.lam_im_in, R.steps_in, R.b_re, R.b_im,
        R.c_re, R.c_im, R.skip_in, R.glu_w, R.glu_b_in, R.cot, R.out, R.in_grad, R.small_o, R.b_o,
        R.c_o, R.w_o, R.xin, R.cin, R.wb_re, R.wb_im, R.wc, R.wg, R.h1, R.h2, R.z1, R.z2, R.r1,
        R.r2, R.u1, R.u2, R.v, R.x1, R.x2, R.s1, R.s2, R.gl1, R.gl2, R.gd1, R.gate1, R.prod1,
        R.d_mid, R.dy1, R.dy2, R.ds1, R.ds2, R.dv1, R.dv2, R.m1, R.m2, R.keep, R.stage, R.result, R.small_g,
        R.b_g, R.c_g, R.w_g, R.msg, R.got, R.in_sem, R.send_sem,
        R.recv_sem, R.put_sem, R.get_sem, R.resets, R.gains, R.lam_re, R.lam_im, R.steps, R.skip,
        R.glu_b,
        *lands,
    ) = refs
    segs = SUB
    per_seg = group // segs
    at = lax.axis_index("tm")
    P2 = 2 * states

    barrier = pltpu.get_barrier_semaphore()
    others = [lax.rem(at + k, n_tm) for k in range(1, n_tm)]
    for other in others:
        pl.semaphore_signal(barrier, inc=1, device_id={"tm": other}, device_id_type=MESH)
    row_at = lax.axis_index("rows")
    grads = {"b": R.b_g, "c": R.c_g, "w": R.w_g, "s": R.small_g}
    sums = {"b": R.b_o, "c": R.c_o, "w": R.w_o, "s": R.small_o}
    mover_refs = (grads, sums, R.put_sem, R.get_sem)
    half_bits = (int(math.log2(n_tm)) - 1) // 2
    mover = Mover(chunks, mover_refs, lands, {"tm": at, "rows": row_at}, half_bits)
    row_bits = int(math.log2(n_rows))
    for k in range(row_bits):
        pl.semaphore_signal(
            barrier, inc=1, device_id=mover.peer(("rows", k)), device_id_type=MESH
        )

    def load(k, src, dst):
        copy = pltpu.make_async_copy(src, dst, R.in_sem.at[k])
        copy.start()
        return copy

    cp_x = [load(r, R.inputs.at[r], R.xin.at[pl.ds(r * group, group)]) for r in range(rows_dev)]
    k0 = 2 * rows_dev + 5
    pairs = [
        (R.resets_in, R.resets), (R.lam_re_in, R.lam_re), (R.lam_im_in, R.lam_im),
        (R.steps_in, R.steps), (R.gains_in, R.gains), (R.skip_in, R.skip), (R.glu_b_in, R.glu_b),
    ]
    cp_small = [load(k0 + k, src, dst) for k, (src, dst) in enumerate(pairs)]
    k0 = rows_dev
    cp_b = [load(k0, R.b_re.at[0], R.wb_re.at[0]), load(k0 + 1, R.b_im.at[0], R.wb_im.at[0])]
    cp_c = [
        load(k0 + 2, R.c_re, R.wc.at[:, pl.ds(0, states)]),
        load(k0 + 3, R.c_im, R.wc.at[:, pl.ds(states, states)]),
    ]
    k1 = 2 * rows_dev + 12
    cp_w = [
        load(k0 + 4, R.glu_w, R.wg),
        load(k1, R.b_re.at[1], R.wb_re.at[1]),
        load(k1 + 1, R.b_im.at[1], R.wb_im.at[1]),
    ]
    cp_t = [
        load(k0 + 5 + r, R.cot.at[r], R.cin.at[pl.ds(r * group, group)])
        for r in range(rows_dev)
    ]

    for cp in cp_small:
        cp.wait()

    place_bits = int(math.log2(per_seg))
    i0 = lax.broadcasted_iota(jnp.int32, (group, group), 0)
    i1 = lax.broadcasted_iota(jnp.int32, (group, group), 1)
    hit = i1 == (i0 & (SUB - 1)) * per_seg + (i0 >> 3)
    gather = jnp.where(hit, 1.0, 0.0).astype(BF16)
    kept = 1.0 - R.resets[...].astype(F32)
    for r in range(rows_dev):
        spread = jnp.where(hit, jnp.broadcast_to(kept[r : r + 1], (group, group)), 0.0)
        R.keep[r * group : (r + 1) * group, :] = dot(
            spread.astype(BF16), jnp.ones((group, 128), BF16)
        )

    seg_id = lax.broadcasted_iota(jnp.int32, (SUB, 128), 0)

    def shift(value, forward, by=1):
        return pltpu.roll(value, by if forward else SUB - by, 0)

    def wide(mask, cols):
        return jnp.concatenate([mask] * (cols // 128), axis=1)

    def inside(forward, by):
        return seg_id >= by if forward else seg_id < SUB - by

    window, excl, total_mask = {}, {}, {}
    for r in range(rows_dev):
        places = [R.keep[r * group + j * SUB : r * group + (j + 1) * SUB] for j in range(per_seg)]
        while len(places) > 1:
            places = [a * b for a, b in zip(places[::2], places[1::2])]
        for forward in (True, False):
            run, seen = places[0], places[0]
            for by in (1, 2, 4):
                ok = inside(forward, by)
                window[r, forward, by] = jnp.where(ok, run, 0.0)
                seen = jnp.where(ok, seen * shift(seen, forward, by), seen)
                run = run * shift(run, forward, by)
            excl[r, forward] = jnp.where(inside(forward, 1), shift(seen, forward), 1.0)
            if forward:
                total_mask[r] = seen[SUB - 1 : SUB]

    L = []
    for l in range(2):
        lam = [n[l : l + 1, :] for n in (R.lam_re, R.lam_im, R.steps)]
        a_re, a_im, q_re, q_im = discretize(*lam)
        power = (a_re, a_im)
        for _ in range(place_bits):
            power = cmul(power, power)
        powers = {1: power}
        for by in (1, 2, 4):
            powers[2 * by] = cmul(powers[by], powers[by])
        for forward in (True, False):
            index = wide(seg_id if forward else SUB - 1 - seg_id, states)
            at_seg = (jnp.ones((SUB, states), F32), jnp.zeros((SUB, states), F32))
            for by in (1, 2, 4):
                more = cmul(at_seg, powers[by])
                at_seg = tuple(
                    jnp.where((index & by) != 0, m, o) for m, o in zip(more, at_seg)
                )
            powers[forward, 0] = at_seg
        L.append(dict(lam=lam, a=(a_re, a_im), q=(q_re, q_im), powers=powers, l=l))

    def input_matrix(layer, m_ref):
        q_re, q_im = layer["q"]
        l = layer["l"]
        step = 128
        for i in range(width // step):
            sl = slice(i * step, (i + 1) * step)
            br = R.wb_re[l, sl, :].astype(F32)
            bi = R.wb_im[l, sl, :].astype(F32)
            m_ref[sl, 0:states] = (q_re * br - q_im * bi).astype(BF16)
            m_ref[sl, states:P2] = (q_re * bi + q_im * br).astype(BF16)

    def scan_pass(r, layer, forward, start, sink):
        a = [jnp.broadcast_to(p, (SUB, states)) for p in layer["a"]]
        v_ref, keep_ref = R.v, R.keep

        def one(j, carry):
            base = pl.multiple_of(r * group + j * SUB, SUB)
            keep = wide(keep_ref[pl.ds(base, SUB), :], states)
            v = (v_ref[pl.ds(base, SUB), 0:states], v_ref[pl.ds(base, SUB), states:P2])
            if forward:
                held = (keep * carry[0], keep * carry[1])
                prod = cmul(a, held)
                x = (prod[0] + v[0], prod[1] + v[1])
                return x, held, x
            prod = cmul(a, carry)
            x = (prod[0] + v[0], prod[1] + v[1])
            held = (keep * x[0], keep * x[1])
            return x, carry, held

        pair = 2

        def body(i, carry):
            state, extra = carry
            if forward:
                js = [i * pair + k for k in range(pair)]
            else:
                js = [per_seg - 1 - (i * pair + k) for k in range(pair)]
            xs = []
            for j in js:
                x, held, state = one(j, state)
                xs.append(x)
                if sink is not None:
                    extra = sink.each(r * group + j * SUB, x, held, extra)
            if sink is not None:
                low = js[0] if forward else js[-1]
                ordered = xs if forward else xs[::-1]
                sink.pair(r * group + low * SUB, ordered)
            return state, extra

        extra0 = sink.zero() if sink is not None else ()
        return lax.fori_loop(0, per_seg // pair, body, (start, extra0), unroll=UNROLL)

    class Forward:
        def __init__(self, x_ref, s_ref):
            self.x_ref, self.s_ref = x_ref, s_ref

        def zero(self):
            return ()

        def each(self, base, x, held, extra):
            base = pl.multiple_of(base, SUB)
            self.x_ref[pl.ds(base, SUB), 0:states] = x[0]
            self.x_ref[pl.ds(base, SUB), states:P2] = x[1]
            return extra

        def pair(self, base, xs):
            base = pl.multiple_of(base, 2 * SUB)
            re = jnp.concatenate([x[0] for x in xs], axis=0)
            im = jnp.concatenate([x[1] for x in xs], axis=0)
            self.s_ref[pl.ds(base, 2 * SUB), 0:states] = re.astype(BF16)
            self.s_ref[pl.ds(base, 2 * SUB), states:P2] = (-im).astype(BF16)

    class Adjoint:
        def __init__(self, x_ref, d_ref):
            self.x_ref, self.d_ref = x_ref, d_ref

        def zero(self):
            return (jnp.zeros((SUB, states), F32), jnp.zeros((SUB, states), F32))

        def each(self, base, x, held, extra):
            base = pl.multiple_of(base, SUB)
            xv = (self.x_ref[pl.ds(base, SUB), 0:states], self.x_ref[pl.ds(base, SUB), states:P2])
            prod = cmul(xv, held)
            return (extra[0] + prod[0], extra[1] + prod[1])

        def pair(self, base, xs):
            base = pl.multiple_of(base, 2 * SUB)
            re = jnp.concatenate([x[0] for x in xs], axis=0)
            im = jnp.concatenate([x[1] for x in xs], axis=0)
            self.d_ref[pl.ds(base, 2 * SUB), 0:states] = re.astype(BF16)
            self.d_ref[pl.ds(base, 2 * SUB), states:P2] = (-im).astype(BF16)

    first_wait = [True]

    def send_carry(e, r, layer, forward, ends):
        seen = ends
        for by in (1, 2, 4):
            mask = wide(window[r, forward, by], states)
            prod = cmul(layer["powers"][by], tuple(shift(p, forward, by) for p in seen))
            seen = (seen[0] + mask * prod[0], seen[1] + mask * prod[1])
        ok = wide(inside(forward, 1), states)
        run = tuple(jnp.where(ok, shift(p, forward), 0.0) for p in seen)
        last = slice(SUB - 1, SUB) if forward else slice(0, 1)
        R.msg[e, r, :, 0:states] = seen[0][last]
        R.msg[e, r, :, states:P2] = seen[1][last]
        R.msg[e, r, :, P2 : P2 + 128] = total_mask[r]
        if first_wait[0]:
            pl.semaphore_wait(barrier, n_tm - 1 + row_bits)
            first_wait[0] = False
        for other in others:
            copy = pltpu.make_async_remote_copy(
                R.msg.at[e, r],
                R.got.at[e, r, at],
                R.send_sem.at[e, r],
                R.recv_sem.at[e, r],
                device_id={"tm": other},
                device_id_type=MESH,
            )
            copy.start()
        return run, mover.message()

    def take_carry(e, r, layer, forward, sent):
        run, arrival = sent
        mover.until(arrival)
        slots = R.got.at[e, r, pl.ds(0, n_tm - 1)]
        pltpu.make_async_copy(slots, slots, R.recv_sem.at[e, r]).wait()
        pltpu.make_async_copy(slots, slots, R.send_sem.at[e, r]).wait()
        span = layer["powers"][SUB]
        carry = (jnp.zeros((1, states), F32), jnp.zeros((1, states), F32))
        order = range(n_tm) if forward else range(n_tm - 1, -1, -1)
        for k in list(order)[:-1]:
            before = (at > k) if forward else (at < k)
            mask = wide(R.got[e, r, k, :, P2 : P2 + 128], states)
            prod = cmul(span, carry)
            new = (
                R.got[e, r, k, :, 0:states] + mask * prod[0],
                R.got[e, r, k, :, states:P2] + mask * prod[1],
            )
            carry = tuple(jnp.where(before, n, c) for n, c in zip(new, carry))
        prod = cmul(layer["powers"][forward, 0], carry)
        mask = wide(excl[r, forward], states)
        return (run[0] + mask * prod[0], run[1] + mask * prod[1])

    zero_state = (jnp.zeros((SUB, states), F32), jnp.zeros((SUB, states), F32))

    tiles = {
        r: [(slice(r * group + i, r * group + i + TILE), slice(i, i + TILE)) for i in range(0, group, TILE)]
        for r in range(rows_dev)
    }
    line = [slice(r * group, (r + 1) * group) for r in range(rows_dev)]
    rows = range(rows_dev)

    def norm_front(h, layer, z_ref, r_ref, u_ref, m_ref, sl):
        mean = jnp.mean(h, axis=1, keepdims=True)
        centred = h - mean
        var = jnp.mean(centred * centred, axis=1, keepdims=True)
        r = lax.rsqrt(var + NORM_EPS)
        z = centred * r
        u = (z * R.gains[layer["l"] : layer["l"] + 1, :]).astype(BF16)
        z_ref[sl, :] = z
        r_ref[sl, :] = jnp.broadcast_to(r, (r.shape[0], 128))
        u_ref[sl, :] = u
        R.v[sl, :] = dot(u, m_ref[...])

    def mixer(layer, s_ref, u_ref, gl_ref, sl):
        l = layer["l"]
        s = s_ref[sl, :]
        y = dot(s, R.wc[l]) + R.skip[l : l + 1, :] * u_ref[sl, :].astype(F32)
        cdf, dens = gauss(y)
        gelu = y * cdf
        low = gelu.astype(BF16)
        gl_ref[sl, :] = low
        pre = dot(low, R.wg[l]) + R.glu_b[l : l + 1, :]
        gate = 0.5 * jnp.tanh(0.5 * pre) + 0.5
        gated = gelu * gate
        return gated, cdf + dens, gate, gated * (1.0 - gate)

    def back_front(layer, d_out, slope, gate, prod, u_ref, ds_ref, dy_ref, sums, sl):
        l = layer["l"]
        ds = (d_out * prod).astype(BF16)
        ds_ref[sl, :] = ds
        d_gelu = d_out * gate + dot_nt(ds, R.wg[l])
        dy = (d_gelu * slope).astype(BF16)
        dy_ref[sl, :] = dy
        R.v[sl, :] = dot_nt(dy, R.wc[l])
        sums["bias"] = sums["bias"] + fold(ds.astype(F32))
        sums["skip"] = sums["skip"] + fold(dy.astype(F32) * u_ref[sl, :].astype(F32))

    def back_norm(layer, d_out, dv_ref, m_ref, dy_ref, z_ref, r_ref, sums, sl):
        l = layer["l"]
        dn = dy_ref[sl, :].astype(F32) * R.skip[l : l + 1, :] + dot_nt(dv_ref[sl, :], m_ref[...])
        z = z_ref[sl, :]
        sums["gain"] = sums["gain"] + fold(dn * z)
        w = dn * R.gains[l : l + 1, :]
        mean_w = jnp.mean(w, axis=1, keepdims=True)
        mean_wz = jnp.mean(w * z, axis=1, keepdims=True)
        r = wide(r_ref[sl, :], width)
        return d_out + r * (w - mean_w - z * mean_wz)

    def fresh():
        return {k: jnp.zeros((SUB, width), F32) for k in ("gain", "skip", "bias")}

    def start(name, l, first, count):
        for k in range(first, first + count, SUB):
            if (name, l, k) in chunks:
                mover.start(chunks[name, l, k])

    def product_grads(layer, gl_ref, ds_ref, s_ref, dy_ref):
        l = layer["l"]
        for name, left, right in (("w", gl_ref, ds_ref), ("c", s_ref, dy_ref)):
            for k in range(0, width, 256):
                grads[name][l, :, k : k + 256] = dot_tn(left[...], right[:, k : k + 256])
                start(name, l, k, 256)
                mover.run(0.15)

    def matrix_grads(layer, u_ref, dv_ref, da):
        l = layer["l"]
        q_re, q_im = layer["q"]
        full = dot_tn(u_ref[...], dv_ref[...])
        g_re, g_im = full[:, 0:states], full[:, states:P2]
        R.b_g[l, :, 0:states] = q_re * g_re + q_im * g_im
        R.b_g[l, :, states:P2] = q_re * g_im - q_im * g_re
        start("b", l, 0, P2)
        br, bi = R.wb_re[l].astype(F32), R.wb_im[l].astype(F32)
        dq_re = jnp.sum(fold(br * g_re + bi * g_im), axis=0, keepdims=True)
        dq_im = jnp.sum(fold(br * g_im - bi * g_re), axis=0, keepdims=True)
        da_re = jnp.sum(da[0], axis=0, keepdims=True)
        da_im = -jnp.sum(da[1], axis=0, keepdims=True)
        _, pull = jax.vjp(discretize, *layer["lam"])
        lam_grads = pull((da_re, da_im, dq_re, dq_im))
        for k, grad in enumerate(lam_grads):
            row = 6 + 2 * k + l
            R.small_g[row : row + 1, 0:states] = grad

    one, two = L
    for cp in cp_b:
        cp.wait()
    input_matrix(one, R.m1)
    for cp in cp_x:
        cp.wait()
    sent = {}
    for r in rows:
        for sl, part in tiles[r]:
            h = dot(gather[part, :], R.xin[line[r], :])
            R.h1[sl, :] = h
            norm_front(h, one, R.z1, R.r1, R.u1, R.m1, sl)
        ends, _ = scan_pass(r, one, True, zero_state, None)
        sent[0, r] = send_carry(0, r, one, True, ends)
    for cp in cp_c + cp_w + cp_t:
        cp.wait()
    input_matrix(two, R.m2)

    for r in rows:
        carry = take_carry(0, r, one, True, sent[0, r])
        scan_pass(r, one, True, carry, Forward(R.x1, R.s1))
        for sl, _ in tiles[r]:
            gated, slope, gate, prod = mixer(one, R.s1, R.u1, R.gl1, sl)
            R.gd1[sl, :] = slope
            R.gate1[sl, :] = gate
            R.prod1[sl, :] = prod
            h = R.h1[sl, :] + gated
            R.h2[sl, :] = h
            norm_front(h, two, R.z2, R.r2, R.u2, R.m2, sl)
        ends, _ = scan_pass(r, two, False, zero_state, None)
        sent[1, r] = send_carry(1, r, two, False, ends)

    sums2 = fresh()
    for r in rows:
        carry = take_carry(1, r, two, False, sent[1, r])
        scan_pass(r, two, False, carry, Forward(R.x2, R.s2))
        for sl, part in tiles[r]:
            gated, slope, gate, prod = mixer(two, R.s2, R.u2, R.gl2, sl)
            R.result[sl, :] = (R.h2[sl, :] + gated).astype(BF16)
            d_out = dot(gather[part, :], R.cin[line[r], :])
            R.d_mid[sl, :] = d_out
            back_front(two, d_out, slope, gate, prod, R.u2, R.ds2, R.dy2, sums2, sl)
        mover.run(2.0)
        ends, _ = scan_pass(r, two, True, zero_state, None)
        sent[2, r] = send_carry(2, r, two, True, ends)
    product_grads(two, R.gl2, R.ds2, R.s2, R.dy2)

    sums1 = fresh()
    da2, da1 = Adjoint(R.x2, R.dv2).zero(), Adjoint(R.x1, R.dv1).zero()
    for r in rows:
        carry = take_carry(2, r, two, True, sent[2, r])
        mover.run(0.3)
        _, da = scan_pass(r, two, True, carry, Adjoint(R.x2, R.dv2))
        da2 = (da2[0] + da[0], da2[1] + da[1])
        mover.run(0.3)
        for sl, _ in tiles[r]:
            d_mid = back_norm(two, R.d_mid[sl, :], R.dv2, R.m2, R.dy2, R.z2, R.r2, sums2, sl)
            R.d_mid[sl, :] = d_mid
            back_front(
                one, d_mid, R.gd1[sl, :], R.gate1[sl, :], R.prod1[sl, :],
                R.u1, R.ds1, R.dy1, sums1, sl,
            )
            mover.run(1.3)
        ends, _ = scan_pass(r, one, False, zero_state, None)
        mover.run(0.3)
        sent[3, r] = send_carry(3, r, one, False, ends)
    R.small_g[...] = jnp.zeros((2 * SUB, width), F32)
    matrix_grads(two, R.u2, R.dv2, da2)
    mover.run(0.8)
    product_grads(one, R.gl1, R.ds1, R.s1, R.dy1)

    for r in rows:
        carry = take_carry(3, r, one, False, sent[3, r])
        mover.run(0.3)
        _, da = scan_pass(r, one, False, carry, Adjoint(R.x1, R.dv1))
        da1 = (da1[0] + da[0], da1[1] + da[1])
        mover.run(0.3)
        for sl, _ in tiles[r]:
            d_in = back_norm(one, R.d_mid[sl, :], R.dv1, R.m1, R.dy1, R.z1, R.r1, sums1, sl)
            R.stage[sl, :] = d_in.astype(BF16)
        mover.run(0.5)
    matrix_grads(one, R.u1, R.dv1, da1)
    for k, name in enumerate(("gain", "skip", "bias")):
        for l, sums in enumerate((sums1, sums2)):
            row = 2 * k + l
            R.small_g[row : row + 1, :] = jnp.sum(sums[name], axis=0, keepdims=True)
    mover.start(chunks["s"])
    mover.run(0.8)
    ungather = jnp.where(i1 == (i0 & (per_seg - 1)) * SUB + (i0 >> place_bits), 1.0, 0.0).astype(BF16)
    for r in rows:
        R.in_grad[r] = dot(ungather, R.stage[line[r], :]).astype(BF16)
    mover.run(0.3)
    for r in rows:
        R.out[r] = dot(ungather, R.result[line[r], :]).astype(BF16)
    mover.run(0.3)
    mover.drain()


def finish_kernel(states, out_v, in_grad_v, small_v, b_v, c_v, w_v, *refs):
    out, in_grad, gain, lam_re, lam_im, steps, b_re, b_im, c_re, c_im, skip, w, bias = refs[:13]
    sem, *held = refs[13:]
    pairs = [
        (b_v.at[:, :, pl.ds(0, states)], b_re),
        (b_v.at[:, :, pl.ds(states, states)], b_im),
        (c_v.at[:, pl.ds(0, states)], c_re),
        (c_v.at[:, pl.ds(states, states)], c_im),
        (w_v, w),
        (out_v, out),
        (in_grad_v, in_grad),
    ]
    copies = [pltpu.make_async_copy(a, b, sem.at[k]) for k, (a, b) in enumerate(pairs)]
    for copy in copies:
        copy.start()
    for k, (ref, target) in enumerate(zip(held, (gain, skip, bias, lam_re, lam_im, steps))):
        ref[...] = small_v[2 * k : 2 * k + 2, 0 : ref.shape[1]]
        copy = pltpu.make_async_copy(ref, target, sem.at[len(pairs) + k])
        copy.start()
        copies.append(copy)
    for copy in copies:
        copy.wait()


def on_device(n_tm, n_rows, *args):
    inputs, lam_re = args[0], args[3]
    rows_dev, group, width = inputs.shape
    states = lam_re.shape[1]
    tokens = rows_dev * group
    P2 = 2 * states
    chunks = plan_chunks(n_tm, n_rows, width, P2)
    cfg = (tokens, width, states, rows_dev, group, n_tm, n_rows, chunks)
    vm = pl.BlockSpec(memory_space=pltpu.VMEM)
    hbm = pl.BlockSpec(memory_space=pl.ANY)
    far = pl.BlockSpec(memory_space=pltpu.HBM)
    in_specs = [far] * 14
    out_specs = [vm] * 6
    out_shape = [
        jax.ShapeDtypeStruct(inputs.shape, BF16),
        jax.ShapeDtypeStruct(inputs.shape, BF16),
        jax.ShapeDtypeStruct((2 * SUB, width), F32),
        jax.ShapeDtypeStruct((2, width, P2), F32),
        jax.ShapeDtypeStruct((2, P2, width), F32),
        jax.ShapeDtypeStruct((2, width, width), F32),
    ]

    def big(cols, dtype=F32):
        return pltpu.VMEM((tokens, cols), dtype)

    bits = int(math.log2(n_tm * n_rows))
    scratch = [
        big(width, BF16), big(width, BF16),
        pltpu.VMEM((2, width, states), BF16), pltpu.VMEM((2, width, states), BF16),
        pltpu.VMEM((2, P2, width), BF16), pltpu.VMEM((2, width, width), BF16),
        big(width), big(width), big(width), big(width), big(128), big(128),
        big(width, BF16), big(width, BF16), big(P2), big(P2), big(P2),
        big(P2, BF16), big(P2, BF16), big(width, BF16), big(width, BF16),
        big(width), big(width), big(width), big(width),
        big(width, BF16), big(width, BF16), big(width, BF16), big(width, BF16),
        big(P2, BF16), big(P2, BF16),
        pltpu.VMEM((width, P2), BF16), pltpu.VMEM((width, P2), BF16),
        big(128), big(width, BF16), big(width, BF16),
        pltpu.VMEM((2 * SUB, width), F32), pltpu.VMEM((2, width, P2), F32),
        pltpu.VMEM((2, P2, width), F32), pltpu.VMEM((2, width, width), F32),
        pltpu.VMEM((4, rows_dev, 1, P2 + 128), F32),
        pltpu.VMEM((4, rows_dev, n_tm, 1, P2 + 128), F32),
        pltpu.SemaphoreType.DMA((2 * rows_dev + 14,)),
        pltpu.SemaphoreType.DMA((4, rows_dev)), pltpu.SemaphoreType.DMA((4, rows_dev)),
        pltpu.SemaphoreType.DMA((PUTS,)), pltpu.SemaphoreType.DMA((bits * GETS,)),
    ]
    for k in (1, 2, 3, 4, 5, 10, 12):
        scratch.append(pltpu.VMEM(args[k].shape, args[k].dtype))
    for chunk in chunks.values():
        scratch.append(pltpu.VMEM((chunk.land_rows, chunk.width), F32))
    held = pl.pallas_call(
        functools.partial(kernel, cfg),
        out_shape=[pltpu.VMEM(o.shape, o.dtype) for o in out_shape],
        in_specs=in_specs,
        out_specs=out_specs,
        scratch_shapes=scratch,
        compiler_params=pltpu.CompilerParams(
            collective_id=0, has_side_effects=True, vmem_limit_bytes=53 * 2**20
        ),
    )(*args)
    grads = [args[k] for k in range(2, 13)]
    final_shape = [out_shape[0]] * 2 + [jax.ShapeDtypeStruct(g.shape, F32) for g in grads]
    final_specs = [hbm] * 13
    return tuple(
        pl.pallas_call(
            functools.partial(finish_kernel, states),
            out_shape=final_shape,
            in_specs=[hbm, hbm, vm, hbm, hbm, hbm],
            out_specs=final_specs,
            scratch_shapes=[pltpu.SemaphoreType.DMA((13,))]
            + [pltpu.VMEM((2, width), F32)] * 3
            + [pltpu.VMEM((2, states), F32)] * 3,
            compiler_params=pltpu.CompilerParams(vmem_limit_bytes=2**20),
        )(*held)
    )


def solution(mesh):
    rows = P("rows", "tm", None)
    in_specs = (rows, P("rows", "tm")) + (P(),) * 11 + (rows,)
    out_specs = (rows, rows) + (P(),) * 11
    return jax.shard_map(
        functools.partial(on_device, mesh.shape["tm"], mesh.shape["rows"]),
        mesh=mesh,
        in_specs=in_specs,
        out_specs=out_specs,
        check_vma=False,
    )
```

```python
import functools
import math

import jax
import jax.numpy as jnp
from jax import lax
from jax.experimental import pallas as pl
from jax.experimental.pallas import tpu as pltpu
from jax.sharding import PartitionSpec as P

NORM_EPS = 1e-05
MESH = pl.DeviceIdType.MESH
F32 = jnp.float32
BF16 = jnp.bfloat16
SUB = 8
UNROLL = 16
PUTS, GETS = 24, 15
TILE = 256
STEPS = [256, 128, 128, 256, 128, 128]
ORDERS = [
    "zy", "XY", "yx", "xy", "YX", "ZX", "ZY", "yx", "yx", "yx", "YX", "XY", "XY", "yx", "xz",
    "xy", "YX", "zx", "YX", "YX", "yx", "xy", "xy", "xz",
]


class Refs:
    pass


def horner(value, coeffs):
    total = coeffs[-1]
    for coeff in coeffs[-2::-1]:
        total = total * value + coeff
    return total


def discretize(lam_re, lam_im, time_steps):
    growth = lam_re * time_steps
    angles = lam_im * time_steps
    square = angles * angles
    fact = math.factorial
    grow = growth * horner(growth, [1.0 / fact(k + 1) for k in range(8)])
    sine = angles * horner(square, [(-1.0) ** k / fact(2 * k + 1) for k in range(7)])
    dip = square * horner(square, [(-1.0) ** k / fact(2 * k + 2) for k in range(7)])
    cosine = 1.0 - dip
    magnitude = 1.0 + grow
    a_re = magnitude * cosine
    a_im = magnitude * sine
    e_re = grow * cosine - dip
    modulus = lam_re * lam_re + lam_im * lam_im
    q_re = (e_re * lam_re + a_im * lam_im) / modulus
    q_im = (a_im * lam_re - e_re * lam_im) / modulus
    return (a_re, a_im, q_re, q_im)


def cmul(a, b):
    return (a[0] * b[0] - a[1] * b[1], a[0] * b[1] + a[1] * b[0])


def dot(a, b):
    return jnp.dot(a, b, preferred_element_type=F32)


def dot_nt(a, b):
    return lax.dot_general(a, b, (((1,), (1,)), ((), ())), preferred_element_type=F32)


def dot_tn(a, b):
    return lax.dot_general(a, b, (((0,), (0,)), ((), ())), preferred_element_type=F32)


def fold(value):
    rows, cols = value.shape
    return jnp.sum(value.reshape(rows // SUB, SUB, cols), axis=0)


def gauss(y):
    size = jnp.abs(y) * (0.5**0.5)
    bell = jnp.exp(-0.5 * (y * y))
    t = pltpu.reciprocal(1.0 + 0.3275911 * size, approx=True)
    tail = (0.5 * t * bell) * horner(
        t, [0.254829592, -0.284496736, 1.421413741, -1.453152027, 1.061405429]
    )
    cdf = jnp.where(y >= 0.0, 1.0 - tail, tail)
    return cdf, y * bell * ((2.0 * math.pi) ** -0.5)


class Chunk:
    def __init__(self, index, grad, rows, cols, groups):
        self.index, self.grad, self.rows, self.cols = index, grad, rows, cols
        self.width = cols[1] - cols[0]
        self.stages = []
        size, land, bits = rows, 0, []
        for group in groups:
            fits = size % (SUB << len(group)) == 0
            for part in [group] if fits else [(bit,) for bit in group]:
                halved = size % (SUB << len(part)) == 0
                size = size >> len(part) if halved else size
                self.stages.append((part, size, halved, land))
                land += size * ((1 << len(part)) - 1)
                bits.append(part)
        self.bits, self.land_rows = bits, land
        self.steps = [("sum", i) for i in range(len(bits))]
        self.steps += [("get", i) for i in reversed(range(len(bits))) if self.stages[i][2]]


def plan_chunks(n_tm, n_rows, width, P2):
    tm_bits, row_bits = int(math.log2(n_tm)), int(math.log2(n_rows))
    core = [("tm", 0)]
    half = (tm_bits - 1) // 2
    xs = [("tm", 1 + k) for k in range(half)]
    ys = [("tm", 1 + half + k) for k in range(tm_bits - 1 - half)]
    zs = [("rows", k) for k in range(row_bits)]

    def order(name):
        pair = name.isupper()
        axes = {"x": [(b,) for b in xs], "y": [(b,) for b in ys]}
        axes["z"] = [tuple(zs[:2])] if pair else [(b,) for b in zs[:1]]
        first, second = name.lower()
        third = ({"x", "y", "z"} - {first, second}).pop()
        rest = [(b,) for b in zs[2 if pair else 1 :]]
        return [(core[0],)] + axes[first] + axes[second] + axes[third] + rest

    chunks = {}
    count = 0
    plan, steps = iter(ORDERS), iter(STEPS)
    for l in (1, 0):
        for name, rows, cols in (("w", width, width), ("c", P2, width), ("b", width, P2)):
            step = next(steps)
            for k in range(0, cols, step):
                chunks[name, l, k] = Chunk(
                    count, (name, l), rows, (k, k + step), order(next(plan))
                )
                count += 1
    chunks["s"] = Chunk(count, ("s", None), 2 * SUB, (0, width), order("yx"))
    return chunks


class Mover:
    RATE = {"c": 650e3, "x": 46e3, "y": 46e3, "z": 46e3, "mid": 46e3}
    DELAY = {"c": 0.8, "x": 1.7, "y": 1.7, "z": 1.7}
    EXCHANGE = 3.2
    AHEAD = 2.5

    def __init__(self, chunks, refs, lands, at, half_bits):
        self.chunks, self.refs, self.at, self.half_bits = chunks, refs, at, half_bits
        self.lands = lands
        self.now = 0.0
        self.free = {k: 0.0 for k in self.RATE}
        self.queue = {k: [] for k in self.DELAY}
        self.pending = []
        self.copies = {}
        self.starts = {}
        self.clock = 0
        self.gets, self.acked, self.puts, self.used = {}, {}, [], {}

    def coord(self, bit):
        return lax.rem(self.at[bit[0]] // (1 << bit[1]), 2)

    def peer(self, bits):
        ids = {}
        for bit in bits:
            own = ids.get(bit[0], self.at[bit[0]])
            ids[bit[0]] = own + (1 - 2 * self.coord(bit)) * (1 << bit[1])
        return ids

    def share(self, bits, other=()):
        part = 0
        for bit in bits:
            own = self.coord(bit)
            part = 2 * part + (1 - own if bit in other else own)
        return part

    def begin(self, chunk, level):
        key = (chunk.rows, tuple(chunk.bits[:level]))
        if key not in self.starts:
            if level == 0:
                self.starts[key] = 0
            else:
                bits, size, halved, _ = chunk.stages[level - 1]
                before = self.begin(chunk, level - 1)
                self.starts[key] = before + self.share(bits) * size if halved else before
        return self.starts[key]

    def view(self, chunk, start, size, done=False):
        ref = self.refs[1 if done else 0][chunk.grad[0]]
        rows = pl.ds(pl.multiple_of(start, SUB) if not isinstance(start, int) else start, size)
        cols = pl.ds(chunk.cols[0], chunk.width)
        l = chunk.grad[1]
        return ref.at[rows, cols] if l is None else ref.at[l, rows, cols]

    def link(self, bits):
        bit = bits[0]
        if bit[0] == "rows":
            return "z"
        return "c" if bit[1] == 0 else ("x" if bit[1] <= self.half_bits else "y")

    def cost(self, chunk, k):
        bit, size, _, _ = chunk.stages[chunk.steps[k][1]]
        return size * chunk.width * 4 / self.RATE[self.link(bit)] * (3 if len(bit) > 1 else 1)

    def left(self, chunk, k):
        total = 0.0
        for j in range(k, len(chunk.steps)):
            bit = chunk.stages[chunk.steps[j][1]][0]
            total += self.cost(chunk, j) + self.DELAY[self.link(bit)]
        return total

    def push(self, chunk, k):
        bit = chunk.stages[chunk.steps[k][1]][0]
        self.queue[self.link(bit)].append((-self.left(chunk, k), chunk.index, k, chunk))

    def take_get(self, bit):
        pool = self.gets.setdefault(bit, {})
        for k, released in pool.items():
            if released is not None and released < self.acked.get(bit, 0):
                pool[k] = None
                return k
        k = sum(len(other) for other in self.gets.values())
        pool[k] = None
        return k

    def take_put(self):
        if True in self.puts:
            k = self.puts.index(True)
            self.puts[k] = False
            return k
        self.puts.append(False)
        return len(self.puts) - 1

    def pump(self):
        for link, queue in self.queue.items():
            while queue and self.free[link] < self.now + self.AHEAD:
                item = min(queue, key=lambda entry: entry[:3])
                queue.remove(item)
                self.launch(item[3], item[2])

    def launch(self, chunk, k):
        kind, i = chunk.steps[k]
        bit, size, halved, land = chunk.stages[i]
        put, get = self.take_put(), self.take_get(bit)
        self.clock += 1
        self.used[chunk.index, k] = (put, get, self.clock)
        if self.refs is not None:
            self.copies[chunk.index, k] = copies = []
            for m in range(1, 1 << len(bit)):
                other = [b for n, b in enumerate(bit) if m >> n & 1]
                if kind == "sum":
                    before = self.begin(chunk, i)
                    if halved:
                        before = before + self.share(bit, other) * size
                    src = self.view(chunk, before, size)
                    dst = self.lands[chunk.index].at[pl.ds(land + (m - 1) * size, size)]
                else:
                    src = dst = self.view(chunk, self.begin(chunk, i + 1), size, True)
                copy = pltpu.make_async_remote_copy(
                    src,
                    dst,
                    self.refs[2].at[put],
                    self.refs[3].at[get],
                    device_id=self.peer(other),
                    device_id_type=MESH,
                )
                copy.start()
                copies.append(copy)
        link = self.link(bit)
        cost = self.cost(chunk, k)
        far = link == "z" and bit[-1][1] > 0
        began = max(self.now, self.free[link], self.free["mid"] if far else 0.0)
        self.free[link] = done = began + cost
        if far:
            self.free["mid"] = done = began + cost * (2 if len(bit) == 1 else 4 / 3)
        self.pending.append((done + self.DELAY[link], chunk.index, k, chunk))
        self.now += 0.04 * ((1 << len(bit)) - 1)

    def finish(self, item):
        _, _, k, chunk = item
        kind, i = chunk.steps[k]
        bit, size, _, land = chunk.stages[i]
        real = self.refs is not None
        copies = self.copies.get((chunk.index, k))
        many = (1 << len(bit)) - 1
        if real and many == 1:
            copies[0].wait()
        elif real:
            whole = self.lands[chunk.index].at[pl.ds(land, many * size)]
            put, get, _ = self.used[chunk.index, k]
            pltpu.make_async_copy(whole, whole, self.refs[3].at[get]).wait()
            pltpu.make_async_copy(whole, whole, self.refs[2].at[put]).wait()
        put, get, launched = self.used[chunk.index, k]
        self.clock += 1
        self.puts[put] = True
        self.gets[bit][get] = self.clock
        self.acked[bit] = max(self.acked.get(bit, 0), launched)
        self.now += 0.08
        more = k + 1 < len(chunk.steps)
        if kind == "get":
            if more:
                self.push(chunk, k + 1)
            self.pump()
            return
        start = self.begin(chunk, i + 1) if real else 0

        def add(off, rows):
            self.now += rows * chunk.width * 4 / 3e6 * (many + 1) / 2
            if not real:
                return
            ref = self.view(chunk, start + off, rows)
            total = ref[...]
            for m in range(many):
                at = land + m * size + off
                at = pl.multiple_of(at, SUB) if not isinstance(at, int) else at
                total = total + self.lands[chunk.index][pl.ds(at, rows), :]
            last = i + 1 == len(chunk.bits)
            into = self.view(chunk, start + off, rows, True) if last else ref
            into[...] = total

        follows = chunk.stages[i + 1] if i + 1 < len(chunk.bits) else None
        if follows is not None and follows[2] and len(follows[0]) == 1:
            half = size // 2
            mine = self.share(follows[0]) if real else 0
            add((1 - mine) * half, half)
            self.push(chunk, k + 1)
            self.pump()
            add(mine * half, half)
        else:
            add(0, size)
            if more:
                self.push(chunk, k + 1)
            self.pump()

    def first(self):
        return min(self.pending, key=lambda item: item[:3])

    def start(self, chunk):
        self.push(chunk, 0)
        self.pump()

    def run(self, spent):
        self.now += spent
        while self.pending and self.first()[0] <= self.now:
            item = self.first()
            self.pending.remove(item)
            self.finish(item)

    def message(self):
        return max(self.now, self.free["x"], self.free["y"]) + self.EXCHANGE

    def until(self, time):
        while self.pending and self.first()[0] <= time:
            item = self.first()
            self.pending.remove(item)
            self.now = max(self.now, item[0])
            self.finish(item)
        self.now = max(self.now, time)

    def drain(self):
        while self.pending:
            item = self.first()
            self.pending.remove(item)
            self.now = max(self.now, item[0])
            self.finish(item)


def kernel(cfg, *refs):
    tokens, width, states, rows_dev, group, n_tm, n_rows, chunks = cfg
    R = Refs()
    (
        R.inputs, R.resets_in, R.gains_in, R.lam_re_in, R.lam_im_in, R.steps_in, R.b_re, R.b_im,
        R.c_re, R.c_im, R.skip_in, R.glu_w, R.glu_b_in, R.cot, R.out, R.in_grad, R.small_o, R.b_o,
        R.c_o, R.w_o, R.xin, R.cin, R.wb_re, R.wb_im, R.wc, R.wg, R.h1, R.h2, R.z1, R.z2, R.r1,
        R.r2, R.u1, R.u2, R.v, R.x1, R.x2, R.s1, R.s2, R.gl1, R.gl2, R.gd1, R.gate1, R.prod1,
        R.d_mid, R.dy1, R.dy2, R.ds1, R.ds2, R.dv1, R.dv2, R.m1, R.m2, R.keep, R.stage, R.result, R.small_g,
        R.b_g, R.c_g, R.w_g, R.msg, R.got, R.in_sem, R.send_sem,
        R.recv_sem, R.put_sem, R.get_sem, R.resets, R.gains, R.lam_re, R.lam_im, R.steps, R.skip,
        R.glu_b,
        *lands,
    ) = refs
    segs = SUB
    per_seg = group // segs
    at = lax.axis_index("tm")
    P2 = 2 * states

    barrier = pltpu.get_barrier_semaphore()
    tm_bits = int(math.log2(n_tm))
    others = []
    for m in reversed(range(1, n_tm)):
        flips = [(1 - 2 * lax.rem(at // (1 << b), 2)) * (1 << b) for b in range(tm_bits) if m >> b & 1]
        others.append(at + sum(flips))
    for other in others:
        pl.semaphore_signal(barrier, inc=1, device_id={"tm": other}, device_id_type=MESH)
    row_at = lax.axis_index("rows")
    grads = {"b": R.b_g, "c": R.c_g, "w": R.w_g, "s": R.small_g}
    sums = {"b": R.b_o, "c": R.c_o, "w": R.w_o, "s": R.small_o}
    mover_refs = (grads, sums, R.put_sem, R.get_sem)
    half_bits = (int(math.log2(n_tm)) - 1) // 2
    mover = Mover(chunks, mover_refs, lands, {"tm": at, "rows": row_at}, half_bits)
    row_bits = int(math.log2(n_rows))
    zs = [("rows", k) for k in range(row_bits)]
    greeted = [[z] for z in zs] + ([zs[:2]] if row_bits > 1 else [])
    for bits in greeted:
        pl.semaphore_signal(barrier, inc=1, device_id=mover.peer(bits), device_id_type=MESH)

    def load(k, src, dst):
        copy = pltpu.make_async_copy(src, dst, R.in_sem.at[k])
        copy.start()
        return copy

    cp_x = [load(r, R.inputs.at[r], R.xin.at[pl.ds(r * group, group)]) for r in range(rows_dev)]
    k0 = 2 * rows_dev + 5
    pairs = [
        (R.resets_in, R.resets), (R.lam_re_in, R.lam_re), (R.lam_im_in, R.lam_im),
        (R.steps_in, R.steps), (R.gains_in, R.gains), (R.skip_in, R.skip), (R.glu_b_in, R.glu_b),
    ]
    cp_small = [load(k0 + k, src, dst) for k, (src, dst) in enumerate(pairs)]
    k0 = rows_dev
    cp_b = [load(k0, R.b_re.at[0], R.wb_re.at[0]), load(k0 + 1, R.b_im.at[0], R.wb_im.at[0])]
    cp_c = [
        load(k0 + 2, R.c_re, R.wc.at[:, pl.ds(0, states)]),
        load(k0 + 3, R.c_im, R.wc.at[:, pl.ds(states, states)]),
    ]
    k1 = 2 * rows_dev + 12
    cp_w = [
        load(k0 + 4, R.glu_w, R.wg),
        load(k1, R.b_re.at[1], R.wb_re.at[1]),
        load(k1 + 1, R.b_im.at[1], R.wb_im.at[1]),
    ]
    cp_t = [
        load(k0 + 5 + r, R.cot.at[r], R.cin.at[pl.ds(r * group, group)])
        for r in range(rows_dev)
    ]

    for cp in cp_small:
        cp.wait()

    place_bits = int(math.log2(per_seg))
    i0 = lax.broadcasted_iota(jnp.int32, (group, group), 0)
    i1 = lax.broadcasted_iota(jnp.int32, (group, group), 1)
    hit = i1 == (i0 & (SUB - 1)) * per_seg + (i0 >> 3)
    gather = jnp.where(hit, 1.0, 0.0).astype(BF16)
    kept = 1.0 - R.resets[...].astype(F32)
    for r in range(rows_dev):
        spread = jnp.where(hit, jnp.broadcast_to(kept[r : r + 1], (group, group)), 0.0)
        R.keep[r * group : (r + 1) * group, :] = dot(
            spread.astype(BF16), jnp.ones((group, 128), BF16)
        )

    seg_id = lax.broadcasted_iota(jnp.int32, (SUB, 128), 0)

    def shift(value, forward, by=1):
        return pltpu.roll(value, by if forward else SUB - by, 0)

    def wide(mask, cols):
        return jnp.concatenate([mask] * (cols // 128), axis=1)

    def inside(forward, by):
        return seg_id >= by if forward else seg_id < SUB - by

    window, excl, total_mask = {}, {}, {}
    for r in range(rows_dev):
        places = [R.keep[r * group + j * SUB : r * group + (j + 1) * SUB] for j in range(per_seg)]
        while len(places) > 1:
            places = [a * b for a, b in zip(places[::2], places[1::2])]
        for forward in (True, False):
            run, seen = places[0], places[0]
            for by in (1, 2, 4):
                ok = inside(forward, by)
                window[r, forward, by] = jnp.where(ok, run, 0.0)
                seen = jnp.where(ok, seen * shift(seen, forward, by), seen)
                run = run * shift(run, forward, by)
            excl[r, forward] = jnp.where(inside(forward, 1), shift(seen, forward), 1.0)
            if forward:
                total_mask[r] = seen[SUB - 1 : SUB]

    L = []
    for l in range(2):
        lam = [n[l : l + 1, :] for n in (R.lam_re, R.lam_im, R.steps)]
        a_re, a_im, q_re, q_im = discretize(*lam)
        power = (a_re, a_im)
        for _ in range(place_bits):
            power = cmul(power, power)
        powers = {1: power}
        for by in (1, 2, 4):
            powers[2 * by] = cmul(powers[by], powers[by])
        for forward in (True, False):
            index = wide(seg_id if forward else SUB - 1 - seg_id, states)
            at_seg = (jnp.ones((SUB, states), F32), jnp.zeros((SUB, states), F32))
            for by in (1, 2, 4):
                more = cmul(at_seg, powers[by])
                at_seg = tuple(
                    jnp.where((index & by) != 0, m, o) for m, o in zip(more, at_seg)
                )
            powers[forward, 0] = at_seg
        L.append(dict(lam=lam, a=(a_re, a_im), q=(q_re, q_im), powers=powers, l=l))

    def input_matrix(layer, m_ref):
        q_re, q_im = layer["q"]
        l = layer["l"]
        step = 128
        for i in range(width // step):
            sl = slice(i * step, (i + 1) * step)
            br = R.wb_re[l, sl, :].astype(F32)
            bi = R.wb_im[l, sl, :].astype(F32)
            m_ref[sl, 0:states] = (q_re * br - q_im * bi).astype(BF16)
            m_ref[sl, states:P2] = (q_re * bi + q_im * br).astype(BF16)

    def scan_pass(r, layer, forward, start, sink):
        a = [jnp.broadcast_to(p, (SUB, states)) for p in layer["a"]]
        v_ref, keep_ref = R.v, R.keep

        def one(j, carry):
            base = pl.multiple_of(r * group + j * SUB, SUB)
            keep = wide(keep_ref[pl.ds(base, SUB), :], states)
            v = (v_ref[pl.ds(base, SUB), 0:states], v_ref[pl.ds(base, SUB), states:P2])
            if forward:
                held = (keep * carry[0], keep * carry[1])
                prod = cmul(a, held)
                x = (prod[0] + v[0], prod[1] + v[1])
                return x, held, x
            prod = cmul(a, carry)
            x = (prod[0] + v[0], prod[1] + v[1])
            held = (keep * x[0], keep * x[1])
            return x, carry, held

        pair = 2

        def body(i, carry):
            state, extra = carry
            if forward:
                js = [i * pair + k for k in range(pair)]
            else:
                js = [per_seg - 1 - (i * pair + k) for k in range(pair)]
            xs = []
            for j in js:
                x, held, state = one(j, state)
                xs.append(x)
                if sink is not None:
                    extra = sink.each(r * group + j * SUB, x, held, extra)
            if sink is not None:
                low = js[0] if forward else js[-1]
                ordered = xs if forward else xs[::-1]
                sink.pair(r * group + low * SUB, ordered)
            return state, extra

        extra0 = sink.zero() if sink is not None else ()
        return lax.fori_loop(0, per_seg // pair, body, (start, extra0), unroll=UNROLL)

    class Forward:
        def __init__(self, x_ref, s_ref):
            self.x_ref, self.s_ref = x_ref, s_ref

        def zero(self):
            return ()

        def each(self, base, x, held, extra):
            base = pl.multiple_of(base, SUB)
            self.x_ref[pl.ds(base, SUB), 0:states] = x[0]
            self.x_ref[pl.ds(base, SUB), states:P2] = x[1]
            return extra

        def pair(self, base, xs):
            base = pl.multiple_of(base, 2 * SUB)
            re = jnp.concatenate([x[0] for x in xs], axis=0)
            im = jnp.concatenate([x[1] for x in xs], axis=0)
            self.s_ref[pl.ds(base, 2 * SUB), 0:states] = re.astype(BF16)
            self.s_ref[pl.ds(base, 2 * SUB), states:P2] = (-im).astype(BF16)

    class Adjoint:
        def __init__(self, x_ref, d_ref):
            self.x_ref, self.d_ref = x_ref, d_ref

        def zero(self):
            return (jnp.zeros((SUB, states), F32), jnp.zeros((SUB, states), F32))

        def each(self, base, x, held, extra):
            base = pl.multiple_of(base, SUB)
            xv = (self.x_ref[pl.ds(base, SUB), 0:states], self.x_ref[pl.ds(base, SUB), states:P2])
            prod = cmul(xv, held)
            return (extra[0] + prod[0], extra[1] + prod[1])

        def pair(self, base, xs):
            base = pl.multiple_of(base, 2 * SUB)
            re = jnp.concatenate([x[0] for x in xs], axis=0)
            im = jnp.concatenate([x[1] for x in xs], axis=0)
            self.d_ref[pl.ds(base, 2 * SUB), 0:states] = re.astype(BF16)
            self.d_ref[pl.ds(base, 2 * SUB), states:P2] = (-im).astype(BF16)

    first_wait = [True]

    def send_carry(e, r, layer, forward, ends):
        seen = ends
        for by in (1, 2, 4):
            mask = wide(window[r, forward, by], states)
            prod = cmul(layer["powers"][by], tuple(shift(p, forward, by) for p in seen))
            seen = (seen[0] + mask * prod[0], seen[1] + mask * prod[1])
        ok = wide(inside(forward, 1), states)
        run = tuple(jnp.where(ok, shift(p, forward), 0.0) for p in seen)
        last = slice(SUB - 1, SUB) if forward else slice(0, 1)
        R.msg[e, r, :, 0:states] = seen[0][last]
        R.msg[e, r, :, states:P2] = seen[1][last]
        R.msg[e, r, :, P2 : P2 + 128] = total_mask[r]
        if first_wait[0]:
            pl.semaphore_wait(barrier, n_tm - 1 + len(greeted))
            first_wait[0] = False
        for other in others:
            copy = pltpu.make_async_remote_copy(
                R.msg.at[e, r],
                R.got.at[e, r, at],
                R.send_sem.at[e, r],
                R.recv_sem.at[e, r],
                device_id={"tm": other},
                device_id_type=MESH,
            )
            copy.start()
        return run, mover.message()

    def take_carry(e, r, layer, forward, sent):
        run, arrival = sent
        mover.until(arrival)
        slots = R.got.at[e, r, pl.ds(0, n_tm - 1)]
        pltpu.make_async_copy(slots, slots, R.recv_sem.at[e, r]).wait()
        pltpu.make_async_copy(slots, slots, R.send_sem.at[e, r]).wait()
        span = layer["powers"][SUB]
        carry = (jnp.zeros((1, states), F32), jnp.zeros((1, states), F32))
        order = range(n_tm) if forward else range(n_tm - 1, -1, -1)
        for k in list(order)[:-1]:
            before = (at > k) if forward else (at < k)
            mask = wide(R.got[e, r, k, :, P2 : P2 + 128], states)
            prod = cmul(span, carry)
            new = (
                R.got[e, r, k, :, 0:states] + mask * prod[0],
                R.got[e, r, k, :, states:P2] + mask * prod[1],
            )
            carry = tuple(jnp.where(before, n, c) for n, c in zip(new, carry))
        prod = cmul(layer["powers"][forward, 0], carry)
        mask = wide(excl[r, forward], states)
        return (run[0] + mask * prod[0], run[1] + mask * prod[1])

    zero_state = (jnp.zeros((SUB, states), F32), jnp.zeros((SUB, states), F32))

    tiles = {
        r: [(slice(r * group + i, r * group + i + TILE), slice(i, i + TILE)) for i in range(0, group, TILE)]
        for r in range(rows_dev)
    }
    line = [slice(r * group, (r + 1) * group) for r in range(rows_dev)]
    rows = range(rows_dev)

    def norm_front(h, layer, z_ref, r_ref, u_ref, m_ref, sl):
        mean = jnp.mean(h, axis=1, keepdims=True)
        centred = h - mean
        var = jnp.mean(centred * centred, axis=1, keepdims=True)
        r = lax.rsqrt(var + NORM_EPS)
        z = centred * r
        u = (z * R.gains[layer["l"] : layer["l"] + 1, :]).astype(BF16)
        z_ref[sl, :] = z
        r_ref[sl, :] = jnp.broadcast_to(r, (r.shape[0], 128))
        u_ref[sl, :] = u
        R.v[sl, :] = dot(u, m_ref[...])

    def mixer(layer, s_ref, u_ref, gl_ref, sl):
        l = layer["l"]
        s = s_ref[sl, :]
        y = dot(s, R.wc[l]) + R.skip[l : l + 1, :] * u_ref[sl, :].astype(F32)
        cdf, dens = gauss(y)
        gelu = y * cdf
        low = gelu.astype(BF16)
        gl_ref[sl, :] = low
        pre = dot(low, R.wg[l]) + R.glu_b[l : l + 1, :]
        gate = 0.5 * jnp.tanh(0.5 * pre) + 0.5
        gated = gelu * gate
        return gated, cdf + dens, gate, gated * (1.0 - gate)

    def back_front(layer, d_out, slope, gate, prod, u_ref, ds_ref, dy_ref, sums, sl):
        l = layer["l"]
        ds = (d_out * prod).astype(BF16)
        ds_ref[sl, :] = ds
        d_gelu = d_out * gate + dot_nt(ds, R.wg[l])
        dy = (d_gelu * slope).astype(BF16)
        dy_ref[sl, :] = dy
        R.v[sl, :] = dot_nt(dy, R.wc[l])
        sums["bias"] = sums["bias"] + fold(ds.astype(F32))
        sums["skip"] = sums["skip"] + fold(dy.astype(F32) * u_ref[sl, :].astype(F32))

    def back_norm(layer, d_out, dv_ref, m_ref, dy_ref, z_ref, r_ref, sums, sl):
        l = layer["l"]
        dn = dy_ref[sl, :].astype(F32) * R.skip[l : l + 1, :] + dot_nt(dv_ref[sl, :], m_ref[...])
        z = z_ref[sl, :]
        sums["gain"] = sums["gain"] + fold(dn * z)
        w = dn * R.gains[l : l + 1, :]
        mean_w = jnp.mean(w, axis=1, keepdims=True)
        mean_wz = jnp.mean(w * z, axis=1, keepdims=True)
        r = wide(r_ref[sl, :], width)
        return d_out + r * (w - mean_w - z * mean_wz)

    def fresh():
        return {k: jnp.zeros((SUB, width), F32) for k in ("gain", "skip", "bias")}

    def start(name, l, first, count):
        for k in range(first, first + count, SUB):
            if (name, l, k) in chunks:
                mover.start(chunks[name, l, k])

    def product_grads(layer, gl_ref, ds_ref, s_ref, dy_ref):
        l = layer["l"]
        for name, left, right in (("w", gl_ref, ds_ref), ("c", s_ref, dy_ref)):
            for k in range(0, width, 256):
                grads[name][l, :, k : k + 256] = dot_tn(left[...], right[:, k : k + 256])
                start(name, l, k, 256)
                mover.run(0.15)

    def matrix_grads(layer, u_ref, dv_ref, da):
        l = layer["l"]
        q_re, q_im = layer["q"]
        full = dot_tn(u_ref[...], dv_ref[...])
        g_re, g_im = full[:, 0:states], full[:, states:P2]
        R.b_g[l, :, 0:states] = q_re * g_re + q_im * g_im
        R.b_g[l, :, states:P2] = q_re * g_im - q_im * g_re
        start("b", l, 0, P2)
        br, bi = R.wb_re[l].astype(F32), R.wb_im[l].astype(F32)
        dq_re = jnp.sum(fold(br * g_re + bi * g_im), axis=0, keepdims=True)
        dq_im = jnp.sum(fold(br * g_im - bi * g_re), axis=0, keepdims=True)
        da_re = jnp.sum(da[0], axis=0, keepdims=True)
        da_im = -jnp.sum(da[1], axis=0, keepdims=True)
        _, pull = jax.vjp(discretize, *layer["lam"])
        lam_grads = pull((da_re, da_im, dq_re, dq_im))
        for k, grad in enumerate(lam_grads):
            row = 6 + 2 * k + l
            R.small_g[row : row + 1, 0:states] = grad

    one, two = L
    for cp in cp_b:
        cp.wait()
    input_matrix(one, R.m1)
    for cp in cp_x:
        cp.wait()
    sent = {}
    for r in rows:
        for sl, part in tiles[r]:
            h = dot(gather[part, :], R.xin[line[r], :])
            R.h1[sl, :] = h
            norm_front(h, one, R.z1, R.r1, R.u1, R.m1, sl)
        ends, _ = scan_pass(r, one, True, zero_state, None)
        sent[0, r] = send_carry(0, r, one, True, ends)
    for cp in cp_c + cp_w + cp_t:
        cp.wait()
    input_matrix(two, R.m2)

    for r in rows:
        carry = take_carry(0, r, one, True, sent[0, r])
        scan_pass(r, one, True, carry, Forward(R.x1, R.s1))
        for sl, _ in tiles[r]:
            gated, slope, gate, prod = mixer(one, R.s1, R.u1, R.gl1, sl)
            R.gd1[sl, :] = slope
            R.gate1[sl, :] = gate
            R.prod1[sl, :] = prod
            h = R.h1[sl, :] + gated
            R.h2[sl, :] = h
            norm_front(h, two, R.z2, R.r2, R.u2, R.m2, sl)
        ends, _ = scan_pass(r, two, False, zero_state, None)
        sent[1, r] = send_carry(1, r, two, False, ends)

    sums2 = fresh()
    for r in rows:
        carry = take_carry(1, r, two, False, sent[1, r])
        scan_pass(r, two, False, carry, Forward(R.x2, R.s2))
        for sl, part in tiles[r]:
            gated, slope, gate, prod = mixer(two, R.s2, R.u2, R.gl2, sl)
            R.result[sl, :] = (R.h2[sl, :] + gated).astype(BF16)
            d_out = dot(gather[part, :], R.cin[line[r], :])
            R.d_mid[sl, :] = d_out
            back_front(two, d_out, slope, gate, prod, R.u2, R.ds2, R.dy2, sums2, sl)
        mover.run(2.0)
        ends, _ = scan_pass(r, two, True, zero_state, None)
        sent[2, r] = send_carry(2, r, two, True, ends)
    product_grads(two, R.gl2, R.ds2, R.s2, R.dy2)

    sums1 = fresh()
    da2, da1 = Adjoint(R.x2, R.dv2).zero(), Adjoint(R.x1, R.dv1).zero()
    for r in rows:
        carry = take_carry(2, r, two, True, sent[2, r])
        mover.run(0.3)
        _, da = scan_pass(r, two, True, carry, Adjoint(R.x2, R.dv2))
        da2 = (da2[0] + da[0], da2[1] + da[1])
        mover.run(0.3)
        for sl, _ in tiles[r]:
            d_mid = back_norm(two, R.d_mid[sl, :], R.dv2, R.m2, R.dy2, R.z2, R.r2, sums2, sl)
            R.d_mid[sl, :] = d_mid
            back_front(
                one, d_mid, R.gd1[sl, :], R.gate1[sl, :], R.prod1[sl, :],
                R.u1, R.ds1, R.dy1, sums1, sl,
            )
            mover.run(1.3)
        ends, _ = scan_pass(r, one, False, zero_state, None)
        mover.run(0.3)
        sent[3, r] = send_carry(3, r, one, False, ends)
    R.small_g[...] = jnp.zeros((2 * SUB, width), F32)
    matrix_grads(two, R.u2, R.dv2, da2)
    mover.run(0.8)
    product_grads(one, R.gl1, R.ds1, R.s1, R.dy1)

    for r in rows:
        carry = take_carry(3, r, one, False, sent[3, r])
        mover.run(0.3)
        _, da = scan_pass(r, one, False, carry, Adjoint(R.x1, R.dv1))
        da1 = (da1[0] + da[0], da1[1] + da[1])
        mover.run(0.3)
        for sl, _ in tiles[r]:
            d_in = back_norm(one, R.d_mid[sl, :], R.dv1, R.m1, R.dy1, R.z1, R.r1, sums1, sl)
            R.stage[sl, :] = d_in.astype(BF16)
        mover.run(0.5)
    matrix_grads(one, R.u1, R.dv1, da1)
    for k, name in enumerate(("gain", "skip", "bias")):
        for l, sums in enumerate((sums1, sums2)):
            row = 2 * k + l
            R.small_g[row : row + 1, :] = jnp.sum(sums[name], axis=0, keepdims=True)
    mover.start(chunks["s"])
    mover.run(0.8)
    ungather = jnp.where(i1 == (i0 & (per_seg - 1)) * SUB + (i0 >> place_bits), 1.0, 0.0).astype(BF16)
    for r in rows:
        R.in_grad[r] = dot(ungather, R.stage[line[r], :]).astype(BF16)
    mover.run(0.3)
    for r in rows:
        R.out[r] = dot(ungather, R.result[line[r], :]).astype(BF16)
    mover.run(0.3)
    mover.drain()


def finish_kernel(states, out_v, in_grad_v, small_v, b_v, c_v, w_v, *refs):
    out, in_grad, gain, lam_re, lam_im, steps, b_re, b_im, c_re, c_im, skip, w, bias = refs[:13]
    sem, *held = refs[13:]
    pairs = [
        (b_v.at[:, :, pl.ds(0, states)], b_re),
        (b_v.at[:, :, pl.ds(states, states)], b_im),
        (c_v.at[:, pl.ds(0, states)], c_re),
        (c_v.at[:, pl.ds(states, states)], c_im),
        (w_v, w),
        (out_v, out),
        (in_grad_v, in_grad),
    ]
    copies = [pltpu.make_async_copy(a, b, sem.at[k]) for k, (a, b) in enumerate(pairs)]
    for copy in copies:
        copy.start()
    for k, (ref, target) in enumerate(zip(held, (gain, skip, bias, lam_re, lam_im, steps))):
        ref[...] = small_v[2 * k : 2 * k + 2, 0 : ref.shape[1]]
        copy = pltpu.make_async_copy(ref, target, sem.at[len(pairs) + k])
        copy.start()
        copies.append(copy)
    for copy in copies:
        copy.wait()


def on_device(n_tm, n_rows, *args):
    inputs, lam_re = args[0], args[3]
    rows_dev, group, width = inputs.shape
    states = lam_re.shape[1]
    tokens = rows_dev * group
    P2 = 2 * states
    chunks = plan_chunks(n_tm, n_rows, width, P2)
    cfg = (tokens, width, states, rows_dev, group, n_tm, n_rows, chunks)
    vm = pl.BlockSpec(memory_space=pltpu.VMEM)
    hbm = pl.BlockSpec(memory_space=pl.ANY)
    far = pl.BlockSpec(memory_space=pltpu.HBM)
    in_specs = [far] * 14
    out_specs = [vm] * 6
    out_shape = [
        jax.ShapeDtypeStruct(inputs.shape, BF16),
        jax.ShapeDtypeStruct(inputs.shape, BF16),
        jax.ShapeDtypeStruct((2 * SUB, width), F32),
        jax.ShapeDtypeStruct((2, width, P2), F32),
        jax.ShapeDtypeStruct((2, P2, width), F32),
        jax.ShapeDtypeStruct((2, width, width), F32),
    ]

    def big(cols, dtype=F32):
        return pltpu.VMEM((tokens, cols), dtype)

    bits = int(math.log2(n_tm * n_rows))
    scratch = [
        big(width, BF16), big(width, BF16),
        pltpu.VMEM((2, width, states), BF16), pltpu.VMEM((2, width, states), BF16),
        pltpu.VMEM((2, P2, width), BF16), pltpu.VMEM((2, width, width), BF16),
        big(width), big(width), big(width), big(width), big(128), big(128),
        big(width, BF16), big(width, BF16), big(P2), big(P2), big(P2),
        big(P2, BF16), big(P2, BF16), big(width, BF16), big(width, BF16),
        big(width), big(width), big(width), big(width),
        big(width, BF16), big(width, BF16), big(width, BF16), big(width, BF16),
        big(P2, BF16), big(P2, BF16),
        pltpu.VMEM((width, P2), BF16), pltpu.VMEM((width, P2), BF16),
        big(128), big(width, BF16), big(width, BF16),
        pltpu.VMEM((2 * SUB, width), F32), pltpu.VMEM((2, width, P2), F32),
        pltpu.VMEM((2, P2, width), F32), pltpu.VMEM((2, width, width), F32),
        pltpu.VMEM((4, rows_dev, 1, P2 + 128), F32),
        pltpu.VMEM((4, rows_dev, n_tm, 1, P2 + 128), F32),
        pltpu.SemaphoreType.DMA((2 * rows_dev + 14,)),
        pltpu.SemaphoreType.DMA((4, rows_dev)), pltpu.SemaphoreType.DMA((4, rows_dev)),
        pltpu.SemaphoreType.DMA((PUTS,)), pltpu.SemaphoreType.DMA((bits * GETS,)),
    ]
    for k in (1, 2, 3, 4, 5, 10, 12):
        scratch.append(pltpu.VMEM(args[k].shape, args[k].dtype))
    for chunk in chunks.values():
        scratch.append(pltpu.VMEM((chunk.land_rows, chunk.width), F32))
    held = pl.pallas_call(
        functools.partial(kernel, cfg),
        out_shape=[pltpu.VMEM(o.shape, o.dtype) for o in out_shape],
        in_specs=in_specs,
        out_specs=out_specs,
        scratch_shapes=scratch,
        compiler_params=pltpu.CompilerParams(
            collective_id=0, has_side_effects=True, vmem_limit_bytes=53 * 2**20
        ),
    )(*args)
    grads = [args[k] for k in range(2, 13)]
    final_shape = [out_shape[0]] * 2 + [jax.ShapeDtypeStruct(g.shape, F32) for g in grads]
    final_specs = [hbm] * 13
    return tuple(
        pl.pallas_call(
            functools.partial(finish_kernel, states),
            out_shape=final_shape,
            in_specs=[hbm, hbm, vm, hbm, hbm, hbm],
            out_specs=final_specs,
            scratch_shapes=[pltpu.SemaphoreType.DMA((13,))]
            + [pltpu.VMEM((2, width), F32)] * 3
            + [pltpu.VMEM((2, states), F32)] * 3,
            compiler_params=pltpu.CompilerParams(vmem_limit_bytes=2**20),
        )(*held)
    )


def solution(mesh):
    rows = P("rows", "tm", None)
    in_specs = (rows, P("rows", "tm")) + (P(),) * 11 + (rows,)
    out_specs = (rows, rows) + (P(),) * 11
    return jax.shard_map(
        functools.partial(on_device, mesh.shape["tm"], mesh.shape["rows"]),
        mesh=mesh,
        in_specs=in_specs,
        out_specs=out_specs,
        check_vma=False,
    )
```

```python
import functools
import math

import jax
import jax.numpy as jnp
from jax import lax
from jax.experimental import pallas as pl
from jax.experimental.pallas import tpu as pltpu
from jax.sharding import PartitionSpec as P

NORM_EPS = 1e-05
MESH = pl.DeviceIdType.MESH
F32 = jnp.float32
BF16 = jnp.bfloat16
SUB = 8
UNROLL = 16
PUTS, GETS = 24, 15
TILE = 256
STEPS = [128, 128, 256, 256, 128, 128]
ORDERS = [
    "YX", "XY", "YX", "ZX", "yx", "XY", "zy", "ZY", "YX", "xy", "zx", "yx", "xy", "xy", "XY",
    "YX", "yz", "YX", "xy", "XY", "xy", "xy", "yz",
]


class Refs:
    pass


def horner(value, coeffs):
    total = coeffs[-1]
    for coeff in coeffs[-2::-1]:
        total = total * value + coeff
    return total


def discretize(lam_re, lam_im, time_steps):
    growth = lam_re * time_steps
    angles = lam_im * time_steps
    square = angles * angles
    fact = math.factorial
    grow = growth * horner(growth, [1.0 / fact(k + 1) for k in range(8)])
    sine = angles * horner(square, [(-1.0) ** k / fact(2 * k + 1) for k in range(7)])
    dip = square * horner(square, [(-1.0) ** k / fact(2 * k + 2) for k in range(7)])
    cosine = 1.0 - dip
    magnitude = 1.0 + grow
    a_re = magnitude * cosine
    a_im = magnitude * sine
    e_re = grow * cosine - dip
    modulus = lam_re * lam_re + lam_im * lam_im
    q_re = (e_re * lam_re + a_im * lam_im) / modulus
    q_im = (a_im * lam_re - e_re * lam_im) / modulus
    return (a_re, a_im, q_re, q_im)


def cmul(a, b):
    return (a[0] * b[0] - a[1] * b[1], a[0] * b[1] + a[1] * b[0])


def dot(a, b):
    return jnp.dot(a, b, preferred_element_type=F32)


def dot_nt(a, b):
    return lax.dot_general(a, b, (((1,), (1,)), ((), ())), preferred_element_type=F32)


def dot_tn(a, b):
    return lax.dot_general(a, b, (((0,), (0,)), ((), ())), preferred_element_type=F32)


def fold(value):
    rows, cols = value.shape
    return jnp.sum(value.reshape(rows // SUB, SUB, cols), axis=0)


def gauss(y):
    size = jnp.abs(y) * (0.5**0.5)
    bell = jnp.exp(-0.5 * (y * y))
    t = pltpu.reciprocal(1.0 + 0.3275911 * size, approx=True)
    tail = (0.5 * t * bell) * horner(
        t, [0.254829592, -0.284496736, 1.421413741, -1.453152027, 1.061405429]
    )
    cdf = jnp.where(y >= 0.0, 1.0 - tail, tail)
    return cdf, y * bell * ((2.0 * math.pi) ** -0.5)


class Chunk:
    def __init__(self, index, grad, rows, cols, groups):
        self.index, self.grad, self.rows, self.cols = index, grad, rows, cols
        self.width = cols[1] - cols[0]
        self.stages = []
        size, land, bits = rows, 0, []
        for group in groups:
            fits = size % (SUB << len(group)) == 0
            for part in [group] if fits else [(bit,) for bit in group]:
                halved = size % (SUB << len(part)) == 0
                size = size >> len(part) if halved else size
                self.stages.append((part, size, halved, land))
                land += size * ((1 << len(part)) - 1)
                bits.append(part)
        self.bits, self.land_rows = bits, land
        self.steps = [("sum", i) for i in range(len(bits))]
        self.steps += [("get", i) for i in reversed(range(len(bits))) if self.stages[i][2]]


def plan_chunks(n_tm, n_rows, width, P2):
    tm_bits, row_bits = int(math.log2(n_tm)), int(math.log2(n_rows))
    core = [("tm", 0)]
    half = (tm_bits - 1) // 2
    xs = [("tm", 1 + k) for k in range(half)]
    ys = [("tm", 1 + half + k) for k in range(tm_bits - 1 - half)]
    zs = [("rows", k) for k in range(row_bits)]

    def order(name):
        pair = name.isupper()
        axes = {"x": [(b,) for b in xs], "y": [(b,) for b in ys]}
        axes["z"] = [tuple(zs[:2])] if pair else [(b,) for b in zs[:1]]
        first, second = name.lower()
        third = ({"x", "y", "z"} - {first, second}).pop()
        rest = [(b,) for b in zs[2 if pair else 1 :]]
        return [(core[0],)] + axes[first] + axes[second] + axes[third] + rest

    chunks = {}
    count = 0
    plan, steps = iter(ORDERS), iter(STEPS)
    for l in (1, 0):
        for name, rows, cols in (("w", width, width), ("c", P2, width), ("b", width, P2)):
            step = next(steps)
            for k in range(0, cols, step):
                chunks[name, l, k] = Chunk(
                    count, (name, l), rows, (k, k + step), order(next(plan))
                )
                count += 1
    chunks["s"] = Chunk(count, ("s", None), 2 * SUB, (0, width), order("yx"))
    return chunks


class Mover:
    RATE = {"c": 650e3, "x": 46e3, "y": 46e3, "z": 46e3, "mid": 46e3}
    DELAY = {"c": 0.8, "x": 1.7, "y": 1.7, "z": 1.7}
    EXCHANGE = 3.2
    AHEAD = 2.5

    def __init__(self, chunks, refs, lands, at, half_bits):
        self.chunks, self.refs, self.at, self.half_bits = chunks, refs, at, half_bits
        self.lands = lands
        self.now = 0.0
        self.free = {k: 0.0 for k in self.RATE}
        self.queue = {k: [] for k in self.DELAY}
        self.pending = []
        self.copies = {}
        self.starts = {}
        self.clock = 0
        self.gets, self.acked, self.puts, self.used = {}, {}, [], {}

    def coord(self, bit):
        return lax.rem(self.at[bit[0]] // (1 << bit[1]), 2)

    def peer(self, bits):
        ids = {}
        for bit in bits:
            own = ids.get(bit[0], self.at[bit[0]])
            ids[bit[0]] = own + (1 - 2 * self.coord(bit)) * (1 << bit[1])
        return ids

    def share(self, bits, other=()):
        part = 0
        for bit in bits:
            own = self.coord(bit)
            part = 2 * part + (1 - own if bit in other else own)
        return part

    def begin(self, chunk, level):
        key = (chunk.rows, tuple(chunk.bits[:level]))
        if key not in self.starts:
            if level == 0:
                self.starts[key] = 0
            else:
                bits, size, halved, _ = chunk.stages[level - 1]
                before = self.begin(chunk, level - 1)
                self.starts[key] = before + self.share(bits) * size if halved else before
        return self.starts[key]

    def view(self, chunk, start, size, done=False):
        ref = self.refs[1 if done else 0][chunk.grad[0]]
        rows = pl.ds(pl.multiple_of(start, SUB) if not isinstance(start, int) else start, size)
        cols = pl.ds(chunk.cols[0], chunk.width)
        l = chunk.grad[1]
        return ref.at[rows, cols] if l is None else ref.at[l, rows, cols]

    def link(self, bits):
        bit = bits[0]
        if bit[0] == "rows":
            return "z"
        return "c" if bit[1] == 0 else ("x" if bit[1] <= self.half_bits else "y")

    def cost(self, chunk, k):
        bit, size, _, _ = chunk.stages[chunk.steps[k][1]]
        return size * chunk.width * 4 / self.RATE[self.link(bit)] * (3 if len(bit) > 1 else 1)

    def left(self, chunk, k):
        total = 0.0
        for j in range(k, len(chunk.steps)):
            bit = chunk.stages[chunk.steps[j][1]][0]
            total += self.cost(chunk, j) + self.DELAY[self.link(bit)]
        return total

    def push(self, chunk, k):
        bit = chunk.stages[chunk.steps[k][1]][0]
        self.queue[self.link(bit)].append((-self.left(chunk, k), chunk.index, k, chunk))

    def take_get(self, bit):
        pool = self.gets.setdefault(bit, {})
        for k, released in pool.items():
            if released is not None and released < self.acked.get(bit, 0):
                pool[k] = None
                return k
        k = sum(len(other) for other in self.gets.values())
        pool[k] = None
        return k

    def take_put(self):
        if True in self.puts:
            k = self.puts.index(True)
            self.puts[k] = False
            return k
        self.puts.append(False)
        return len(self.puts) - 1

    def pump(self):
        for link, queue in self.queue.items():
            while queue and self.free[link] < self.now + self.AHEAD:
                item = min(queue, key=lambda entry: entry[:3])
                queue.remove(item)
                self.launch(item[3], item[2])

    def launch(self, chunk, k):
        kind, i = chunk.steps[k]
        bit, size, halved, land = chunk.stages[i]
        put, get = self.take_put(), self.take_get(bit)
        self.clock += 1
        self.used[chunk.index, k] = (put, get, self.clock)
        if self.refs is not None:
            self.copies[chunk.index, k] = copies = []
            for m in range(1, 1 << len(bit)):
                other = [b for n, b in enumerate(bit) if m >> n & 1]
                if kind == "sum":
                    before = self.begin(chunk, i)
                    if halved:
                        before = before + self.share(bit, other) * size
                    src = self.view(chunk, before, size)
                    dst = self.lands[chunk.index].at[pl.ds(land + (m - 1) * size, size)]
                else:
                    src = dst = self.view(chunk, self.begin(chunk, i + 1), size, True)
                copy = pltpu.make_async_remote_copy(
                    src,
                    dst,
                    self.refs[2].at[put],
                    self.refs[3].at[get],
                    device_id=self.peer(other),
                    device_id_type=MESH,
                )
                copy.start()
                copies.append(copy)
        link = self.link(bit)
        cost = self.cost(chunk, k)
        far = link == "z" and bit[-1][1] > 0
        began = max(self.now, self.free[link], self.free["mid"] if far else 0.0)
        self.free[link] = done = began + cost
        if far:
            self.free["mid"] = done = began + cost * (2 if len(bit) == 1 else 4 / 3)
        self.pending.append((done + self.DELAY[link], chunk.index, k, chunk))
        self.now += 0.04 * ((1 << len(bit)) - 1)

    def finish(self, item):
        _, _, k, chunk = item
        kind, i = chunk.steps[k]
        bit, size, _, land = chunk.stages[i]
        real = self.refs is not None
        copies = self.copies.get((chunk.index, k))
        many = (1 << len(bit)) - 1
        if real and many == 1:
            copies[0].wait()
        elif real:
            whole = self.lands[chunk.index].at[pl.ds(land, many * size)]
            put, get, _ = self.used[chunk.index, k]
            pltpu.make_async_copy(whole, whole, self.refs[3].at[get]).wait()
            pltpu.make_async_copy(whole, whole, self.refs[2].at[put]).wait()
        put, get, launched = self.used[chunk.index, k]
        self.clock += 1
        self.puts[put] = True
        self.gets[bit][get] = self.clock
        self.acked[bit] = max(self.acked.get(bit, 0), launched)
        self.now += 0.08
        more = k + 1 < len(chunk.steps)
        if kind == "get":
            if more:
                self.push(chunk, k + 1)
            self.pump()
            return
        start = self.begin(chunk, i + 1) if real else 0

        def add(off, rows):
            self.now += rows * chunk.width * 4 / 3e6 * (many + 1) / 2
            if not real:
                return
            ref = self.view(chunk, start + off, rows)
            total = ref[...]
            for m in range(many):
                at = land + m * size + off
                at = pl.multiple_of(at, SUB) if not isinstance(at, int) else at
                total = total + self.lands[chunk.index][pl.ds(at, rows), :]
            last = i + 1 == len(chunk.bits)
            into = self.view(chunk, start + off, rows, True) if last else ref
            into[...] = total

        follows = chunk.stages[i + 1] if i + 1 < len(chunk.bits) else None
        if follows is not None and follows[2] and len(follows[0]) == 1:
            half = size // 2
            mine = self.share(follows[0]) if real else 0
            add((1 - mine) * half, half)
            self.push(chunk, k + 1)
            self.pump()
            add(mine * half, half)
        else:
            add(0, size)
            if more:
                self.push(chunk, k + 1)
            self.pump()

    def first(self):
        return min(self.pending, key=lambda item: item[:3])

    def start(self, chunk):
        self.push(chunk, 0)
        self.pump()

    def run(self, spent):
        self.now += spent
        while self.pending and self.first()[0] <= self.now:
            item = self.first()
            self.pending.remove(item)
            self.finish(item)

    def message(self):
        return max(self.now, self.free["x"], self.free["y"]) + self.EXCHANGE

    def until(self, time):
        while self.pending and self.first()[0] <= time:
            item = self.first()
            self.pending.remove(item)
            self.now = max(self.now, item[0])
            self.finish(item)
        self.now = max(self.now, time)

    def drain(self):
        while self.pending:
            item = self.first()
            self.pending.remove(item)
            self.now = max(self.now, item[0])
            self.finish(item)


def kernel(cfg, *refs):
    tokens, width, states, rows_dev, group, n_tm, n_rows, chunks = cfg
    R = Refs()
    (
        R.inputs, R.resets_in, R.gains_in, R.lam_re_in, R.lam_im_in, R.steps_in, R.b_re, R.b_im,
        R.c_re, R.c_im, R.skip_in, R.glu_w, R.glu_b_in, R.cot, R.out, R.in_grad, R.small_o, R.b_o,
        R.c_o, R.w_o, R.xin, R.cin, R.wb_re, R.wb_im, R.wc, R.wg, R.h1, R.h2, R.z1, R.z2, R.r1,
        R.r2, R.u1, R.u2, R.v, R.x1, R.x2, R.s1, R.s2, R.gl1, R.gl2, R.gd1, R.gate1, R.prod1,
        R.d_mid, R.dy1, R.dy2, R.ds1, R.ds2, R.dv1, R.dv2, R.m1, R.m2, R.keep, R.stage, R.result, R.small_g,
        R.b_g, R.c_g, R.w_g, R.msg, R.got, R.in_sem, R.send_sem,
        R.recv_sem, R.put_sem, R.get_sem, R.resets, R.gains, R.lam_re, R.lam_im, R.steps, R.skip,
        R.glu_b,
        *lands,
    ) = refs
    segs = SUB
    per_seg = group // segs
    at = lax.axis_index("tm")
    P2 = 2 * states

    barrier = pltpu.get_barrier_semaphore()
    tm_bits = int(math.log2(n_tm))
    others = []
    for m in reversed(range(1, n_tm)):
        flips = [(1 - 2 * lax.rem(at // (1 << b), 2)) * (1 << b) for b in range(tm_bits) if m >> b & 1]
        others.append(at + sum(flips))
    for other in others:
        pl.semaphore_signal(barrier, inc=1, device_id={"tm": other}, device_id_type=MESH)
    row_at = lax.axis_index("rows")
    grads = {"b": R.b_g, "c": R.c_g, "w": R.w_g, "s": R.small_g}
    sums = {"b": R.b_o, "c": R.c_o, "w": R.w_o, "s": R.small_o}
    mover_refs = (grads, sums, R.put_sem, R.get_sem)
    half_bits = (int(math.log2(n_tm)) - 1) // 2
    mover = Mover(chunks, mover_refs, lands, {"tm": at, "rows": row_at}, half_bits)
    row_bits = int(math.log2(n_rows))
    zs = [("rows", k) for k in range(row_bits)]
    greeted = [[z] for z in zs] + ([zs[:2]] if row_bits > 1 else [])
    for bits in greeted:
        pl.semaphore_signal(barrier, inc=1, device_id=mover.peer(bits), device_id_type=MESH)

    def load(k, src, dst):
        copy = pltpu.make_async_copy(src, dst, R.in_sem.at[k])
        copy.start()
        return copy

    cp_x = [load(r, R.inputs.at[r], R.xin.at[pl.ds(r * group, group)]) for r in range(rows_dev)]
    k0 = 2 * rows_dev + 5
    pairs = [
        (R.resets_in, R.resets), (R.lam_re_in, R.lam_re), (R.lam_im_in, R.lam_im),
        (R.steps_in, R.steps), (R.gains_in, R.gains), (R.skip_in, R.skip), (R.glu_b_in, R.glu_b),
    ]
    cp_small = [load(k0 + k, src, dst) for k, (src, dst) in enumerate(pairs)]
    k0 = rows_dev
    cp_b = [load(k0, R.b_re.at[0], R.wb_re.at[0]), load(k0 + 1, R.b_im.at[0], R.wb_im.at[0])]
    cp_c = [
        load(k0 + 2, R.c_re, R.wc.at[:, pl.ds(0, states)]),
        load(k0 + 3, R.c_im, R.wc.at[:, pl.ds(states, states)]),
    ]
    k1 = 2 * rows_dev + 12
    cp_w = [
        load(k0 + 4, R.glu_w, R.wg),
        load(k1, R.b_re.at[1], R.wb_re.at[1]),
        load(k1 + 1, R.b_im.at[1], R.wb_im.at[1]),
    ]
    cp_t = [
        load(k0 + 5 + r, R.cot.at[r], R.cin.at[pl.ds(r * group, group)])
        for r in range(rows_dev)
    ]

    for cp in cp_small:
        cp.wait()

    place_bits = int(math.log2(per_seg))
    i0 = lax.broadcasted_iota(jnp.int32, (group, group), 0)
    i1 = lax.broadcasted_iota(jnp.int32, (group, group), 1)
    hit = i1 == (i0 & (SUB - 1)) * per_seg + (i0 >> 3)
    gather = jnp.where(hit, 1.0, 0.0).astype(BF16)
    kept = 1.0 - R.resets[...].astype(F32)
    for r in range(rows_dev):
        spread = jnp.where(hit, jnp.broadcast_to(kept[r : r + 1], (group, group)), 0.0)
        R.keep[r * group : (r + 1) * group, :] = dot(
            spread.astype(BF16), jnp.ones((group, 128), BF16)
        )

    seg_id = lax.broadcasted_iota(jnp.int32, (SUB, 128), 0)

    def shift(value, forward, by=1):
        return pltpu.roll(value, by if forward else SUB - by, 0)

    def wide(mask, cols):
        return jnp.concatenate([mask] * (cols // 128), axis=1)

    def inside(forward, by):
        return seg_id >= by if forward else seg_id < SUB - by

    window, excl, total_mask, whole = {}, {}, {}, {}
    for r in range(rows_dev):
        places = [R.keep[r * group + j * SUB : r * group + (j + 1) * SUB] for j in range(per_seg)]
        while len(places) > 1:
            places = [a * b for a, b in zip(places[::2], places[1::2])]
        whole[r] = places[0]

    def masks(forward):
        for r in range(rows_dev):
            run, seen = whole[r], whole[r]
            for by in (1, 2, 4):
                ok = inside(forward, by)
                window[r, forward, by] = jnp.where(ok, run, 0.0)
                seen = jnp.where(ok, seen * shift(seen, forward, by), seen)
                run = run * shift(run, forward, by)
            excl[r, forward] = jnp.where(inside(forward, 1), shift(seen, forward), 1.0)
            if forward:
                total_mask[r] = seen[SUB - 1 : SUB]

    def constants(l):
        lam = [n[l : l + 1, :] for n in (R.lam_re, R.lam_im, R.steps)]
        a_re, a_im, q_re, q_im = discretize(*lam)
        power = (a_re, a_im)
        for _ in range(place_bits):
            power = cmul(power, power)
        powers = {1: power}
        for by in (1, 2, 4):
            powers[2 * by] = cmul(powers[by], powers[by])
        for forward in (True, False):
            index = wide(seg_id if forward else SUB - 1 - seg_id, states)
            at_seg = (jnp.ones((SUB, states), F32), jnp.zeros((SUB, states), F32))
            for by in (1, 2, 4):
                more = cmul(at_seg, powers[by])
                at_seg = tuple(
                    jnp.where((index & by) != 0, m, o) for m, o in zip(more, at_seg)
                )
            powers[forward, 0] = at_seg
        return dict(lam=lam, a=(a_re, a_im), q=(q_re, q_im), powers=powers, l=l)

    def input_matrix(layer, m_ref):
        q_re, q_im = layer["q"]
        l = layer["l"]
        step = 128
        for i in range(width // step):
            sl = slice(i * step, (i + 1) * step)
            br = R.wb_re[l, sl, :].astype(F32)
            bi = R.wb_im[l, sl, :].astype(F32)
            m_ref[sl, 0:states] = (q_re * br - q_im * bi).astype(BF16)
            m_ref[sl, states:P2] = (q_re * bi + q_im * br).astype(BF16)

    def scan_pass(r, layer, forward, start, sink):
        a = [jnp.broadcast_to(p, (SUB, states)) for p in layer["a"]]
        v_ref, keep_ref = R.v, R.keep

        def one(j, carry):
            base = pl.multiple_of(r * group + j * SUB, SUB)
            keep = wide(keep_ref[pl.ds(base, SUB), :], states)
            v = (v_ref[pl.ds(base, SUB), 0:states], v_ref[pl.ds(base, SUB), states:P2])
            if forward:
                held = (keep * carry[0], keep * carry[1])
                prod = cmul(a, held)
                x = (prod[0] + v[0], prod[1] + v[1])
                return x, held, x
            prod = cmul(a, carry)
            x = (prod[0] + v[0], prod[1] + v[1])
            held = (keep * x[0], keep * x[1])
            return x, carry, held

        pair = 2

        def body(i, carry):
            state, extra = carry
            if forward:
                js = [i * pair + k for k in range(pair)]
            else:
                js = [per_seg - 1 - (i * pair + k) for k in range(pair)]
            xs = []
            for j in js:
                x, held, state = one(j, state)
                xs.append(x)
                if sink is not None:
                    extra = sink.each(r * group + j * SUB, x, held, extra)
            if sink is not None:
                low = js[0] if forward else js[-1]
                ordered = xs if forward else xs[::-1]
                sink.pair(r * group + low * SUB, ordered)
            return state, extra

        extra0 = sink.zero() if sink is not None else ()
        return lax.fori_loop(0, per_seg // pair, body, (start, extra0), unroll=UNROLL)

    class Forward:
        def __init__(self, x_ref, s_ref):
            self.x_ref, self.s_ref = x_ref, s_ref

        def zero(self):
            return ()

        def each(self, base, x, held, extra):
            base = pl.multiple_of(base, SUB)
            self.x_ref[pl.ds(base, SUB), 0:states] = x[0]
            self.x_ref[pl.ds(base, SUB), states:P2] = x[1]
            return extra

        def pair(self, base, xs):
            base = pl.multiple_of(base, 2 * SUB)
            re = jnp.concatenate([x[0] for x in xs], axis=0)
            im = jnp.concatenate([x[1] for x in xs], axis=0)
            self.s_ref[pl.ds(base, 2 * SUB), 0:states] = re.astype(BF16)
            self.s_ref[pl.ds(base, 2 * SUB), states:P2] = (-im).astype(BF16)

    class Adjoint:
        def __init__(self, x_ref, d_ref):
            self.x_ref, self.d_ref = x_ref, d_ref

        def zero(self):
            return (jnp.zeros((SUB, states), F32), jnp.zeros((SUB, states), F32))

        def each(self, base, x, held, extra):
            base = pl.multiple_of(base, SUB)
            xv = (self.x_ref[pl.ds(base, SUB), 0:states], self.x_ref[pl.ds(base, SUB), states:P2])
            prod = cmul(xv, held)
            return (extra[0] + prod[0], extra[1] + prod[1])

        def pair(self, base, xs):
            base = pl.multiple_of(base, 2 * SUB)
            re = jnp.concatenate([x[0] for x in xs], axis=0)
            im = jnp.concatenate([x[1] for x in xs], axis=0)
            self.d_ref[pl.ds(base, 2 * SUB), 0:states] = re.astype(BF16)
            self.d_ref[pl.ds(base, 2 * SUB), states:P2] = (-im).astype(BF16)

    first_wait = [True]

    def send_carry(e, r, layer, forward, ends):
        seen = ends
        for by in (1, 2, 4):
            mask = wide(window[r, forward, by], states)
            prod = cmul(layer["powers"][by], tuple(shift(p, forward, by) for p in seen))
            seen = (seen[0] + mask * prod[0], seen[1] + mask * prod[1])
        ok = wide(inside(forward, 1), states)
        run = tuple(jnp.where(ok, shift(p, forward), 0.0) for p in seen)
        last = slice(SUB - 1, SUB) if forward else slice(0, 1)
        R.msg[e, r, :, 0:states] = seen[0][last]
        R.msg[e, r, :, states:P2] = seen[1][last]
        R.msg[e, r, :, P2 : P2 + 128] = total_mask[r]
        if first_wait[0]:
            pl.semaphore_wait(barrier, n_tm - 1 + len(greeted))
            first_wait[0] = False
        for other in others:
            copy = pltpu.make_async_remote_copy(
                R.msg.at[e, r],
                R.got.at[e, r, at],
                R.send_sem.at[e, r],
                R.recv_sem.at[e, r],
                device_id={"tm": other},
                device_id_type=MESH,
            )
            copy.start()
        return run, mover.message()

    def take_carry(e, r, layer, forward, sent):
        run, arrival = sent
        mover.until(arrival)
        slots = R.got.at[e, r, pl.ds(0, n_tm - 1)]
        pltpu.make_async_copy(slots, slots, R.recv_sem.at[e, r]).wait()
        pltpu.make_async_copy(slots, slots, R.send_sem.at[e, r]).wait()
        span = layer["powers"][SUB]
        carry = (jnp.zeros((1, states), F32), jnp.zeros((1, states), F32))
        order = range(n_tm) if forward else range(n_tm - 1, -1, -1)
        for k in list(order)[:-1]:
            before = (at > k) if forward else (at < k)
            mask = wide(R.got[e, r, k, :, P2 : P2 + 128], states)
            prod = cmul(span, carry)
            new = (
                R.got[e, r, k, :, 0:states] + mask * prod[0],
                R.got[e, r, k, :, states:P2] + mask * prod[1],
            )
            carry = tuple(jnp.where(before, n, c) for n, c in zip(new, carry))
        prod = cmul(layer["powers"][forward, 0], carry)
        mask = wide(excl[r, forward], states)
        return (run[0] + mask * prod[0], run[1] + mask * prod[1])

    zero_state = (jnp.zeros((SUB, states), F32), jnp.zeros((SUB, states), F32))

    tiles = {
        r: [(slice(r * group + i, r * group + i + TILE), slice(i, i + TILE)) for i in range(0, group, TILE)]
        for r in range(rows_dev)
    }
    line = [slice(r * group, (r + 1) * group) for r in range(rows_dev)]
    rows = range(rows_dev)

    def norm_front(h, layer, z_ref, r_ref, u_ref, m_ref, sl):
        mean = jnp.mean(h, axis=1, keepdims=True)
        centred = h - mean
        var = jnp.mean(centred * centred, axis=1, keepdims=True)
        r = lax.rsqrt(var + NORM_EPS)
        z = centred * r
        u = (z * R.gains[layer["l"] : layer["l"] + 1, :]).astype(BF16)
        z_ref[sl, :] = z
        r_ref[sl, :] = jnp.broadcast_to(r, (r.shape[0], 128))
        u_ref[sl, :] = u
        R.v[sl, :] = dot(u, m_ref[...])

    def mixer(layer, s_ref, u_ref, gl_ref, sl):
        l = layer["l"]
        s = s_ref[sl, :]
        y = dot(s, R.wc[l]) + R.skip[l : l + 1, :] * u_ref[sl, :].astype(F32)
        cdf, dens = gauss(y)
        gelu = y * cdf
        low = gelu.astype(BF16)
        gl_ref[sl, :] = low
        pre = dot(low, R.wg[l]) + R.glu_b[l : l + 1, :]
        gate = 0.5 * jnp.tanh(0.5 * pre) + 0.5
        gated = gelu * gate
        return gated, cdf + dens, gate, gated * (1.0 - gate)

    def back_front(layer, d_out, slope, gate, prod, u_ref, ds_ref, dy_ref, sums, sl):
        l = layer["l"]
        ds = (d_out * prod).astype(BF16)
        ds_ref[sl, :] = ds
        d_gelu = d_out * gate + dot_nt(ds, R.wg[l])
        dy = (d_gelu * slope).astype(BF16)
        dy_ref[sl, :] = dy
        R.v[sl, :] = dot_nt(dy, R.wc[l])
        sums["bias"] = sums["bias"] + fold(ds.astype(F32))
        sums["skip"] = sums["skip"] + fold(dy.astype(F32) * u_ref[sl, :].astype(F32))

    def back_norm(layer, d_out, dv_ref, m_ref, dy_ref, z_ref, r_ref, sums, sl):
        l = layer["l"]
        dn = dy_ref[sl, :].astype(F32) * R.skip[l : l + 1, :] + dot_nt(dv_ref[sl, :], m_ref[...])
        z = z_ref[sl, :]
        sums["gain"] = sums["gain"] + fold(dn * z)
        w = dn * R.gains[l : l + 1, :]
        mean_w = jnp.mean(w, axis=1, keepdims=True)
        mean_wz = jnp.mean(w * z, axis=1, keepdims=True)
        r = wide(r_ref[sl, :], width)
        return d_out + r * (w - mean_w - z * mean_wz)

    def fresh():
        return {k: jnp.zeros((SUB, width), F32) for k in ("gain", "skip", "bias")}

    def start(name, l, first, count):
        for k in range(first, first + count, SUB):
            if (name, l, k) in chunks:
                mover.start(chunks[name, l, k])

    def product_grads(layer, gl_ref, ds_ref, s_ref, dy_ref):
        l = layer["l"]
        for name, left, right in (("w", gl_ref, ds_ref), ("c", s_ref, dy_ref)):
            for k in range(0, width, 256):
                grads[name][l, :, k : k + 256] = dot_tn(left[...], right[:, k : k + 256])
                start(name, l, k, 256)
                mover.run(0.15)

    def matrix_grads(layer, u_ref, dv_ref, da):
        l = layer["l"]
        q_re, q_im = layer["q"]
        full = dot_tn(u_ref[...], dv_ref[...])
        g_re, g_im = full[:, 0:states], full[:, states:P2]
        R.b_g[l, :, 0:states] = q_re * g_re + q_im * g_im
        R.b_g[l, :, states:P2] = q_re * g_im - q_im * g_re
        start("b", l, 0, P2)
        br, bi = R.wb_re[l].astype(F32), R.wb_im[l].astype(F32)
        dq_re = jnp.sum(fold(br * g_re + bi * g_im), axis=0, keepdims=True)
        dq_im = jnp.sum(fold(br * g_im - bi * g_re), axis=0, keepdims=True)
        da_re = jnp.sum(da[0], axis=0, keepdims=True)
        da_im = -jnp.sum(da[1], axis=0, keepdims=True)
        _, pull = jax.vjp(discretize, *layer["lam"])
        lam_grads = pull((da_re, da_im, dq_re, dq_im))
        for k, grad in enumerate(lam_grads):
            row = 6 + 2 * k + l
            R.small_g[row : row + 1, 0:states] = grad

    one = constants(0)
    masks(True)
    for cp in cp_b:
        cp.wait()
    input_matrix(one, R.m1)
    for cp in cp_x:
        cp.wait()
    sent = {}
    for r in rows:
        for sl, part in tiles[r]:
            h = dot(gather[part, :], R.xin[line[r], :])
            R.h1[sl, :] = h
            norm_front(h, one, R.z1, R.r1, R.u1, R.m1, sl)
        ends, _ = scan_pass(r, one, True, zero_state, None)
        sent[0, r] = send_carry(0, r, one, True, ends)
    two = constants(1)
    masks(False)
    for cp in cp_c + cp_w + cp_t:
        cp.wait()
    input_matrix(two, R.m2)

    for r in rows:
        carry = take_carry(0, r, one, True, sent[0, r])
        scan_pass(r, one, True, carry, Forward(R.x1, R.s1))
        for sl, _ in tiles[r]:
            gated, slope, gate, prod = mixer(one, R.s1, R.u1, R.gl1, sl)
            R.gd1[sl, :] = slope
            R.gate1[sl, :] = gate
            R.prod1[sl, :] = prod
            h = R.h1[sl, :] + gated
            R.h2[sl, :] = h
            norm_front(h, two, R.z2, R.r2, R.u2, R.m2, sl)
        ends, _ = scan_pass(r, two, False, zero_state, None)
        sent[1, r] = send_carry(1, r, two, False, ends)

    sums2 = fresh()
    for r in rows:
        carry = take_carry(1, r, two, False, sent[1, r])
        scan_pass(r, two, False, carry, Forward(R.x2, R.s2))
        for sl, part in tiles[r]:
            gated, slope, gate, prod = mixer(two, R.s2, R.u2, R.gl2, sl)
            R.result[sl, :] = (R.h2[sl, :] + gated).astype(BF16)
            d_out = dot(gather[part, :], R.cin[line[r], :])
            R.d_mid[sl, :] = d_out
            back_front(two, d_out, slope, gate, prod, R.u2, R.ds2, R.dy2, sums2, sl)
        mover.run(2.0)
        ends, _ = scan_pass(r, two, True, zero_state, None)
        sent[2, r] = send_carry(2, r, two, True, ends)
    product_grads(two, R.gl2, R.ds2, R.s2, R.dy2)

    sums1 = fresh()
    da2, da1 = Adjoint(R.x2, R.dv2).zero(), Adjoint(R.x1, R.dv1).zero()
    for r in rows:
        carry = take_carry(2, r, two, True, sent[2, r])
        _, da = scan_pass(r, two, True, carry, Adjoint(R.x2, R.dv2))
        da2 = (da2[0] + da[0], da2[1] + da[1])
        mover.run(0.3)
    R.small_g[...] = jnp.zeros((2 * SUB, width), F32)
    matrix_grads(two, R.u2, R.dv2, da2)
    mover.run(0.8)
    for r in rows:
        mover.run(0.3)
        for sl, _ in tiles[r]:
            d_mid = back_norm(two, R.d_mid[sl, :], R.dv2, R.m2, R.dy2, R.z2, R.r2, sums2, sl)
            R.d_mid[sl, :] = d_mid
            back_front(
                one, d_mid, R.gd1[sl, :], R.gate1[sl, :], R.prod1[sl, :],
                R.u1, R.ds1, R.dy1, sums1, sl,
            )
            mover.run(1.3)
        ends, _ = scan_pass(r, one, False, zero_state, None)
        mover.run(0.3)
        sent[3, r] = send_carry(3, r, one, False, ends)
    product_grads(one, R.gl1, R.ds1, R.s1, R.dy1)

    for r in rows:
        carry = take_carry(3, r, one, False, sent[3, r])
        mover.run(0.3)
        _, da = scan_pass(r, one, False, carry, Adjoint(R.x1, R.dv1))
        da1 = (da1[0] + da[0], da1[1] + da[1])
        mover.run(0.3)
        for sl, _ in tiles[r]:
            d_in = back_norm(one, R.d_mid[sl, :], R.dv1, R.m1, R.dy1, R.z1, R.r1, sums1, sl)
            R.stage[sl, :] = d_in.astype(BF16)
        mover.run(0.5)
    matrix_grads(one, R.u1, R.dv1, da1)
    for k, name in enumerate(("gain", "skip", "bias")):
        for l, sums in enumerate((sums1, sums2)):
            row = 2 * k + l
            R.small_g[row : row + 1, :] = jnp.sum(sums[name], axis=0, keepdims=True)
    mover.start(chunks["s"])
    mover.run(0.8)
    ungather = jnp.where(i1 == (i0 & (per_seg - 1)) * SUB + (i0 >> place_bits), 1.0, 0.0).astype(BF16)
    for r in rows:
        R.in_grad[r] = dot(ungather, R.stage[line[r], :]).astype(BF16)
    mover.run(0.3)
    for r in rows:
        R.out[r] = dot(ungather, R.result[line[r], :]).astype(BF16)
    mover.run(0.3)
    mover.drain()


def finish_kernel(states, out_v, in_grad_v, small_v, b_v, c_v, w_v, *refs):
    out, in_grad, gain, lam_re, lam_im, steps, b_re, b_im, c_re, c_im, skip, w, bias = refs[:13]
    sem, *held = refs[13:]
    pairs = [
        (b_v.at[:, :, pl.ds(0, states)], b_re),
        (b_v.at[:, :, pl.ds(states, states)], b_im),
        (c_v.at[:, pl.ds(0, states)], c_re),
        (c_v.at[:, pl.ds(states, states)], c_im),
        (w_v, w),
        (out_v, out),
        (in_grad_v, in_grad),
    ]
    copies = [pltpu.make_async_copy(a, b, sem.at[k]) for k, (a, b) in enumerate(pairs)]
    for copy in copies:
        copy.start()
    for k, (ref, target) in enumerate(zip(held, (gain, skip, bias, lam_re, lam_im, steps))):
        ref[...] = small_v[2 * k : 2 * k + 2, 0 : ref.shape[1]]
        copy = pltpu.make_async_copy(ref, target, sem.at[len(pairs) + k])
        copy.start()
        copies.append(copy)
    for copy in copies:
        copy.wait()


def on_device(n_tm, n_rows, *args):
    inputs, lam_re = args[0], args[3]
    rows_dev, group, width = inputs.shape
    states = lam_re.shape[1]
    tokens = rows_dev * group
    P2 = 2 * states
    chunks = plan_chunks(n_tm, n_rows, width, P2)
    cfg = (tokens, width, states, rows_dev, group, n_tm, n_rows, chunks)
    vm = pl.BlockSpec(memory_space=pltpu.VMEM)
    hbm = pl.BlockSpec(memory_space=pl.ANY)
    far = pl.BlockSpec(memory_space=pltpu.HBM)
    in_specs = [far] * 14
    out_specs = [vm] * 6
    out_shape = [
        jax.ShapeDtypeStruct(inputs.shape, BF16),
        jax.ShapeDtypeStruct(inputs.shape, BF16),
        jax.ShapeDtypeStruct((2 * SUB, width), F32),
        jax.ShapeDtypeStruct((2, width, P2), F32),
        jax.ShapeDtypeStruct((2, P2, width), F32),
        jax.ShapeDtypeStruct((2, width, width), F32),
    ]

    def big(cols, dtype=F32):
        return pltpu.VMEM((tokens, cols), dtype)

    bits = int(math.log2(n_tm * n_rows))
    scratch = [
        big(width, BF16), big(width, BF16),
        pltpu.VMEM((2, width, states), BF16), pltpu.VMEM((2, width, states), BF16),
        pltpu.VMEM((2, P2, width), BF16), pltpu.VMEM((2, width, width), BF16),
        big(width), big(width), big(width), big(width), big(128), big(128),
        big(width, BF16), big(width, BF16), big(P2), big(P2), big(P2),
        big(P2, BF16), big(P2, BF16), big(width, BF16), big(width, BF16),
        big(width), big(width), big(width), big(width),
        big(width, BF16), big(width, BF16), big(width, BF16), big(width, BF16),
        big(P2, BF16), big(P2, BF16),
        pltpu.VMEM((width, P2), BF16), pltpu.VMEM((width, P2), BF16),
        big(128), big(width, BF16), big(width, BF16),
        pltpu.VMEM((2 * SUB, width), F32), pltpu.VMEM((2, width, P2), F32),
        pltpu.VMEM((2, P2, width), F32), pltpu.VMEM((2, width, width), F32),
        pltpu.VMEM((4, rows_dev, 1, P2 + 128), F32),
        pltpu.VMEM((4, rows_dev, n_tm, 1, P2 + 128), F32),
        pltpu.SemaphoreType.DMA((2 * rows_dev + 14,)),
        pltpu.SemaphoreType.DMA((4, rows_dev)), pltpu.SemaphoreType.DMA((4, rows_dev)),
        pltpu.SemaphoreType.DMA((PUTS,)), pltpu.SemaphoreType.DMA((bits * GETS,)),
    ]
    for k in (1, 2, 3, 4, 5, 10, 12):
        scratch.append(pltpu.VMEM(args[k].shape, args[k].dtype))
    for chunk in chunks.values():
        scratch.append(pltpu.VMEM((chunk.land_rows, chunk.width), F32))
    held = pl.pallas_call(
        functools.partial(kernel, cfg),
        out_shape=[pltpu.VMEM(o.shape, o.dtype) for o in out_shape],
        in_specs=in_specs,
        out_specs=out_specs,
        scratch_shapes=scratch,
        compiler_params=pltpu.CompilerParams(
            collective_id=0, has_side_effects=True, vmem_limit_bytes=53 * 2**20
        ),
    )(*args)
    grads = [args[k] for k in range(2, 13)]
    final_shape = [out_shape[0]] * 2 + [jax.ShapeDtypeStruct(g.shape, F32) for g in grads]
    final_specs = [hbm] * 13
    return tuple(
        pl.pallas_call(
            functools.partial(finish_kernel, states),
            out_shape=final_shape,
            in_specs=[hbm, hbm, vm, hbm, hbm, hbm],
            out_specs=final_specs,
            scratch_shapes=[pltpu.SemaphoreType.DMA((13,))]
            + [pltpu.VMEM((2, width), F32)] * 3
            + [pltpu.VMEM((2, states), F32)] * 3,
            compiler_params=pltpu.CompilerParams(vmem_limit_bytes=2**20),
        )(*held)
    )


def solution(mesh):
    rows = P("rows", "tm", None)
    in_specs = (rows, P("rows", "tm")) + (P(),) * 11 + (rows,)
    out_specs = (rows, rows) + (P(),) * 11
    return jax.shard_map(
        functools.partial(on_device, mesh.shape["tm"], mesh.shape["rows"]),
        mesh=mesh,
        in_specs=in_specs,
        out_specs=out_specs,
        check_vma=False,
    )
```

```python
import functools
import math

import jax
import jax.numpy as jnp
from jax import lax
from jax.experimental import pallas as pl
from jax.experimental.pallas import tpu as pltpu
from jax.sharding import PartitionSpec as P

NORM_EPS = 1e-05
MESH = pl.DeviceIdType.MESH
F32 = jnp.float32
BF16 = jnp.bfloat16
SUB = 8
UNROLL = 16
PUTS, GETS = 24, 15
TILE = 256
STEPS = [128, 128, 256, 256, 128, 128]
ORDERS = [
    "YX", "XY", "YX", "ZX", "yx", "XY", "zy", "ZY", "YX", "xy", "zx", "yx", "xy", "xy", "XY",
    "YX", "yz", "YX", "xy", "XY", "xy", "xy", "yz",
]


class Refs:
    pass


def horner(value, coeffs):
    total = coeffs[-1]
    for coeff in coeffs[-2::-1]:
        total = total * value + coeff
    return total


def discretize(lam_re, lam_im, time_steps):
    growth = lam_re * time_steps
    angles = lam_im * time_steps
    square = angles * angles
    fact = math.factorial
    grow = growth * horner(growth, [1.0 / fact(k + 1) for k in range(8)])
    sine = angles * horner(square, [(-1.0) ** k / fact(2 * k + 1) for k in range(7)])
    dip = square * horner(square, [(-1.0) ** k / fact(2 * k + 2) for k in range(7)])
    cosine = 1.0 - dip
    magnitude = 1.0 + grow
    a_re = magnitude * cosine
    a_im = magnitude * sine
    e_re = grow * cosine - dip
    modulus = lam_re * lam_re + lam_im * lam_im
    q_re = (e_re * lam_re + a_im * lam_im) / modulus
    q_im = (a_im * lam_re - e_re * lam_im) / modulus
    return (a_re, a_im, q_re, q_im)


def cmul(a, b):
    return (a[0] * b[0] - a[1] * b[1], a[0] * b[1] + a[1] * b[0])


def dot(a, b):
    return jnp.dot(a, b, preferred_element_type=F32)


def dot_nt(a, b):
    return lax.dot_general(a, b, (((1,), (1,)), ((), ())), preferred_element_type=F32)


def dot_tn(a, b):
    return lax.dot_general(a, b, (((0,), (0,)), ((), ())), preferred_element_type=F32)


def fold(value):
    rows, cols = value.shape
    return jnp.sum(value.reshape(rows // SUB, SUB, cols), axis=0)


def gauss(y):
    size = jnp.abs(y) * (0.5**0.5)
    bell = jnp.exp(-0.5 * (y * y))
    t = pltpu.reciprocal(1.0 + 0.3275911 * size, approx=True)
    tail = (0.5 * t * bell) * horner(
        t, [0.254829592, -0.284496736, 1.421413741, -1.453152027, 1.061405429]
    )
    cdf = jnp.where(y >= 0.0, 1.0 - tail, tail)
    return cdf, y * bell * ((2.0 * math.pi) ** -0.5)


class Chunk:
    def __init__(self, index, grad, rows, cols, groups):
        self.index, self.grad, self.rows, self.cols = index, grad, rows, cols
        self.width = cols[1] - cols[0]
        self.stages = []
        size, land, bits = rows, 0, []
        for group in groups:
            fits = size % (SUB << len(group)) == 0
            for part in [group] if fits else [(bit,) for bit in group]:
                halved = size % (SUB << len(part)) == 0
                size = size >> len(part) if halved else size
                self.stages.append((part, size, halved, land))
                land += size * ((1 << len(part)) - 1)
                bits.append(part)
        self.bits, self.land_rows = bits, land
        self.steps = [("sum", i) for i in range(len(bits))]
        self.steps += [("get", i) for i in reversed(range(len(bits))) if self.stages[i][2]]


def plan_chunks(n_tm, n_rows, width, P2):
    tm_bits, row_bits = int(math.log2(n_tm)), int(math.log2(n_rows))
    core = [("tm", 0)]
    half = (tm_bits - 1) // 2
    xs = [("tm", 1 + k) for k in range(half)]
    ys = [("tm", 1 + half + k) for k in range(tm_bits - 1 - half)]
    zs = [("rows", k) for k in range(row_bits)]

    def order(name):
        pair = name.isupper()
        axes = {"x": [(b,) for b in xs], "y": [(b,) for b in ys]}
        axes["z"] = [tuple(zs[:2])] if pair else [(b,) for b in zs[:1]]
        first, second = name.lower()
        third = ({"x", "y", "z"} - {first, second}).pop()
        rest = [(b,) for b in zs[2 if pair else 1 :]]
        return [(core[0],)] + axes[first] + axes[second] + axes[third] + rest

    chunks = {}
    count = 0
    plan, steps = iter(ORDERS), iter(STEPS)
    for l in (1, 0):
        for name, rows, cols in (("w", width, width), ("c", P2, width), ("b", width, P2)):
            step = next(steps)
            for k in range(0, cols, step):
                chunks[name, l, k] = Chunk(
                    count, (name, l), rows, (k, k + step), order(next(plan))
                )
                count += 1
    chunks["s"] = Chunk(count, ("s", None), 2 * SUB, (0, width), order("yx"))
    return chunks


class Mover:
    RATE = {"c": 650e3, "x": 46e3, "y": 46e3, "z": 46e3, "mid": 46e3}
    DELAY = {"c": 0.8, "x": 1.7, "y": 1.7, "z": 1.7}
    EXCHANGE = 3.2
    AHEAD = 2.5

    def __init__(self, chunks, refs, lands, at, half_bits):
        self.chunks, self.refs, self.at, self.half_bits = chunks, refs, at, half_bits
        self.lands = lands
        self.now = 0.0
        self.free = {k: 0.0 for k in self.RATE}
        self.queue = {k: [] for k in self.DELAY}
        self.pending = []
        self.copies = {}
        self.starts = {}
        self.clock = 0
        self.gets, self.acked, self.puts, self.used = {}, {}, [], {}

    def coord(self, bit):
        return lax.rem(self.at[bit[0]] // (1 << bit[1]), 2)

    def peer(self, bits):
        ids = {}
        for bit in bits:
            own = ids.get(bit[0], self.at[bit[0]])
            ids[bit[0]] = own + (1 - 2 * self.coord(bit)) * (1 << bit[1])
        return ids

    def share(self, bits, other=()):
        part = 0
        for bit in bits:
            own = self.coord(bit)
            part = 2 * part + (1 - own if bit in other else own)
        return part

    def begin(self, chunk, level):
        key = (chunk.rows, tuple(chunk.bits[:level]))
        if key not in self.starts:
            if level == 0:
                self.starts[key] = 0
            else:
                bits, size, halved, _ = chunk.stages[level - 1]
                before = self.begin(chunk, level - 1)
                self.starts[key] = before + self.share(bits) * size if halved else before
        return self.starts[key]

    def view(self, chunk, start, size, done=False):
        ref = self.refs[1 if done else 0][chunk.grad[0]]
        rows = pl.ds(pl.multiple_of(start, SUB) if not isinstance(start, int) else start, size)
        cols = pl.ds(chunk.cols[0], chunk.width)
        l = chunk.grad[1]
        return ref.at[rows, cols] if l is None else ref.at[l, rows, cols]

    def link(self, bits):
        bit = bits[0]
        if bit[0] == "rows":
            return "z"
        return "c" if bit[1] == 0 else ("x" if bit[1] <= self.half_bits else "y")

    def cost(self, chunk, k):
        bit, size, _, _ = chunk.stages[chunk.steps[k][1]]
        return size * chunk.width * 4 / self.RATE[self.link(bit)] * (3 if len(bit) > 1 else 1)

    def left(self, chunk, k):
        total = 0.0
        for j in range(k, len(chunk.steps)):
            bit = chunk.stages[chunk.steps[j][1]][0]
            total += self.cost(chunk, j) + self.DELAY[self.link(bit)]
        return total

    def push(self, chunk, k):
        bit = chunk.stages[chunk.steps[k][1]][0]
        self.queue[self.link(bit)].append((-self.left(chunk, k), chunk.index, k, chunk))

    def take_get(self, bit):
        pool = self.gets.setdefault(bit, {})
        for k, released in pool.items():
            if released is not None and released < self.acked.get(bit, 0):
                pool[k] = None
                return k
        k = sum(len(other) for other in self.gets.values())
        pool[k] = None
        return k

    def take_put(self):
        if True in self.puts:
            k = self.puts.index(True)
            self.puts[k] = False
            return k
        self.puts.append(False)
        return len(self.puts) - 1

    def pump(self):
        for link, queue in self.queue.items():
            while queue and self.free[link] < self.now + self.AHEAD:
                item = min(queue, key=lambda entry: entry[:3])
                queue.remove(item)
                self.launch(item[3], item[2])

    def launch(self, chunk, k):
        kind, i = chunk.steps[k]
        bit, size, halved, land = chunk.stages[i]
        put, get = self.take_put(), self.take_get(bit)
        self.clock += 1
        self.used[chunk.index, k] = (put, get, self.clock)
        if self.refs is not None:
            self.copies[chunk.index, k] = copies = []
            for m in range(1, 1 << len(bit)):
                other = [b for n, b in enumerate(bit) if m >> n & 1]
                if kind == "sum":
                    before = self.begin(chunk, i)
                    if halved:
                        before = before + self.share(bit, other) * size
                    src = self.view(chunk, before, size)
                    dst = self.lands[chunk.index].at[pl.ds(land + (m - 1) * size, size)]
                else:
                    src = dst = self.view(chunk, self.begin(chunk, i + 1), size, True)
                copy = pltpu.make_async_remote_copy(
                    src,
                    dst,
                    self.refs[2].at[put],
                    self.refs[3].at[get],
                    device_id=self.peer(other),
                    device_id_type=MESH,
                )
                copy.start()
                copies.append(copy)
        link = self.link(bit)
        cost = self.cost(chunk, k)
        far = link == "z" and bit[-1][1] > 0
        began = max(self.now, self.free[link], self.free["mid"] if far else 0.0)
        self.free[link] = done = began + cost
        if far:
            self.free["mid"] = done = began + cost * (2 if len(bit) == 1 else 4 / 3)
        self.pending.append((done + self.DELAY[link], chunk.index, k, chunk))
        self.now += 0.04 * ((1 << len(bit)) - 1)

    def finish(self, item):
        _, _, k, chunk = item
        kind, i = chunk.steps[k]
        bit, size, _, land = chunk.stages[i]
        real = self.refs is not None
        copies = self.copies.get((chunk.index, k))
        many = (1 << len(bit)) - 1
        if real and many == 1:
            copies[0].wait()
        elif real:
            whole = self.lands[chunk.index].at[pl.ds(land, many * size)]
            put, get, _ = self.used[chunk.index, k]
            pltpu.make_async_copy(whole, whole, self.refs[3].at[get]).wait()
            pltpu.make_async_copy(whole, whole, self.refs[2].at[put]).wait()
        put, get, launched = self.used[chunk.index, k]
        self.clock += 1
        self.puts[put] = True
        self.gets[bit][get] = self.clock
        self.acked[bit] = max(self.acked.get(bit, 0), launched)
        self.now += 0.08
        more = k + 1 < len(chunk.steps)
        if kind == "get":
            if more:
                self.push(chunk, k + 1)
            self.pump()
            return
        start = self.begin(chunk, i + 1) if real else 0

        def add(off, rows):
            self.now += rows * chunk.width * 4 / 3e6 * (many + 1) / 2
            if not real:
                return
            ref = self.view(chunk, start + off, rows)
            total = ref[...]
            for m in range(many):
                at = land + m * size + off
                at = pl.multiple_of(at, SUB) if not isinstance(at, int) else at
                total = total + self.lands[chunk.index][pl.ds(at, rows), :]
            last = i + 1 == len(chunk.bits)
            into = self.view(chunk, start + off, rows, True) if last else ref
            into[...] = total

        follows = chunk.stages[i + 1] if i + 1 < len(chunk.bits) else None
        if follows is not None and follows[2] and len(follows[0]) == 1:
            half = size // 2
            mine = self.share(follows[0]) if real else 0
            add((1 - mine) * half, half)
            self.push(chunk, k + 1)
            self.pump()
            add(mine * half, half)
        else:
            add(0, size)
            if more:
                self.push(chunk, k + 1)
            self.pump()

    def first(self):
        return min(self.pending, key=lambda item: item[:3])

    def start(self, chunk):
        self.push(chunk, 0)
        self.pump()

    def run(self, spent):
        self.now += spent
        while self.pending and self.first()[0] <= self.now:
            item = self.first()
            self.pending.remove(item)
            self.finish(item)

    def message(self):
        return max(self.now, self.free["x"], self.free["y"]) + self.EXCHANGE

    def until(self, time):
        while self.pending and self.first()[0] <= time:
            item = self.first()
            self.pending.remove(item)
            self.now = max(self.now, item[0])
            self.finish(item)
        self.now = max(self.now, time)

    def drain(self):
        while self.pending:
            item = self.first()
            self.pending.remove(item)
            self.now = max(self.now, item[0])
            self.finish(item)


def kernel(cfg, *refs):
    tokens, width, states, rows_dev, group, n_tm, n_rows, chunks = cfg
    R = Refs()
    (
        R.inputs, R.resets_in, R.gains_in, R.lam_re_in, R.lam_im_in, R.steps_in, R.b_re, R.b_im,
        R.c_re, R.c_im, R.skip_in, R.glu_w, R.glu_b_in, R.cot, R.out, R.in_grad, R.small_o, R.b_o,
        R.c_o, R.w_o, R.xin, R.cin, R.wb_re, R.wb_im, R.wc, R.wg, R.h1, R.h2, R.z1, R.z2, R.r1,
        R.r2, R.u1, R.u2, R.v, R.x1, R.x2, R.s1, R.s2, R.gl1, R.gl2, R.gd1, R.gate1, R.prod1,
        R.d_mid, R.dy1, R.dy2, R.ds1, R.ds2, R.dv1, R.dv2, R.m1, R.m2, R.keep, R.stage, R.result, R.small_g,
        R.b_g, R.c_g, R.w_g, R.msg, R.got, R.in_sem, R.send_sem,
        R.recv_sem, R.put_sem, R.get_sem, R.resets, R.gains, R.lam_re, R.lam_im, R.steps, R.skip,
        R.glu_b,
        *lands,
    ) = refs
    segs = SUB
    per_seg = group // segs
    at = lax.axis_index("tm")
    P2 = 2 * states

    barrier = pltpu.get_barrier_semaphore()
    tm_bits = int(math.log2(n_tm))
    others = []
    for m in reversed(range(1, n_tm)):
        flips = [(1 - 2 * lax.rem(at // (1 << b), 2)) * (1 << b) for b in range(tm_bits) if m >> b & 1]
        others.append(at + sum(flips))
    row_at = lax.axis_index("rows")
    grads = {"b": R.b_g, "c": R.c_g, "w": R.w_g, "s": R.small_g}
    sums = {"b": R.b_o, "c": R.c_o, "w": R.w_o, "s": R.small_o}
    mover_refs = (grads, sums, R.put_sem, R.get_sem)
    half_bits = (int(math.log2(n_tm)) - 1) // 2
    mover = Mover(chunks, mover_refs, lands, {"tm": at, "rows": row_at}, half_bits)
    row_bits = int(math.log2(n_rows))
    zs = [("rows", k) for k in range(row_bits)]
    greeted = [[z] for z in zs] + ([zs[:2]] if row_bits > 1 else [])

    def load(k, src, dst):
        copy = pltpu.make_async_copy(src, dst, R.in_sem.at[k])
        copy.start()
        return copy

    cp_x = [load(r, R.inputs.at[r], R.xin.at[pl.ds(r * group, group)]) for r in range(rows_dev)]
    k0 = 2 * rows_dev + 5
    pairs = [
        (R.resets_in, R.resets), (R.lam_re_in, R.lam_re), (R.lam_im_in, R.lam_im),
        (R.steps_in, R.steps), (R.gains_in, R.gains), (R.skip_in, R.skip), (R.glu_b_in, R.glu_b),
    ]
    cp_small = [load(k0 + k, src, dst) for k, (src, dst) in enumerate(pairs)]
    k0 = rows_dev
    cp_b = [load(k0, R.b_re.at[0], R.wb_re.at[0]), load(k0 + 1, R.b_im.at[0], R.wb_im.at[0])]
    for other in others:
        pl.semaphore_signal(barrier, inc=1, device_id={"tm": other}, device_id_type=MESH)
    for bits in greeted:
        pl.semaphore_signal(barrier, inc=1, device_id=mover.peer(bits), device_id_type=MESH)
    cp_c = [
        load(k0 + 2, R.c_re, R.wc.at[:, pl.ds(0, states)]),
        load(k0 + 3, R.c_im, R.wc.at[:, pl.ds(states, states)]),
    ]
    k1 = 2 * rows_dev + 12
    cp_w = [
        load(k0 + 4, R.glu_w, R.wg),
        load(k1, R.b_re.at[1], R.wb_re.at[1]),
        load(k1 + 1, R.b_im.at[1], R.wb_im.at[1]),
    ]
    cp_t = [
        load(k0 + 5 + r, R.cot.at[r], R.cin.at[pl.ds(r * group, group)])
        for r in range(rows_dev)
    ]

    for cp in cp_small:
        cp.wait()

    place_bits = int(math.log2(per_seg))
    i0 = lax.broadcasted_iota(jnp.int32, (group, group), 0)
    i1 = lax.broadcasted_iota(jnp.int32, (group, group), 1)
    hit = i1 == (i0 & (SUB - 1)) * per_seg + (i0 >> 3)
    gather = jnp.where(hit, 1.0, 0.0).astype(BF16)
    kept = 1.0 - R.resets[...].astype(F32)
    for r in range(rows_dev):
        spread = jnp.where(hit, jnp.broadcast_to(kept[r : r + 1], (group, group)), 0.0)
        R.keep[r * group : (r + 1) * group, :] = dot(
            spread.astype(BF16), jnp.ones((group, 128), BF16)
        )

    seg_id = lax.broadcasted_iota(jnp.int32, (SUB, 128), 0)

    def shift(value, forward, by=1):
        return pltpu.roll(value, by if forward else SUB - by, 0)

    def wide(mask, cols):
        return jnp.concatenate([mask] * (cols // 128), axis=1)

    def inside(forward, by):
        return seg_id >= by if forward else seg_id < SUB - by

    window, excl, total_mask, whole = {}, {}, {}, {}
    for r in range(rows_dev):
        places = [R.keep[r * group + j * SUB : r * group + (j + 1) * SUB] for j in range(per_seg)]
        while len(places) > 1:
            places = [a * b for a, b in zip(places[::2], places[1::2])]
        whole[r] = places[0]

    def masks(forward):
        for r in range(rows_dev):
            run, seen = whole[r], whole[r]
            for by in (1, 2, 4):
                ok = inside(forward, by)
                window[r, forward, by] = jnp.where(ok, run, 0.0)
                seen = jnp.where(ok, seen * shift(seen, forward, by), seen)
                run = run * shift(run, forward, by)
            excl[r, forward] = jnp.where(inside(forward, 1), shift(seen, forward), 1.0)
            if forward:
                total_mask[r] = seen[SUB - 1 : SUB]

    def constants(l):
        lam = [n[l : l + 1, :] for n in (R.lam_re, R.lam_im, R.steps)]
        a_re, a_im, q_re, q_im = discretize(*lam)
        power = (a_re, a_im)
        for _ in range(place_bits):
            power = cmul(power, power)
        powers = {1: power}
        for by in (1, 2, 4):
            powers[2 * by] = cmul(powers[by], powers[by])
        for forward in (True, False):
            index = wide(seg_id if forward else SUB - 1 - seg_id, states)
            at_seg = (jnp.ones((SUB, states), F32), jnp.zeros((SUB, states), F32))
            for by in (1, 2, 4):
                more = cmul(at_seg, powers[by])
                at_seg = tuple(
                    jnp.where((index & by) != 0, m, o) for m, o in zip(more, at_seg)
                )
            powers[forward, 0] = at_seg
        return dict(lam=lam, a=(a_re, a_im), q=(q_re, q_im), powers=powers, l=l)

    def input_matrix(layer, m_ref):
        q_re, q_im = layer["q"]
        l = layer["l"]
        step = 128
        for i in range(width // step):
            sl = slice(i * step, (i + 1) * step)
            br = R.wb_re[l, sl, :].astype(F32)
            bi = R.wb_im[l, sl, :].astype(F32)
            m_ref[sl, 0:states] = (q_re * br - q_im * bi).astype(BF16)
            m_ref[sl, states:P2] = (q_re * bi + q_im * br).astype(BF16)

    def scan_pass(r, layer, forward, start, sink):
        a = [jnp.broadcast_to(p, (SUB, states)) for p in layer["a"]]
        v_ref, keep_ref = R.v, R.keep

        def one(j, carry):
            base = pl.multiple_of(r * group + j * SUB, SUB)
            keep = wide(keep_ref[pl.ds(base, SUB), :], states)
            v = (v_ref[pl.ds(base, SUB), 0:states], v_ref[pl.ds(base, SUB), states:P2])
            if forward:
                held = (keep * carry[0], keep * carry[1])
                prod = cmul(a, held)
                x = (prod[0] + v[0], prod[1] + v[1])
                return x, held, x
            prod = cmul(a, carry)
            x = (prod[0] + v[0], prod[1] + v[1])
            held = (keep * x[0], keep * x[1])
            return x, carry, held

        pair = 2

        def body(i, carry):
            state, extra = carry
            if forward:
                js = [i * pair + k for k in range(pair)]
            else:
                js = [per_seg - 1 - (i * pair + k) for k in range(pair)]
            xs = []
            for j in js:
                x, held, state = one(j, state)
                xs.append(x)
                if sink is not None:
                    extra = sink.each(r * group + j * SUB, x, held, extra)
            if sink is not None:
                low = js[0] if forward else js[-1]
                ordered = xs if forward else xs[::-1]
                sink.pair(r * group + low * SUB, ordered)
            return state, extra

        extra0 = sink.zero() if sink is not None else ()
        return lax.fori_loop(0, per_seg // pair, body, (start, extra0), unroll=UNROLL)

    class Forward:
        def __init__(self, x_ref, s_ref):
            self.x_ref, self.s_ref = x_ref, s_ref

        def zero(self):
            return ()

        def each(self, base, x, held, extra):
            base = pl.multiple_of(base, SUB)
            self.x_ref[pl.ds(base, SUB), 0:states] = x[0]
            self.x_ref[pl.ds(base, SUB), states:P2] = x[1]
            return extra

        def pair(self, base, xs):
            base = pl.multiple_of(base, 2 * SUB)
            re = jnp.concatenate([x[0] for x in xs], axis=0)
            im = jnp.concatenate([x[1] for x in xs], axis=0)
            self.s_ref[pl.ds(base, 2 * SUB), 0:states] = re.astype(BF16)
            self.s_ref[pl.ds(base, 2 * SUB), states:P2] = (-im).astype(BF16)

    class Adjoint:
        def __init__(self, x_ref, d_ref):
            self.x_ref, self.d_ref = x_ref, d_ref

        def zero(self):
            return (jnp.zeros((SUB, states), F32), jnp.zeros((SUB, states), F32))

        def each(self, base, x, held, extra):
            base = pl.multiple_of(base, SUB)
            xv = (self.x_ref[pl.ds(base, SUB), 0:states], self.x_ref[pl.ds(base, SUB), states:P2])
            prod = cmul(xv, held)
            return (extra[0] + prod[0], extra[1] + prod[1])

        def pair(self, base, xs):
            base = pl.multiple_of(base, 2 * SUB)
            re = jnp.concatenate([x[0] for x in xs], axis=0)
            im = jnp.concatenate([x[1] for x in xs], axis=0)
            self.d_ref[pl.ds(base, 2 * SUB), 0:states] = re.astype(BF16)
            self.d_ref[pl.ds(base, 2 * SUB), states:P2] = (-im).astype(BF16)

    first_wait = [True]

    def send_carry(e, r, layer, forward, ends):
        seen = ends
        for by in (1, 2, 4):
            mask = wide(window[r, forward, by], states)
            prod = cmul(layer["powers"][by], tuple(shift(p, forward, by) for p in seen))
            seen = (seen[0] + mask * prod[0], seen[1] + mask * prod[1])
        ok = wide(inside(forward, 1), states)
        run = tuple(jnp.where(ok, shift(p, forward), 0.0) for p in seen)
        last = slice(SUB - 1, SUB) if forward else slice(0, 1)
        R.msg[e, r, :, 0:states] = seen[0][last]
        R.msg[e, r, :, states:P2] = seen[1][last]
        R.msg[e, r, :, P2 : P2 + 128] = total_mask[r]
        if first_wait[0]:
            pl.semaphore_wait(barrier, n_tm - 1 + len(greeted))
            first_wait[0] = False
        for other in others:
            copy = pltpu.make_async_remote_copy(
                R.msg.at[e, r],
                R.got.at[e, r, at],
                R.send_sem.at[e, r],
                R.recv_sem.at[e, r],
                device_id={"tm": other},
                device_id_type=MESH,
            )
            copy.start()
        return run, mover.message()

    def take_carry(e, r, layer, forward, sent):
        run, arrival = sent
        mover.until(arrival)
        slots = R.got.at[e, r, pl.ds(0, n_tm - 1)]
        pltpu.make_async_copy(slots, slots, R.recv_sem.at[e, r]).wait()
        pltpu.make_async_copy(slots, slots, R.send_sem.at[e, r]).wait()
        span = layer["powers"][SUB]
        carry = (jnp.zeros((1, states), F32), jnp.zeros((1, states), F32))
        order = range(n_tm) if forward else range(n_tm - 1, -1, -1)
        for k in list(order)[:-1]:
            before = (at > k) if forward else (at < k)
            mask = wide(R.got[e, r, k, :, P2 : P2 + 128], states)
            prod = cmul(span, carry)
            new = (
                R.got[e, r, k, :, 0:states] + mask * prod[0],
                R.got[e, r, k, :, states:P2] + mask * prod[1],
            )
            carry = tuple(jnp.where(before, n, c) for n, c in zip(new, carry))
        prod = cmul(layer["powers"][forward, 0], carry)
        mask = wide(excl[r, forward], states)
        return (run[0] + mask * prod[0], run[1] + mask * prod[1])

    zero_state = (jnp.zeros((SUB, states), F32), jnp.zeros((SUB, states), F32))

    tiles = {
        r: [(slice(r * group + i, r * group + i + TILE), slice(i, i + TILE)) for i in range(0, group, TILE)]
        for r in range(rows_dev)
    }
    line = [slice(r * group, (r + 1) * group) for r in range(rows_dev)]
    rows = range(rows_dev)

    def norm_front(h, layer, z_ref, r_ref, u_ref, m_ref, sl):
        mean = jnp.mean(h, axis=1, keepdims=True)
        centred = h - mean
        var = jnp.mean(centred * centred, axis=1, keepdims=True)
        r = lax.rsqrt(var + NORM_EPS)
        z = centred * r
        u = (z * R.gains[layer["l"] : layer["l"] + 1, :]).astype(BF16)
        z_ref[sl, :] = z
        r_ref[sl, :] = jnp.broadcast_to(r, (r.shape[0], 128))
        u_ref[sl, :] = u
        R.v[sl, :] = dot(u, m_ref[...])

    def mixer(layer, s_ref, u_ref, gl_ref, sl):
        l = layer["l"]
        s = s_ref[sl, :]
        y = dot(s, R.wc[l]) + R.skip[l : l + 1, :] * u_ref[sl, :].astype(F32)
        cdf, dens = gauss(y)
        gelu = y * cdf
        low = gelu.astype(BF16)
        gl_ref[sl, :] = low
        pre = dot(low, R.wg[l]) + R.glu_b[l : l + 1, :]
        gate = 0.5 * jnp.tanh(0.5 * pre) + 0.5
        gated = gelu * gate
        return gated, cdf + dens, gate, gated * (1.0 - gate)

    def back_front(layer, d_out, slope, gate, prod, u_ref, ds_ref, dy_ref, sums, sl):
        l = layer["l"]
        ds = (d_out * prod).astype(BF16)
        ds_ref[sl, :] = ds
        d_gelu = d_out * gate + dot_nt(ds, R.wg[l])
        dy = (d_gelu * slope).astype(BF16)
        dy_ref[sl, :] = dy
        R.v[sl, :] = dot_nt(dy, R.wc[l])
        sums["bias"] = sums["bias"] + fold(ds.astype(F32))
        sums["skip"] = sums["skip"] + fold(dy.astype(F32) * u_ref[sl, :].astype(F32))

    def back_norm(layer, d_out, dv_ref, m_ref, dy_ref, z_ref, r_ref, sums, sl):
        l = layer["l"]
        dn = dy_ref[sl, :].astype(F32) * R.skip[l : l + 1, :] + dot_nt(dv_ref[sl, :], m_ref[...])
        z = z_ref[sl, :]
        sums["gain"] = sums["gain"] + fold(dn * z)
        w = dn * R.gains[l : l + 1, :]
        mean_w = jnp.mean(w, axis=1, keepdims=True)
        mean_wz = jnp.mean(w * z, axis=1, keepdims=True)
        r = wide(r_ref[sl, :], width)
        return d_out + r * (w - mean_w - z * mean_wz)

    def fresh():
        return {k: jnp.zeros((SUB, width), F32) for k in ("gain", "skip", "bias")}

    def start(name, l, first, count):
        for k in range(first, first + count, SUB):
            if (name, l, k) in chunks:
                mover.start(chunks[name, l, k])

    def product_grads(layer, gl_ref, ds_ref, s_ref, dy_ref):
        l = layer["l"]
        for name, left, right in (("w", gl_ref, ds_ref), ("c", s_ref, dy_ref)):
            for k in range(0, width, 256):
                grads[name][l, :, k : k + 256] = dot_tn(left[...], right[:, k : k + 256])
                start(name, l, k, 256)
                mover.run(0.15)

    def matrix_grads(layer, u_ref, dv_ref, da):
        l = layer["l"]
        q_re, q_im = layer["q"]
        full = dot_tn(u_ref[...], dv_ref[...])
        g_re, g_im = full[:, 0:states], full[:, states:P2]
        R.b_g[l, :, 0:states] = q_re * g_re + q_im * g_im
        R.b_g[l, :, states:P2] = q_re * g_im - q_im * g_re
        start("b", l, 0, P2)
        br, bi = R.wb_re[l].astype(F32), R.wb_im[l].astype(F32)
        dq_re = jnp.sum(fold(br * g_re + bi * g_im), axis=0, keepdims=True)
        dq_im = jnp.sum(fold(br * g_im - bi * g_re), axis=0, keepdims=True)
        da_re = jnp.sum(da[0], axis=0, keepdims=True)
        da_im = -jnp.sum(da[1], axis=0, keepdims=True)
        _, pull = jax.vjp(discretize, *layer["lam"])
        lam_grads = pull((da_re, da_im, dq_re, dq_im))
        for k, grad in enumerate(lam_grads):
            row = 6 + 2 * k + l
            R.small_g[row : row + 1, 0:states] = grad

    one = constants(0)
    masks(True)
    for cp in cp_b:
        cp.wait()
    input_matrix(one, R.m1)
    for cp in cp_x:
        cp.wait()
    sent = {}
    for r in rows:
        for sl, part in tiles[r]:
            h = dot(gather[part, :], R.xin[line[r], :])
            R.h1[sl, :] = h
            norm_front(h, one, R.z1, R.r1, R.u1, R.m1, sl)
        ends, _ = scan_pass(r, one, True, zero_state, None)
        sent[0, r] = send_carry(0, r, one, True, ends)
    two = constants(1)
    masks(False)
    for cp in cp_c + cp_w + cp_t:
        cp.wait()
    input_matrix(two, R.m2)

    for r in rows:
        carry = take_carry(0, r, one, True, sent[0, r])
        scan_pass(r, one, True, carry, Forward(R.x1, R.s1))
        for sl, _ in tiles[r]:
            gated, slope, gate, prod = mixer(one, R.s1, R.u1, R.gl1, sl)
            R.gd1[sl, :] = slope
            R.gate1[sl, :] = gate
            R.prod1[sl, :] = prod
            h = R.h1[sl, :] + gated
            R.h2[sl, :] = h
            norm_front(h, two, R.z2, R.r2, R.u2, R.m2, sl)
        ends, _ = scan_pass(r, two, False, zero_state, None)
        sent[1, r] = send_carry(1, r, two, False, ends)

    sums2 = fresh()
    for r in rows:
        carry = take_carry(1, r, two, False, sent[1, r])
        scan_pass(r, two, False, carry, Forward(R.x2, R.s2))
        for sl, part in tiles[r]:
            gated, slope, gate, prod = mixer(two, R.s2, R.u2, R.gl2, sl)
            R.result[sl, :] = (R.h2[sl, :] + gated).astype(BF16)
            d_out = dot(gather[part, :], R.cin[line[r], :])
            R.d_mid[sl, :] = d_out
            back_front(two, d_out, slope, gate, prod, R.u2, R.ds2, R.dy2, sums2, sl)
        mover.run(2.0)
        ends, _ = scan_pass(r, two, True, zero_state, None)
        sent[2, r] = send_carry(2, r, two, True, ends)
    product_grads(two, R.gl2, R.ds2, R.s2, R.dy2)

    sums1 = fresh()
    da2, da1 = Adjoint(R.x2, R.dv2).zero(), Adjoint(R.x1, R.dv1).zero()
    for r in rows:
        carry = take_carry(2, r, two, True, sent[2, r])
        _, da = scan_pass(r, two, True, carry, Adjoint(R.x2, R.dv2))
        da2 = (da2[0] + da[0], da2[1] + da[1])
        mover.run(0.3)
    R.small_g[...] = jnp.zeros((2 * SUB, width), F32)
    matrix_grads(two, R.u2, R.dv2, da2)
    mover.run(0.8)
    for r in rows:
        mover.run(0.3)
        for sl, _ in tiles[r]:
            d_mid = back_norm(two, R.d_mid[sl, :], R.dv2, R.m2, R.dy2, R.z2, R.r2, sums2, sl)
            R.d_mid[sl, :] = d_mid
            back_front(
                one, d_mid, R.gd1[sl, :], R.gate1[sl, :], R.prod1[sl, :],
                R.u1, R.ds1, R.dy1, sums1, sl,
            )
            mover.run(1.3)
        ends, _ = scan_pass(r, one, False, zero_state, None)
        mover.run(0.3)
        sent[3, r] = send_carry(3, r, one, False, ends)
    product_grads(one, R.gl1, R.ds1, R.s1, R.dy1)

    for r in rows:
        carry = take_carry(3, r, one, False, sent[3, r])
        mover.run(0.3)
        _, da = scan_pass(r, one, False, carry, Adjoint(R.x1, R.dv1))
        da1 = (da1[0] + da[0], da1[1] + da[1])
        mover.run(0.3)
        for sl, _ in tiles[r]:
            d_in = back_norm(one, R.d_mid[sl, :], R.dv1, R.m1, R.dy1, R.z1, R.r1, sums1, sl)
            R.stage[sl, :] = d_in.astype(BF16)
        mover.run(0.5)
    matrix_grads(one, R.u1, R.dv1, da1)
    for k, name in enumerate(("gain", "skip", "bias")):
        for l, sums in enumerate((sums1, sums2)):
            row = 2 * k + l
            R.small_g[row : row + 1, :] = jnp.sum(sums[name], axis=0, keepdims=True)
    mover.start(chunks["s"])
    mover.run(0.8)
    ungather = jnp.where(i1 == (i0 & (per_seg - 1)) * SUB + (i0 >> place_bits), 1.0, 0.0).astype(BF16)
    for r in rows:
        R.in_grad[r] = dot(ungather, R.stage[line[r], :]).astype(BF16)
    mover.run(0.3)
    for r in rows:
        R.out[r] = dot(ungather, R.result[line[r], :]).astype(BF16)
    mover.run(0.3)
    mover.drain()


def finish_kernel(states, out_v, in_grad_v, small_v, b_v, c_v, w_v, *refs):
    out, in_grad, gain, lam_re, lam_im, steps, b_re, b_im, c_re, c_im, skip, w, bias = refs[:13]
    sem, *held = refs[13:]
    pairs = [
        (b_v.at[:, :, pl.ds(0, states)], b_re),
        (b_v.at[:, :, pl.ds(states, states)], b_im),
        (c_v.at[:, pl.ds(0, states)], c_re),
        (c_v.at[:, pl.ds(states, states)], c_im),
        (w_v, w),
        (out_v, out),
        (in_grad_v, in_grad),
    ]
    copies = [pltpu.make_async_copy(a, b, sem.at[k]) for k, (a, b) in enumerate(pairs)]
    for copy in copies:
        copy.start()
    for k, (ref, target) in enumerate(zip(held, (gain, skip, bias, lam_re, lam_im, steps))):
        ref[...] = small_v[2 * k : 2 * k + 2, 0 : ref.shape[1]]
        copy = pltpu.make_async_copy(ref, target, sem.at[len(pairs) + k])
        copy.start()
        copies.append(copy)
    for copy in copies:
        copy.wait()


def on_device(n_tm, n_rows, *args):
    inputs, lam_re = args[0], args[3]
    rows_dev, group, width = inputs.shape
    states = lam_re.shape[1]
    tokens = rows_dev * group
    P2 = 2 * states
    chunks = plan_chunks(n_tm, n_rows, width, P2)
    cfg = (tokens, width, states, rows_dev, group, n_tm, n_rows, chunks)
    vm = pl.BlockSpec(memory_space=pltpu.VMEM)
    hbm = pl.BlockSpec(memory_space=pl.ANY)
    far = pl.BlockSpec(memory_space=pltpu.HBM)
    in_specs = [far] * 14
    out_specs = [vm] * 6
    out_shape = [
        jax.ShapeDtypeStruct(inputs.shape, BF16),
        jax.ShapeDtypeStruct(inputs.shape, BF16),
        jax.ShapeDtypeStruct((2 * SUB, width), F32),
        jax.ShapeDtypeStruct((2, width, P2), F32),
        jax.ShapeDtypeStruct((2, P2, width), F32),
        jax.ShapeDtypeStruct((2, width, width), F32),
    ]

    def big(cols, dtype=F32):
        return pltpu.VMEM((tokens, cols), dtype)

    bits = int(math.log2(n_tm * n_rows))
    scratch = [
        big(width, BF16), big(width, BF16),
        pltpu.VMEM((2, width, states), BF16), pltpu.VMEM((2, width, states), BF16),
        pltpu.VMEM((2, P2, width), BF16), pltpu.VMEM((2, width, width), BF16),
        big(width), big(width), big(width), big(width), big(128), big(128),
        big(width, BF16), big(width, BF16), big(P2), big(P2), big(P2),
        big(P2, BF16), big(P2, BF16), big(width, BF16), big(width, BF16),
        big(width), big(width), big(width), big(width),
        big(width, BF16), big(width, BF16), big(width, BF16), big(width, BF16),
        big(P2, BF16), big(P2, BF16),
        pltpu.VMEM((width, P2), BF16), pltpu.VMEM((width, P2), BF16),
        big(128), big(width, BF16), big(width, BF16),
        pltpu.VMEM((2 * SUB, width), F32), pltpu.VMEM((2, width, P2), F32),
        pltpu.VMEM((2, P2, width), F32), pltpu.VMEM((2, width, width), F32),
        pltpu.VMEM((4, rows_dev, 1, P2 + 128), F32),
        pltpu.VMEM((4, rows_dev, n_tm, 1, P2 + 128), F32),
        pltpu.SemaphoreType.DMA((2 * rows_dev + 14,)),
        pltpu.SemaphoreType.DMA((4, rows_dev)), pltpu.SemaphoreType.DMA((4, rows_dev)),
        pltpu.SemaphoreType.DMA((PUTS,)), pltpu.SemaphoreType.DMA((bits * GETS,)),
    ]
    for k in (1, 2, 3, 4, 5, 10, 12):
        scratch.append(pltpu.VMEM(args[k].shape, args[k].dtype))
    for chunk in chunks.values():
        scratch.append(pltpu.VMEM((chunk.land_rows, chunk.width), F32))
    held = pl.pallas_call(
        functools.partial(kernel, cfg),
        out_shape=[pltpu.VMEM(o.shape, o.dtype) for o in out_shape],
        in_specs=in_specs,
        out_specs=out_specs,
        scratch_shapes=scratch,
        compiler_params=pltpu.CompilerParams(
            collective_id=0, has_side_effects=True, vmem_limit_bytes=53 * 2**20
        ),
    )(*args)
    grads = [args[k] for k in range(2, 13)]
    final_shape = [out_shape[0]] * 2 + [jax.ShapeDtypeStruct(g.shape, F32) for g in grads]
    final_specs = [hbm] * 13
    return tuple(
        pl.pallas_call(
            functools.partial(finish_kernel, states),
            out_shape=final_shape,
            in_specs=[hbm, hbm, vm, hbm, hbm, hbm],
            out_specs=final_specs,
            scratch_shapes=[pltpu.SemaphoreType.DMA((13,))]
            + [pltpu.VMEM((2, width), F32)] * 3
            + [pltpu.VMEM((2, states), F32)] * 3,
            compiler_params=pltpu.CompilerParams(vmem_limit_bytes=2**20),
        )(*held)
    )


def solution(mesh):
    rows = P("rows", "tm", None)
    in_specs = (rows, P("rows", "tm")) + (P(),) * 11 + (rows,)
    out_specs = (rows, rows) + (P(),) * 11
    return jax.shard_map(
        functools.partial(on_device, mesh.shape["tm"], mesh.shape["rows"]),
        mesh=mesh,
        in_specs=in_specs,
        out_specs=out_specs,
        check_vma=False,
    )
```
